32 devices in a mesh: fsdp: 32 (over z, y, x, core).
Axes of the slice: x: 2, y: 2, z: 4, core: 2. Of those that a mesh axis runs over, the one named last changes fastest.
Arguments:
- hidden_in: bfloat16 [4096, 1024], P('fsdp'), may hold values from -6 to 6
- grad_out: bfloat16 [4096, 1024], P('fsdp'), may hold values from -6 to 6
- seq_lens: int32 [64, 2], P('fsdp'), may hold values from 0 to 64, as said below
- expert_choice: int32 [4096, 2], P('fsdp'), may hold values from 0 to 3, all different within a row; in each aligned block of 128 rows (0 to 127, 128 to 255, ...) at most 80 rows name the same one
- gain_attn: bfloat16 [1024], P('fsdp'), may hold values from 0.099609375 to 1.8984375
- w_query: bfloat16 [1024, 1024], P('fsdp'), may hold values from -0.1875 to 0.1875
- key_weight: bfloat16 [1024, 512], P('fsdp'), may hold values from -0.1875 to 0.1875
- value_weight: bfloat16 [1024, 512], P('fsdp'), may hold values from -0.1875 to 0.1875
- w_attn_out: bfloat16 [1024, 1024], P('fsdp'), may hold values from -0.5 to 0.5
- gain_ffn: bfloat16 [1024], P('fsdp'), may hold values from 0.099609375 to 1.8984375
- w_router: bfloat16 [1024, 4], P('fsdp'), may hold values from -0.125 to 0.125
- w_expert_in: bfloat16 [1024, 4096], P('fsdp'), may hold values from -0.1875 to 0.1875
- w_expert_out: bfloat16 [512, 4096], P('fsdp'), may hold values from -0.5 to 0.5
Outputs:
- block_output: bfloat16 [4096, 1024], P('fsdp')
- grad_in: bfloat16 [4096, 1024], P('fsdp')
- grad_gain_attn: float32 [1024], P('fsdp')
- grad_w_query: float32 [1024, 1024], P('fsdp')
- grad_w_key: float32 [1024, 512], P('fsdp')
- grad_w_value: float32 [1024, 512], P('fsdp')
- grad_w_attn_out: float32 [1024, 1024], P('fsdp')
- grad_gain_ffn: float32 [1024], P('fsdp')
- grad_w_router: float32 [1024, 4], P('fsdp')
- grad_w_expert_in: float32 [1024, 4096], P('fsdp')
- grad_w_expert_out: float32 [512, 4096], P('fsdp')
The draws below stay inside these ranges and needn't reach their ends.
Inputs may be any that keep to these rules, and one draw needn't show every extreme that they name: `seq_lens`: row r holds the lengths of the two sequences of micro-batch r % 2 of block r // 2; the first is 1 or more, the two sum to at most 64, and the remaining slots are padding; row 0 has a first sequence of 64. `expert_choice`: each row names 2 different experts; within one block of 128 rows no expert is named by more than 80 rows, and in some blocks one expert is named by exactly 80.
All inputs are finite; a program needn't handle non-finite values.
Results may differ from the reference program's by a relative error of at most 0.013.
Values may be sent and summed in bfloat16 or wider, within the bound.
No kernel may reach another device: no remote copies, remote signals or barrier semaphores. Data moves between devices by JAX's collectives and lax.ppermute only.
A program may use at most 192 MiB of HBM per device.

```python
import math
import jax
import jax.numpy as jnp
import numpy as np
from jax import lax

MODEL_WIDTH = 1024
QUERY_HEADS = 16
KEY_VALUE_HEADS = 8
HEAD_SIZE = 64
FE = 512
EXPERTS = 4
TOP = 2
MICRO = 2
MB_TOK = 64
TOK_DEV = 128
CAP = 80
TOKENS = 4096
LENS_ROWS = 64
N_FSDP = 32


def draw_seq_lens(key, part):
    key = jax.random.fold_in(key, 11)
    live_key, split_key = jax.random.split(key)
    live_total = jax.random.randint(live_key, (LENS_ROWS,), MB_TOK // 4, MB_TOK + 1)
    first_len = 1 + jax.random.randint(split_key, (LENS_ROWS,), 0, MB_TOK) % live_total
    second_len = live_total - first_len
    first_len = first_len.at[0].set(MB_TOK)
    second_len = second_len.at[0].set(0)
    return jnp.stack([first_len, second_len], axis=1).astype(jnp.int32)


def block_scale(rng, dims, pieces, low, high):
    factor_of = 1.0
    for dim, blocks in pieces:
        draws = jax.random.uniform(jax.random.fold_in(jax.random.fold_in(rng, 6), dim), (blocks,), jnp.float32, low / len(pieces), high / len(pieces))
        factor_of = factor_of * jnp.repeat(jnp.exp(draws), dims[dim] // blocks).reshape((-1,) + (1,) * (len(dims) - 1 - dim))
    return factor_of


def shared_out(own_key, own, number, rows, number_of, top, limit, lean):
    order = jax.random.permutation(own_key, number_of)
    crowded, ordinary = shares(number_of, rows * top, limit, lean, True), shares(number_of, rows * top, limit, lean, False)
    places = jnp.arange(number_of)

    def named(sizes, offset_by):
        used = int((sizes > 0).sum())
        fixed = max(1, used // 4)
        passed = fixed + (places - fixed + offset_by * (used - fixed)) % max(1, number_of - fixed)
        return jnp.zeros((number_of,), jnp.int32).at[order[jnp.where(places < fixed, places, passed)]].set(jnp.asarray(sizes, jnp.int32))

    sizes = jnp.where(number % 4 == 0, named(crowded, number // 4), named(ordinary, number - number // 4 - 1))
    mixed = jax.random.permutation(jax.random.fold_in(own, 3), number_of)
    donor, receiver = mixed[0:number_of // 2 * 2:2], mixed[1:number_of // 2 * 2:2]
    room = jnp.minimum(sizes[donor] - 1, limit - sizes[receiver]) // 2
    room = jnp.where((donor == order[0]) | (receiver == order[0]) | (sizes[receiver] == 0), 0, jnp.maximum(room, 0))
    passed = jax.random.randint(jax.random.fold_in(own, 4), (number_of // 2,), 0, 1 << 20) % (room + 1)
    sizes = sizes.at[donor].add(-passed).at[receiver].add(passed)
    members = jnp.searchsorted(jnp.cumsum(sizes), jnp.arange(rows * top), side="right").astype(jnp.int32)
    grid = members.reshape(top, rows).T
    grid = grid[jax.random.permutation(jax.random.fold_in(own, 1), rows)]
    offset_by = jax.random.randint(jax.random.fold_in(own, 2), (rows, 1), 0, top)
    return jnp.take_along_axis(grid, (jnp.arange(top)[None, :] + offset_by) % top, axis=1)


def shares(count, total, bound, skew, full):
    loads = [(1 << 20) // math.isqrt(grade ** skew) + 1 for grade in range(1, count + 1)]
    largest = bound if full else min(bound, max(-(-total // count), total * loads[0] // sum(loads)))
    least = 1 if total - largest >= count - 1 else 0
    holding, spare = [largest] + [least] * (count - 1), total - largest - least * (count - 1)
    while spare > 0:
        movable = [i for i in range(1, count) if holding[i] < largest] or [i for i in range(1, count) if holding[i] < bound]
        pool, budget = sum([loads[i] for i in movable]), spare
        for i in movable:
            more = min(bound - holding[i], max(1, budget * loads[i] // pool), spare)
            holding[i] = holding[i] + more
            spare = spare - more
    return np.array(holding)


def bell_draw(rng, dims, spread, bound, pieces=(), kind=jnp.bfloat16):
    loudness = block_scale(rng, dims, pieces, -0.22, 0.18) if pieces else 1.0
    array = jax.random.normal(rng, dims, jnp.float32) * spread * loudness
    return jnp.minimum(jnp.maximum(array, -bound), bound).astype(kind)


def setup_inputs(seed: int = 0) -> dict:
    arg_keys = jax.random.split(jax.random.key(seed), 14)
    hidden_in = bell_draw(arg_keys[0], (TOKENS, MODEL_WIDTH), 1.0, 6.0, ((0, 32),))
    grad_out = bell_draw(arg_keys[1], (TOKENS, MODEL_WIDTH), 1.0, 6.0, ((0, 32),))
    seq_lens = draw_seq_lens(jax.random.fold_in(arg_keys[13], 71), 0)
    expert_choice_keys = jax.random.split(jax.random.fold_in(arg_keys[3], 1), TOKENS // TOK_DEV)
    expert_choice_turns = jax.random.permutation(jax.random.fold_in(arg_keys[3], 3), TOKENS // TOK_DEV)
    expert_choice = jax.vmap(lambda own, number: shared_out(jax.random.fold_in(arg_keys[3], 2), own, number, TOK_DEV, EXPERTS, TOP, CAP, 1))(expert_choice_keys, expert_choice_turns).reshape((TOKENS, TOP))
    gain_attn = jnp.clip(1.0 + 0.18 * jax.random.normal(arg_keys[4], (MODEL_WIDTH,), jnp.float32), 0.099609375, 1.8984375).astype(jnp.bfloat16)
    w_query = bell_draw(arg_keys[5], (MODEL_WIDTH, QUERY_HEADS * HEAD_SIZE), MODEL_WIDTH ** -0.5, 0.1875, ((0, 32),))
    key_weight = bell_draw(arg_keys[6], (MODEL_WIDTH, KEY_VALUE_HEADS * HEAD_SIZE), MODEL_WIDTH ** -0.5, 0.1875, ((0, 32),))
    value_weight = bell_draw(arg_keys[7], (MODEL_WIDTH, KEY_VALUE_HEADS * HEAD_SIZE), MODEL_WIDTH ** -0.5, 0.1875, ((0, 32),))
    w_attn_out = bell_draw(arg_keys[8], (QUERY_HEADS * HEAD_SIZE, MODEL_WIDTH), (QUERY_HEADS * HEAD_SIZE // 8) ** -0.5, 0.5, ((0, 32),))
    gain_ffn = jnp.clip(1.0 + 0.18 * jax.random.normal(arg_keys[9], (MODEL_WIDTH,), jnp.float32), 0.099609375, 1.8984375).astype(jnp.bfloat16)
    w_router = bell_draw(arg_keys[10], (MODEL_WIDTH, EXPERTS), (2 * MODEL_WIDTH) ** -0.5, 0.125, ((0, 32),))
    w_expert_in = bell_draw(arg_keys[11], (MODEL_WIDTH, EXPERTS * 2 * FE), MODEL_WIDTH ** -0.5, 0.1875, ((0, 32),))
    w_expert_out = bell_draw(arg_keys[12], (FE, EXPERTS * MODEL_WIDTH), (FE // 4) ** -0.5, 0.5, ((0, 32),))
    return {"hidden_in": hidden_in, "grad_out": grad_out, "seq_lens": seq_lens, "expert_choice": expert_choice, "gain_attn": gain_attn, "w_query": w_query, "key_weight": key_weight, "value_weight": value_weight, "w_attn_out": w_attn_out, "gain_ffn": gain_ffn, "w_router": w_router, "w_expert_in": w_expert_in, "w_expert_out": w_expert_out}


@jax.custom_vjp
def low(v):
    return lax.optimization_barrier(v.astype(jnp.bfloat16)).astype(jnp.float32)

@jax.custom_vjp
def low_back(v):
    return v

def low_keep(v):
    return (low(v), None)

def low_pass(kept, grad):
    return (grad,)

def back_keep(v):
    return (v, None)

def back_low(kept, grad):
    return (low(grad),)
low.defvjp(low_keep, low_pass)
low_back.defvjp(back_keep, back_low)
eps = 1e-06
highest = lax.Precision.HIGHEST

def product(left, right):
    return jnp.dot(left, right, preferred_element_type=jnp.float32, precision=highest)

def rms_scale(values):
    return lax.rsqrt(lax.optimization_barrier(jnp.mean(values * values, axis=-1, keepdims=True)) + eps)

def layout(lengths, count_of_rows):
    microbatch_count = lengths.shape[0]
    microbatch_rows = count_of_rows // microbatch_count
    first_len = jnp.broadcast_to(lengths[:, 0:1], (microbatch_count, microbatch_rows))
    second_len = jnp.broadcast_to(lengths[:, 1:2], (microbatch_count, microbatch_rows))
    inner_grid = jnp.broadcast_to(jnp.arange(microbatch_rows, dtype=jnp.int32)[None, :], (microbatch_count, microbatch_rows))
    section = jnp.where(inner_grid < first_len, 0, jnp.where(inner_grid < first_len + second_len, 1, 2))
    allowed = (section[:, :, None] == section[:, None, :]) & (inner_grid[:, None, :] <= inner_grid[:, :, None])
    live_rows = (section < 2).astype(jnp.float32).reshape(count_of_rows, 1)
    return (live_rows, allowed)

def routing(choice_ids, capacity):
    count_of_rows, top_count = choice_ids.shape
    expert_ids = jnp.arange(EXPERTS, dtype=jnp.int32)
    expert_hits = (choice_ids[:, :, None] == expert_ids[None, None, :]).astype(jnp.int32)
    per_row = lax.optimization_barrier(jnp.sum(expert_hits, axis=1))
    before = jnp.cumsum(per_row, axis=0) - per_row
    position = lax.optimization_barrier(jnp.sum(expert_hits * before[:, None, :], axis=2))
    slot_index = (choice_ids * capacity + position).astype(jnp.int32)
    pair_index = jnp.arange(count_of_rows * top_count, dtype=jnp.int32)
    source = jnp.full((EXPERTS * capacity,), count_of_rows * top_count, jnp.int32).at[slot_index.reshape(-1)].set(pair_index)
    return (expert_hits, slot_index, source)

def block_forward(params, hidden, lengths, choice_ids):
    gain_attn, w_query, key_weight, value_weight, w_attn_out, gain_ffn, w_router, w_expert_in, w_expert_out = params
    count_of_rows = hidden.shape[0]
    microbatch_count = lengths.shape[0]
    microbatch_rows = count_of_rows // microbatch_count
    live_rows, allowed = layout(lengths, count_of_rows)
    normed = low(hidden * rms_scale(hidden) * gain_attn)
    query_rows = low(low_back(product(normed, w_query)))
    every_key = low(low_back(product(normed, key_weight)))
    every_value = low(low_back(product(normed, value_weight)))
    query_tiles = query_rows.reshape(microbatch_count, microbatch_rows, KEY_VALUE_HEADS, QUERY_HEADS // KEY_VALUE_HEADS, HEAD_SIZE)
    key_tiles = every_key.reshape(microbatch_count, microbatch_rows, KEY_VALUE_HEADS, HEAD_SIZE)
    value_tiles = every_value.reshape(microbatch_count, microbatch_rows, KEY_VALUE_HEADS, HEAD_SIZE)
    scores = low_back(jnp.einsum('mqgrd,mkgd->mgrqk', query_tiles, key_tiles, precision=highest) * 0.125)
    scores = jnp.where(allowed[:, None, None], scores, -1e+30)
    top_score = lax.optimization_barrier(jnp.max(scores, axis=-1, keepdims=True))
    weights = jnp.exp(scores - top_score)
    attn_probs = low(weights / lax.optimization_barrier(jnp.sum(weights, axis=-1, keepdims=True)))
    context = jnp.einsum('mgrqk,mkgd->mqgrd', attn_probs, value_tiles, precision=highest).reshape(count_of_rows, QUERY_HEADS * HEAD_SIZE)
    context = low(low_back(context))
    attended = low_back(product(context, w_attn_out))
    middle = hidden + live_rows * attended
    normed_ffn = low(middle * rms_scale(middle) * gain_ffn)
    logits = product(normed_ffn, w_router)
    expert_hits, slot_index, source = routing(choice_ids, CAP)
    chosen = lax.optimization_barrier(jnp.sum(expert_hits.astype(jnp.float32) * logits[:, None, :], axis=2))
    chosen_top = lax.optimization_barrier(jnp.max(chosen, axis=1, keepdims=True))
    gate_exp = jnp.exp(chosen - chosen_top)
    gate_weights = gate_exp / lax.optimization_barrier(jnp.sum(gate_exp, axis=1, keepdims=True))
    padded = jnp.concatenate([normed_ffn, jnp.zeros((1, MODEL_WIDTH), jnp.float32)], axis=0)
    dispatched = padded[source // TOP].reshape(EXPERTS, CAP, MODEL_WIDTH)
    gate_up = low_back(jnp.einsum('ecd,def->ecf', dispatched, w_expert_in.reshape(MODEL_WIDTH, EXPERTS, 2 * FE), precision=highest))
    gate_part = gate_up[:, :, :FE]
    up_part = gate_up[:, :, FE:]
    activated = low(gate_part * lax.logistic(gate_part) * up_part)
    expert_out = low_back(jnp.einsum('ecf,fed->ecd', activated, w_expert_out.reshape(FE, EXPERTS, MODEL_WIDTH), precision=highest))
    picked = expert_out.reshape(EXPERTS * CAP, MODEL_WIDTH)[slot_index]
    mixture = lax.optimization_barrier(jnp.sum(gate_weights[:, :, None] * picked, axis=1))
    return middle + live_rows * mixture

def reference(hidden_in, grad_out, seq_lens, expert_choice, gain_attn, w_query, key_weight, value_weight, w_attn_out, gain_ffn, w_router, w_expert_in, w_expert_out):
    params = tuple((weight.astype(jnp.float32) for weight in (gain_attn, w_query, key_weight, value_weight, w_attn_out, gain_ffn, w_router, w_expert_in, w_expert_out)))
    hidden_blocks = hidden_in.astype(jnp.float32).reshape(N_FSDP, TOK_DEV, MODEL_WIDTH)
    length_blocks = seq_lens.reshape(N_FSDP, MICRO, 2)
    choice_blocks = expert_choice.reshape(N_FSDP, TOK_DEV, TOP)
    forward_one = jax.checkpoint(block_forward)

    def forward_all(weights, blocks):
        return lax.map(lambda block_items: forward_one(weights, block_items[0], block_items[1], block_items[2]), (blocks, length_blocks, choice_blocks))
    outputs, pullback = jax.vjp(forward_all, params, hidden_blocks)
    grad_params, grad_hidden = pullback(grad_out.astype(jnp.float32).reshape(N_FSDP, TOK_DEV, MODEL_WIDTH))
    return (outputs.reshape(TOKENS, MODEL_WIDTH).astype(jnp.bfloat16), grad_hidden.reshape(TOKENS, MODEL_WIDTH).astype(jnp.bfloat16), grad_params[0], grad_params[1], grad_params[2], grad_params[3], grad_params[4], grad_params[5], grad_params[6], grad_params[7], grad_params[8])
```

```python
import jax
import jax.numpy as jnp
from jax import lax
from jax.experimental import pallas as pl
from jax.experimental.pallas import tpu as pltpu
from jax.sharding import PartitionSpec as P

MODEL_WIDTH = 1024
QUERY_HEADS = 16
KEY_VALUE_HEADS = 8
HEAD_SIZE = 64
FE = 512
EXPERTS = 4
TOP = 2
CAP = 80

ROWS = 128
STRIDE = 96
SLOTS = EXPERTS * STRIDE
QKV = (QUERY_HEADS + 2 * KEY_VALUE_HEADS) * HEAD_SIZE
EXTRA = 128
PLANE = 8
f32 = jnp.float32
bf16 = jnp.bfloat16

eps = 1e-06
highest = lax.Precision.HIGHEST
VMEM_LIMIT = 44 * 1024 * 1024


def mm(left, right, left_dim=1, right_dim=0):
    return lax.dot_general(
        left, right, (((left_dim,), (right_dim,)), ((), ())), preferred_element_type=f32
    )


def two_parts(values):
    high = values.astype(bf16)
    return high, (values - high.astype(f32)).astype(bf16)


def iota(shape, dim):
    return lax.broadcasted_iota(jnp.int32, shape, dim)


def row_scale(values):
    return lax.rsqrt(jnp.mean(values * values, axis=-1, keepdims=True) + eps)


def section_of(lens, place):
    batch = place >> 6
    inner = place & 63
    first = jnp.where(batch == 0, lens[0, 0], lens[1, 0])
    total = first + jnp.where(batch == 0, lens[0, 1], lens[1, 1])
    part = jnp.where(inner < first, 0, jnp.where(inner < total, 1, 2))
    return batch, part


def live_of(lens):
    _, part = section_of(lens, iota((ROWS, 1), 0))
    return (part < 2).astype(f32)


def allowed_of(lens):
    row, column = iota((ROWS, 1), 0), iota((1, ROWS), 1)
    row_batch, row_part = section_of(lens, row)
    column_batch, column_part = section_of(lens, column)
    return (
        (row_batch * 4 + row_part) == (column_batch * 4 + column_part)
    ) & (column <= row)


def slots_of(choice, mine):
    lane = iota((ROWS, 128), 1)
    named = [choice[:, k : k + 1] ^ mine for k in range(TOP)]
    hits = jnp.zeros((ROWS, 128), f32)
    for one in named:
        hits = hits + (lane == one).astype(f32)
    earlier = (iota((ROWS, ROWS), 1) < iota((ROWS, ROWS), 0)).astype(bf16)
    before = mm(earlier, hits.astype(bf16))
    places = []
    for one in named:
        position = jnp.sum(jnp.where(lane == one, before, 0.0), axis=1, keepdims=True)
        slot = one * STRIDE + position.astype(jnp.int32)
        places.append((iota((ROWS, SLOTS), 1) == slot).astype(f32).astype(bf16))
    return named, places


def owner(pos, planes_off, chip_off, core_off):
    return ((pos[0] ^ planes_off) * 4 + (pos[1] ^ chip_off)) * 2 + (pos[2] ^ core_off)


def load_rows(pos, pieces, buffer, sems, rows, planes):
    copies = []
    for core in range(2):
        for chip in range(4):
            for k in range(planes):
                place = pl.multiple_of(owner(pos, k, chip, core) * rows, rows)
                copies.append(
                    pltpu.make_async_copy(
                        pieces[core * 4 + chip].at[k],
                        buffer.at[pl.ds(place, rows)],
                        sems.at[len(copies)],
                    )
                )
    for copy in copies:
        copy.start()
    return copies


def store_rows(pos, buffer, kept, sent, sems, rows, planes):
    copies = []
    for core, target in ((1, sent), (0, kept)):
        for chip in range(4):
            for k in range(planes):
                place = pl.multiple_of(owner(pos, k, chip, core) * rows, rows)
                copies.append(
                    pltpu.make_async_copy(
                        buffer.at[pl.ds(place, rows)], target.at[chip, k], sems.at[len(copies)]
                    )
                )
    for copy in copies:
        copy.start()
    return copies


def cotangent_kernel(pos, lens, choice_ref, grad_ref, *outs):
    _, places = slots_of(choice_ref[...], pos[1])
    grad_mix = (live_of(lens) * grad_ref[...].astype(f32)).astype(bf16)
    slotted = mm(places[0] + places[1], grad_mix, 0, 0)
    for f in range(EXPERTS):
        outs[f][...] = slotted[f * STRIDE : f * STRIDE + CAP].astype(bf16)


def masked_probs(allowed, queries, keys):
    raw = mm(queries, keys, 1, 1) * 0.125
    scores = jnp.where(allowed, raw, -1e30)
    weights = jnp.exp(scores - jnp.max(scores, axis=-1, keepdims=True))
    return weights / jnp.sum(weights, axis=-1, keepdims=True)


def head(kind, h):
    base = {"q": 0, "k": QUERY_HEADS, "v": QUERY_HEADS + KEY_VALUE_HEADS}[kind]
    return slice((base + h) * HEAD_SIZE, (base + h + 1) * HEAD_SIZE)


def attention_kernel(planes, rows, pos, lens, hidden_ref, *refs):
    pieces = refs[:8]
    normed_ref, qkv_ref, context_ref, gains_ref, weights, sems = refs[8:]
    copies = load_rows(pos, pieces, weights, sems, rows, planes)
    hidden = hidden_ref[...].astype(f32)
    unit = hidden * row_scale(hidden)
    allowed = allowed_of(lens)
    for copy in copies:
        copy.wait()
    pick = (iota((16, EXTRA), 0) == iota((16, EXTRA), 1)).astype(f32).astype(bf16)
    gains = mm(pick, weights[:, QKV:], 1, 1)
    gains_ref[...] = gains
    normed = (unit * gains[0:1]).astype(bf16)
    normed_ref[...] = normed
    for at in range(0, QKV, 512):
        qkv_ref[:, at : at + 512] = mm(normed, weights[:, at : at + 512]).astype(bf16)
    group = QUERY_HEADS // KEY_VALUE_HEADS
    for g in range(KEY_VALUE_HEADS):
        keys, values = qkv_ref[:, head("k", g)], qkv_ref[:, head("v", g)]
        for h in range(g * group, (g + 1) * group):
            probs = masked_probs(allowed, qkv_ref[:, head("q", h)], keys).astype(bf16)
            context_ref[:, h * HEAD_SIZE : (h + 1) * HEAD_SIZE] = mm(probs, values).astype(bf16)


def router_gates(named, normed_ffn, gains):
    logits = mm(normed_ffn, gains.astype(bf16), 1, 1)
    chosen = []
    for one in named:
        value = jnp.zeros((ROWS, 1), f32)
        for k in range(EXPERTS):
            value = value + jnp.where(one == k, logits[:, 2 + k : 3 + k], 0.0)
        chosen.append(value)
    top = jnp.maximum(chosen[0], chosen[1])
    exps = [jnp.exp(value - top) for value in chosen]
    total = exps[0] + exps[1]
    return [value / total for value in exps]


def dispatch_kernel(planes, rows, pos, lens, choice_ref, hidden_ref, context_ref, gains_ref, *refs):
    pieces = refs[:8]
    middle_ref, gates_ref = refs[8:10]
    outs = refs[10:14]
    weights, sems = refs[14:]
    copies = load_rows(pos, pieces, weights, sems, rows, planes)
    choice = choice_ref[...]
    _, places = slots_of(choice, pos[1])
    for copy in copies:
        copy.wait()
    attended = mm(context_ref[...], weights[...])
    middle = hidden_ref[...].astype(f32) + live_of(lens) * attended
    middle_ref[...] = middle
    gains = gains_ref[...]
    normed_ffn = (middle * row_scale(middle) * gains[1:2]).astype(bf16)
    gates = router_gates([choice[:, k : k + 1] for k in range(TOP)], normed_ffn, gains)
    lane = iota((ROWS, 128), 1)
    gates_ref[...] = jnp.where(lane == 0, gates[0], jnp.where(lane == 1, gates[1], 0.0))
    slotted = mm(places[0] + places[1], normed_ffn, 0, 0)
    beside = jnp.zeros((SLOTS, EXTRA), f32)
    for place, gate in zip(places, gates):
        high, low = two_parts(gate)
        columns = jnp.where(
            lane == 0, high.astype(f32), jnp.where(lane == 1, low.astype(f32), 0.0)
        ).astype(bf16)
        beside = beside + mm(place, columns, 0, 0)
    for f in range(EXPERTS):
        part = slice(f * STRIDE, f * STRIDE + CAP)
        outs[f][:, :MODEL_WIDTH] = slotted[part].astype(bf16)
        outs[f][:, MODEL_WIDTH:] = beside[part].astype(bf16)


def expert_kernel(planes, rows_in, rows_out, pos, *refs):
    tokens, grads, pieces = refs[:4], refs[4:8], refs[8 : 8 + 2 * planes]
    refs = refs[8 + 2 * planes :]
    backs, kept, sent = refs[:4], refs[4], refs[5]
    w_in, w_out, d_in, d_out, sems = refs[6:]
    both = rows_in + rows_out
    copies = []
    places = []
    for core in range(2):
        for k in range(planes):
            for chip in range(4):
                who = owner(pos, k, chip, core)
                in_rows = pl.ds(pl.multiple_of(who * rows_in, rows_in), rows_in)
                out_rows = pl.ds(pl.multiple_of(who * rows_out, rows_out), rows_out)
                places.append((core, k, chip, in_rows, out_rows))
                source = pieces[core * planes + k]
                copies.append(
                    pltpu.make_async_copy(
                        source.at[chip, pl.ds(0, rows_in)], w_in.at[in_rows], sems.at[len(copies)]
                    )
                )
                copies.append(
                    pltpu.make_async_copy(
                        source.at[chip, pl.ds(rows_in, rows_out)],
                        w_out.at[out_rows],
                        sems.at[len(copies)],
                    )
                )
    for copy in copies:
        copy.start()
    x = jnp.concatenate([ref[:, :MODEL_WIDTH] for ref in tokens], axis=0)
    gate_slots = jnp.concatenate(
        [
            ref[:, MODEL_WIDTH : MODEL_WIDTH + 1].astype(f32)
            + ref[:, MODEL_WIDTH + 1 : MODEL_WIDTH + 2].astype(f32)
            for ref in tokens
        ],
        axis=0,
    )
    dy = jnp.concatenate([ref[...] for ref in grads], axis=0)
    d_expert = (gate_slots * dy.astype(f32)).astype(bf16)
    for copy in copies:
        copy.wait()
    gate = mm(x, w_in[:, :FE])
    up = mm(x, w_in[:, FE:])
    sig = 1.0 / (1.0 + jnp.exp(-gate))
    silu = gate * sig
    activated = (silu * up).astype(bf16)
    expert_out = mm(activated, w_out[...]).astype(bf16)
    d_act = mm(d_expert, w_out[...], 1, 1)
    d_gate = (d_act * up * (sig * (1.0 + gate * (1.0 - sig)))).astype(bf16)
    d_up = (d_act * silu).astype(bf16)
    d_x = (mm(d_gate, w_in[:, :FE], 1, 1) + mm(d_up, w_in[:, FE:], 1, 1)).astype(bf16)
    for f in range(EXPERTS):
        backs[f][:CAP] = expert_out[f * CAP : (f + 1) * CAP]
        backs[f][CAP:] = d_x[f * CAP : (f + 1) * CAP]
    d_out[...] = mm(activated, d_expert, 0, 0).astype(bf16)
    d_in[:, :FE] = mm(x, d_gate, 0, 0).astype(bf16)
    d_in[:, FE:] = mm(x, d_up, 0, 0).astype(bf16)
    stores = []
    for core, k, chip, in_rows, out_rows in places:
        target = (kept if core == 0 else sent).at[k, chip]
        stores.append(
            pltpu.make_async_copy(
                d_in.at[in_rows], target.at[pl.ds(0, rows_in)], sems.at[len(stores)]
            )
        )
        stores.append(
            pltpu.make_async_copy(
                d_out.at[out_rows], target.at[pl.ds(rows_in, rows_out)], sems.at[len(stores)]
            )
        )
    for copy in stores:
        copy.start()
    for copy in stores:
        copy.wait()


def combine_kernel(
    planes, rows, pos, lens, choice_ref, middle_ref, gates_ref, grad_ref, gains_ref, context_ref, *refs
):
    backs, pieces = refs[:4], refs[4:12]
    out_ref, grad_middle_ref, grad_context_ref, kept, sent = refs[12:17]
    weights, d_weights, sems = refs[17:]
    copies = load_rows(pos, pieces, weights, sems, rows, planes)
    choice = choice_ref[...]
    _, places = slots_of(choice, pos[1])
    live = live_of(lens)
    empty = jnp.zeros((STRIDE - CAP, MODEL_WIDTH), bf16)
    outs, grads = [], []
    for back in backs:
        outs += [back[:CAP], empty]
        grads += [back[CAP:], empty]
    outs = jnp.concatenate(outs, axis=0)
    grads = jnp.concatenate(grads, axis=0)
    picked = [mm(place, outs) for place in places]
    gates = [gates_ref[:, k : k + 1] for k in range(TOP)]
    middle = middle_ref[...]
    mixture = gates[0] * picked[0] + gates[1] * picked[1]
    out_ref[...] = (middle + live * mixture).astype(bf16)
    cotangent = grad_ref[...].astype(f32)
    grad_mix = live * cotangent
    grad_gates = [jnp.sum(grad_mix * one, axis=1, keepdims=True) for one in picked]
    total = gates[0] * grad_gates[0] + gates[1] * grad_gates[1]
    grad_chosen = [gate * (grad - total) for gate, grad in zip(gates, grad_gates)]
    gains = gains_ref[...]
    grad_normed = mm(places[0] + places[1], grads)
    lane = iota((ROWS, EXTRA), 1)
    grad_logits = jnp.zeros((ROWS, EXTRA), f32)
    for k in range(EXPERTS):
        one = jnp.zeros((ROWS, 1), f32)
        for choice_at in range(TOP):
            one = one + jnp.where(choice[:, choice_at : choice_at + 1] == k, grad_chosen[choice_at], 0.0)
        grad_normed = grad_normed + one * gains[2 + k : 3 + k]
        grad_logits = jnp.where(lane == 2 + k, one, grad_logits)
    scale = row_scale(middle)
    unit = middle * scale
    normed_ffn = (unit * gains[1:2]).astype(bf16)
    logits_high, logits_low = two_parts(grad_logits)
    gain_high, gain_low = two_parts(grad_normed * unit)
    first = (lane == 1).astype(f32).astype(bf16)
    d_weights[:, MODEL_WIDTH:] = (
        mm(normed_ffn, logits_high, 0, 0)
        + mm(normed_ffn, logits_low, 0, 0)
        + mm(gain_high, first, 0, 0)
        + mm(gain_low, first, 0, 0)
    ).astype(bf16)
    scaled = grad_normed * gains[1:2]
    grad_middle = cotangent + scale * (
        scaled - unit * jnp.mean(scaled * unit, axis=-1, keepdims=True)
    )
    grad_middle_ref[...] = grad_middle
    grad_attended = (live * grad_middle).astype(bf16)
    for copy in copies:
        copy.wait()
    grad_context_ref[...] = mm(grad_attended, weights[...], 1, 1).astype(bf16)
    context = context_ref[...]
    for at in range(0, MODEL_WIDTH, 512):
        d_weights[:, at : at + 512] = mm(context, grad_attended[:, at : at + 512], 0, 0).astype(bf16)
    stores = store_rows(pos, d_weights, kept, sent, sems, rows, planes)
    for copy in stores:
        copy.wait()


def attention_back_kernel(
    planes, rows, pos, lens, hidden_ref, normed_ref, qkv_ref, grad_context_ref, grad_middle_ref, gains_ref, *refs
):
    pieces = refs[:8]
    grad_in_ref, kept, sent, weights, d_weights, grads, sems = refs[8:]
    copies = load_rows(pos, pieces, weights, sems, rows, planes)
    allowed = allowed_of(lens)
    group = QUERY_HEADS // KEY_VALUE_HEADS
    for g in range(KEY_VALUE_HEADS):
        keys, values = qkv_ref[:, head("k", g)], qkv_ref[:, head("v", g)]
        d_keys = jnp.zeros((ROWS, HEAD_SIZE), f32)
        d_values = jnp.zeros((ROWS, HEAD_SIZE), f32)
        for h in range(g * group, (g + 1) * group):
            queries = qkv_ref[:, head("q", h)]
            probs = masked_probs(allowed, queries, keys)
            d_context = grad_context_ref[:, h * HEAD_SIZE : (h + 1) * HEAD_SIZE]
            d_probs = mm(d_context, values, 1, 1)
            d_values = d_values + mm(probs.astype(bf16), d_context, 0, 0)
            d_scores = (
                probs * (d_probs - jnp.sum(probs * d_probs, axis=-1, keepdims=True))
            ).astype(bf16)
            grads[:, head("q", h)] = (mm(d_scores, keys) * 0.125).astype(bf16)
            d_keys = d_keys + mm(d_scores, queries, 0, 0)
        grads[:, head("k", g)] = (d_keys * 0.125).astype(bf16)
        grads[:, head("v", g)] = d_values.astype(bf16)
    normed = normed_ref[...]
    for at in range(0, QKV, 512):
        d_weights[:, at : at + 512] = mm(normed, grads[:, at : at + 512], 0, 0).astype(bf16)
    for copy in copies:
        copy.wait()
    grad_normed = mm(grads[...], weights[:, :QKV], 1, 1)
    hidden = hidden_ref[...].astype(f32)
    scale = row_scale(hidden)
    unit = hidden * scale
    gain_high, gain_low = two_parts(grad_normed * unit)
    first = (iota((ROWS, EXTRA), 1) == 0).astype(f32).astype(bf16)
    d_weights[:, QKV:] = (mm(gain_high, first, 0, 0) + mm(gain_low, first, 0, 0)).astype(bf16)
    stores = store_rows(pos, d_weights, kept, sent, sems, rows, planes)
    scaled = grad_normed * gains_ref[0:1, :]
    grad_hidden = grad_middle_ref[...] + scale * (
        scaled - unit * jnp.mean(scaled * unit, axis=-1, keepdims=True)
    )
    grad_in_ref[...] = grad_hidden.astype(bf16)
    for copy in stores:
        copy.wait()


def call(kernel, operands, n_scalars, n_any, outs, any_outs, scratch, flops, name):
    n_plain = len(operands) - n_scalars - n_any
    here = pl.BlockSpec(memory_space=pltpu.VMEM)
    there = pl.BlockSpec(memory_space=pl.ANY)
    scalar = pl.BlockSpec(memory_space=pltpu.SMEM)
    moved = sum(v.size * v.dtype.itemsize for v in operands)
    moved += sum(v.size * v.dtype.itemsize for v in outs)
    return pl.pallas_call(
        kernel,
        out_shape=tuple(outs),
        in_specs=[scalar] * n_scalars + [here] * n_plain + [there] * n_any,
        out_specs=tuple(there if i in any_outs else here for i in range(len(outs))),
        scratch_shapes=scratch,
        compiler_params=pltpu.CompilerParams(vmem_limit_bytes=VMEM_LIMIT),
        cost_estimate=pl.CostEstimate(flops=flops, bytes_accessed=moved, transcendentals=0),
        name=name,
    )(*operands)


def exchanged(
    hidden_in,
    grad_out,
    seq_lens,
    expert_choice,
    gain_attn,
    w_query,
    key_weight,
    value_weight,
    w_attn_out,
    gain_ffn,
    w_router,
    w_expert_in,
    w_expert_out,
):
    n = lax.axis_size("fsdp")
    planes = n // PLANE
    me = lax.axis_index("fsdp")
    plane, chip, core = me // PLANE, (me // 2) % 4, me % 2
    pos = jnp.stack([plane, chip, core]).astype(jnp.int32)
    rows = w_query.shape[0]
    rows_out = w_expert_out.shape[0]
    both = rows + rows_out

    def swap(value, offset):
        return lax.ppermute(value, "fsdp", [(i, i ^ offset) for i in range(n)])

    def gathered(shard):
        column = jnp.stack([shard] + [swap(shard, PLANE * k) for k in range(1, planes)])
        chips = [column] + [swap(column, 2 * f) for f in range(1, 4)]
        return chips + [swap(one, 1) for one in chips]

    def added(values):
        total = values[0].astype(f32)
        for one in values[1:]:
            total = total + one.astype(f32)
        return total

    def scattered(kept, sent):
        other = swap(sent, 1)
        parts = [(kept[f].astype(f32) + other[f].astype(f32)).astype(bf16) for f in range(4)]
        column = added([parts[0]] + [swap(parts[f], 2 * f) for f in range(1, 4)]).astype(bf16)
        return added([column[0]] + [swap(column[k], PLANE * k) for k in range(1, planes)])

    beside = jnp.concatenate(
        [gain_attn[:, None], gain_ffn[:, None], w_router, jnp.zeros((rows, EXTRA - 6), bf16)], axis=1
    )
    qkv_pieces = gathered(
        jnp.concatenate([w_query, key_weight, value_weight, beside], axis=1)
    )
    out_pieces = gathered(w_attn_out)

    by_expert = jnp.concatenate(
        [
            w_expert_in.reshape(rows, EXPERTS, 2 * FE),
            w_expert_out.reshape(rows_out, EXPERTS, MODEL_WIDTH),
        ],
        axis=0,
    ).transpose(1, 0, 2)
    mine = [lax.dynamic_index_in_dim(by_expert, chip ^ f, 0, False) for f in range(4)]
    shard = jnp.stack([mine[0]] + [swap(mine[f], 2 * f) for f in range(1, 4)])
    expert_pieces = [shard] + [swap(shard, PLANE * k) for k in range(1, planes)]
    expert_pieces = expert_pieces + [swap(one, 1) for one in expert_pieces]

    def array(*shape, dtype=bf16):
        return jax.ShapeDtypeStruct(shape, dtype)

    grad_slots = call(
        cotangent_kernel,
        (pos, seq_lens, expert_choice, grad_out),
        2,
        0,
        [array(CAP, MODEL_WIDTH)] * 4,
        (),
        [],
        10**8,
        "slot_cotangents",
    )
    grad_slots = [grad_slots[0]] + [swap(grad_slots[f], 2 * f) for f in range(1, 4)]

    n_copies = 8 * planes
    normed, qkv, context, gains = call(
        lambda *refs: attention_kernel(planes, rows, *refs),
        (pos, seq_lens, hidden_in, *qkv_pieces),
        2,
        8,
        [
            array(ROWS, MODEL_WIDTH),
            array(ROWS, QKV),
            array(ROWS, MODEL_WIDTH),
            array(16, MODEL_WIDTH, dtype=f32),
        ],
        (),
        [pltpu.VMEM((MODEL_WIDTH, QKV + EXTRA), bf16), pltpu.SemaphoreType.DMA((n_copies,))],
        10**9,
        "attention",
    )
    middle, gates, *dispatched = call(
        lambda *refs: dispatch_kernel(planes, rows, *refs),
        (pos, seq_lens, expert_choice, hidden_in, context, gains, *out_pieces),
        2,
        8,
        [array(ROWS, MODEL_WIDTH, dtype=f32), array(ROWS, 128, dtype=f32)]
        + [array(CAP, MODEL_WIDTH + EXTRA)] * 4,
        (),
        [pltpu.VMEM((MODEL_WIDTH, MODEL_WIDTH), bf16), pltpu.SemaphoreType.DMA((n_copies,))],
        10**9,
        "dispatch",
    )
    dispatched = [dispatched[0]] + [swap(dispatched[f], 2 * f) for f in range(1, 4)]

    *backs, kept, sent = call(
        lambda *refs: expert_kernel(planes, rows, rows_out, *refs),
        (pos, *dispatched, *grad_slots, *expert_pieces),
        1,
        2 * planes,
        [array(2 * CAP, MODEL_WIDTH)] * 4 + [array(planes, 4, both, MODEL_WIDTH)] * 2,
        (4, 5),
        [
            pltpu.VMEM((MODEL_WIDTH, 2 * FE), bf16),
            pltpu.VMEM((FE, MODEL_WIDTH), bf16),
            pltpu.VMEM((MODEL_WIDTH, 2 * FE), bf16),
            pltpu.VMEM((FE, MODEL_WIDTH), bf16),
            pltpu.SemaphoreType.DMA((2 * n_copies,)),
        ],
        3 * 10**9,
        "experts",
    )
    backs = [backs[0]] + [swap(backs[f], 2 * f) for f in range(1, 4)]
    other = swap(sent, 1)
    parts = [(kept[k].astype(f32) + other[k].astype(f32)).astype(bf16) for k in range(planes)]
    mine = added([parts[0]] + [swap(parts[k], PLANE * k) for k in range(1, planes)]).astype(bf16)
    mine = [mine[0]] + [swap(mine[f], 2 * f) for f in range(1, 4)]

    def placed(pieces, first, count):
        grid = jnp.stack([one[first : first + count] for one in pieces]).astype(f32)
        order = jnp.arange(4, dtype=jnp.int32) ^ chip
        return jnp.take(grid, order, axis=0).transpose(1, 0, 2).reshape(count, -1)

    grad_w_expert_in = placed(mine, 0, rows)
    grad_w_expert_out = placed(mine, rows, rows_out)

    block_output, grad_middle, grad_context, kept, sent = call(
        lambda *refs: combine_kernel(planes, rows, *refs),
        (
            pos,
            seq_lens,
            expert_choice,
            middle,
            gates,
            grad_out,
            gains,
            context,
            *backs,
            *out_pieces,
        ),
        2,
        8,
        [
            array(ROWS, MODEL_WIDTH),
            array(ROWS, MODEL_WIDTH, dtype=f32),
            array(ROWS, MODEL_WIDTH),
        ]
        + [array(4, planes, rows, MODEL_WIDTH + EXTRA)] * 2,
        (3, 4),
        [
            pltpu.VMEM((MODEL_WIDTH, MODEL_WIDTH), bf16),
            pltpu.VMEM((MODEL_WIDTH, MODEL_WIDTH + EXTRA), bf16),
            pltpu.SemaphoreType.DMA((n_copies,)),
        ],
        10**9,
        "combine",
    )
    owned_out = scattered(kept, sent)

    grad_in, kept, sent = call(
        lambda *refs: attention_back_kernel(planes, rows, *refs),
        (
            pos,
            seq_lens,
            hidden_in,
            normed,
            qkv,
            grad_context,
            grad_middle,
            gains,
            *qkv_pieces,
        ),
        2,
        8,
        [array(ROWS, MODEL_WIDTH)] + [array(4, planes, rows, QKV + EXTRA)] * 2,
        (1, 2),
        [
            pltpu.VMEM((MODEL_WIDTH, QKV + EXTRA), bf16),
            pltpu.VMEM((MODEL_WIDTH, QKV + EXTRA), bf16),
            pltpu.VMEM((ROWS, QKV), bf16),
            pltpu.SemaphoreType.DMA((n_copies,)),
        ],
        2 * 10**9,
        "attention_back",
    )
    owned_qkv = scattered(kept, sent)
    q_end = QUERY_HEADS * HEAD_SIZE
    k_end = q_end + KEY_VALUE_HEADS * HEAD_SIZE
    return (
        block_output,
        grad_in,
        owned_qkv[:, QKV],
        owned_qkv[:, :q_end],
        owned_qkv[:, q_end:k_end],
        owned_qkv[:, k_end:QKV],
        owned_out[:, :MODEL_WIDTH],
        owned_out[:, MODEL_WIDTH + 1],
        owned_out[:, MODEL_WIDTH + 2 : MODEL_WIDTH + 2 + EXPERTS],
        grad_w_expert_in,
        grad_w_expert_out,
    )


def rms_scale(values):
    return lax.rsqrt(jnp.mean(values * values, axis=-1, keepdims=True) + eps)


def layout(lengths, count_of_rows):
    microbatch_count = lengths.shape[0]
    microbatch_rows = count_of_rows // microbatch_count
    first_len = jnp.broadcast_to(lengths[:, 0:1], (microbatch_count, microbatch_rows))
    second_len = jnp.broadcast_to(lengths[:, 1:2], (microbatch_count, microbatch_rows))
    inner_grid = jnp.broadcast_to(
        jnp.arange(microbatch_rows, dtype=jnp.int32)[None, :], (microbatch_count, microbatch_rows)
    )
    section = jnp.where(
        inner_grid < first_len, 0, jnp.where(inner_grid < first_len + second_len, 1, 2)
    )
    allowed = (section[:, :, None] == section[:, None, :]) & (
        inner_grid[:, None, :] <= inner_grid[:, :, None]
    )
    live_rows = (section < 2).astype(jnp.float32).reshape(count_of_rows, 1)
    return (live_rows, allowed)


def routing(choice_ids, capacity):
    count_of_rows, top_count = choice_ids.shape
    expert_ids = jnp.arange(EXPERTS, dtype=jnp.int32)
    expert_hits = (choice_ids[:, :, None] == expert_ids[None, None, :]).astype(jnp.int32)
    per_row = jnp.sum(expert_hits, axis=1)
    before = jnp.cumsum(per_row, axis=0) - per_row
    position = jnp.sum(expert_hits * before[:, None, :], axis=2)
    slot_index = choice_ids * capacity + position
    pair_index = jnp.arange(count_of_rows * top_count, dtype=jnp.int32)
    source = (
        jnp.full((EXPERTS * capacity,), count_of_rows * top_count, jnp.int32)
        .at[slot_index.reshape(-1)]
        .set(pair_index)
    )
    return (expert_hits, slot_index, source)


def shards(
    hidden_in,
    grad_out,
    seq_lens,
    expert_choice,
    gain_attn,
    w_query,
    key_weight,
    value_weight,
    w_attn_out,
    gain_ffn,
    w_router,
    w_expert_in,
    w_expert_out,
):
    count_of_rows = hidden_in.shape[0]
    microbatch_count = seq_lens.shape[0]
    microbatch_rows = count_of_rows // microbatch_count
    query_group_size = QUERY_HEADS // KEY_VALUE_HEADS
    device_count = lax.axis_size("fsdp")
    live_rows, allowed = layout(seq_lens, count_of_rows)
    mask_grid = allowed[:, None, None]
    hidden = hidden_in.astype(jnp.float32)
    cotangent = grad_out.astype(jnp.float32)
    attention_set = (
        lax.all_gather(gain_attn, "fsdp", axis=0, tiled=True),
        lax.all_gather(w_query, "fsdp", axis=0, tiled=True),
        lax.all_gather(key_weight, "fsdp", axis=0, tiled=True),
        lax.all_gather(value_weight, "fsdp", axis=0, tiled=True),
        lax.all_gather(w_attn_out, "fsdp", axis=0, tiled=True),
        lax.all_gather(gain_ffn, "fsdp", axis=0, tiled=True),
        lax.all_gather(w_router, "fsdp", axis=0, tiled=True),
    )
    gain_one = attention_set[0].astype(jnp.float32)
    gain_two = attention_set[5].astype(jnp.float32)
    scale_one = rms_scale(hidden)
    unit_one = hidden * scale_one
    normed = (unit_one * gain_one).astype(jnp.bfloat16)
    query_rows = jnp.dot(normed, attention_set[1], preferred_element_type=jnp.float32).astype(
        jnp.bfloat16
    )
    every_key = jnp.dot(normed, attention_set[2], preferred_element_type=jnp.float32).astype(
        jnp.bfloat16
    )
    every_value = jnp.dot(normed, attention_set[3], preferred_element_type=jnp.float32).astype(
        jnp.bfloat16
    )
    query_tiles = query_rows.reshape(
        microbatch_count, microbatch_rows, KEY_VALUE_HEADS, query_group_size, HEAD_SIZE
    )
    key_tiles = every_key.reshape(microbatch_count, microbatch_rows, KEY_VALUE_HEADS, HEAD_SIZE)
    value_tiles = every_value.reshape(microbatch_count, microbatch_rows, KEY_VALUE_HEADS, HEAD_SIZE)

    def score_block():
        raw_scores = (
            jnp.einsum(
                "mqgrd,mkgd->mgrqk", query_tiles, key_tiles, preferred_element_type=jnp.float32
            )
            * 0.125
        )
        return jnp.where(mask_grid, raw_scores, -1e30)

    scores = score_block()
    top_score = jnp.max(scores, axis=-1, keepdims=True)
    weights = jnp.exp(scores - top_score)
    row_total = jnp.sum(weights, axis=-1, keepdims=True)
    probs_low = (weights / row_total).astype(jnp.bfloat16)
    context = jnp.einsum(
        "mgrqk,mkgd->mqgrd", probs_low, value_tiles, preferred_element_type=jnp.float32
    )
    context = context.reshape(count_of_rows, QUERY_HEADS * HEAD_SIZE).astype(jnp.bfloat16)
    attended = jnp.dot(context, attention_set[4], preferred_element_type=jnp.float32)
    middle = hidden + live_rows * attended
    scale_two = rms_scale(middle)
    unit_two = middle * scale_two
    normed_ffn = (unit_two * gain_two).astype(jnp.bfloat16)
    logits = jnp.dot(normed_ffn, attention_set[6], preferred_element_type=jnp.float32)
    expert_hits, slot_index, source = routing(expert_choice, CAP)
    hits_float = expert_hits.astype(jnp.float32)
    chosen = jnp.sum(hits_float * logits[:, None, :], axis=2)
    chosen_top = jnp.max(chosen, axis=1, keepdims=True)
    gate_exp = jnp.exp(chosen - chosen_top)
    gate_weights = gate_exp / jnp.sum(gate_exp, axis=1, keepdims=True)
    padded = jnp.concatenate([normed_ffn, jnp.zeros((1, MODEL_WIDTH), jnp.bfloat16)], axis=0)
    dispatched = padded[source // TOP].reshape(EXPERTS, CAP, MODEL_WIDTH)
    expert_in_full = lax.all_gather(w_expert_in, "fsdp", axis=0, tiled=True)
    expert_out_full = lax.all_gather(w_expert_out, "fsdp", axis=0, tiled=True)
    in_grid = expert_in_full.reshape(MODEL_WIDTH, EXPERTS, 2 * FE)
    out_grid = expert_out_full.reshape(FE, EXPERTS, MODEL_WIDTH)
    gate_up = jnp.einsum("ecd,def->ecf", dispatched, in_grid, preferred_element_type=jnp.float32)
    gate_part = gate_up[:, :, :FE]
    up_part = gate_up[:, :, FE:]
    sigmoid_gate = lax.logistic(gate_part)
    silu_gate = gate_part * sigmoid_gate
    activated = (silu_gate * up_part).astype(jnp.bfloat16)
    expert_out = jnp.einsum("ecf,fed->ecd", activated, out_grid, preferred_element_type=jnp.float32)
    picked = expert_out.reshape(EXPERTS * CAP, MODEL_WIDTH)[slot_index]
    mixture = jnp.sum(gate_weights[:, :, None] * picked, axis=1)
    block_output = (middle + live_rows * mixture).astype(jnp.bfloat16)
    back_set = (
        lax.all_gather(gain_attn, "fsdp", axis=0, tiled=True),
        lax.all_gather(w_query, "fsdp", axis=0, tiled=True),
        lax.all_gather(key_weight, "fsdp", axis=0, tiled=True),
        lax.all_gather(value_weight, "fsdp", axis=0, tiled=True),
        lax.all_gather(w_attn_out, "fsdp", axis=0, tiled=True),
        lax.all_gather(gain_ffn, "fsdp", axis=0, tiled=True),
        lax.all_gather(w_router, "fsdp", axis=0, tiled=True),
    )
    out_back = lax.all_gather(w_expert_out, "fsdp", axis=0, tiled=True).reshape(
        FE, EXPERTS, MODEL_WIDTH
    )
    in_back = lax.all_gather(w_expert_in, "fsdp", axis=0, tiled=True).reshape(
        MODEL_WIDTH, EXPERTS, 2 * FE
    )
    grad_mix = live_rows * cotangent
    grad_gates = jnp.sum(grad_mix[:, None, :] * picked, axis=2)
    grad_chosen = gate_weights * (
        grad_gates - jnp.sum(gate_weights * grad_gates, axis=1, keepdims=True)
    )
    grad_logits = jnp.sum(grad_chosen[:, :, None] * hits_float, axis=1)
    pair_grads = (gate_weights[:, :, None] * grad_mix[:, None, :]).reshape(
        count_of_rows * TOP, MODEL_WIDTH
    )
    pair_padded = jnp.concatenate([pair_grads, jnp.zeros((1, MODEL_WIDTH), jnp.float32)], axis=0)
    grad_expert_out = pair_padded[source].astype(jnp.bfloat16).reshape(EXPERTS, CAP, MODEL_WIDTH)
    grad_activated = jnp.einsum(
        "ecd,fed->ecf", grad_expert_out, out_back, preferred_element_type=jnp.float32
    )
    out_rows = w_expert_out.shape[0]
    columns = activated
    grad_w_expert_out = lax.psum_scatter(
        jnp.einsum(
            "ecn,ecd->ned", columns, grad_expert_out, preferred_element_type=jnp.float32
        ).reshape(1 * lax.axis_size("fsdp"), out_rows * EXPERTS * MODEL_WIDTH),
        "fsdp",
        scatter_dimension=0,
        tiled=True,
    ).reshape(out_rows, EXPERTS * MODEL_WIDTH)
    grad_gate = grad_activated * up_part * (sigmoid_gate * (1.0 + gate_part * (1.0 - sigmoid_gate)))
    grad_up = grad_activated * silu_gate
    grad_gate_up = jnp.concatenate([grad_gate, grad_up], axis=-1).astype(jnp.bfloat16)
    grad_dispatched = jnp.einsum(
        "ecf,def->ecd", grad_gate_up, in_back, preferred_element_type=jnp.float32
    )
    in_rows = w_expert_in.shape[0]
    columns = dispatched
    grad_w_expert_in = lax.psum_scatter(
        jnp.einsum(
            "ecn,ecf->nef", columns, grad_gate_up, preferred_element_type=jnp.float32
        ).reshape(1 * lax.axis_size("fsdp"), in_rows * EXPERTS * 2 * FE),
        "fsdp",
        scatter_dimension=0,
        tiled=True,
    ).reshape(in_rows, EXPERTS * 2 * FE)
    router_full = back_set[6].astype(jnp.float32)
    grad_normed_ffn = jnp.sum(
        grad_dispatched.reshape(EXPERTS * CAP, MODEL_WIDTH)[slot_index], axis=1
    )
    grad_normed_ffn = grad_normed_ffn + jnp.dot(grad_logits, router_full.T, precision=highest)
    grad_router = jnp.dot(normed_ffn.astype(jnp.float32).T, grad_logits, precision=highest)
    back_gain_two = back_set[5].astype(jnp.float32)
    grad_gain_two = jnp.sum(grad_normed_ffn * unit_two, axis=0)
    scaled_two = grad_normed_ffn * back_gain_two
    grad_middle = cotangent + scale_two * (
        scaled_two - unit_two * jnp.mean(scaled_two * unit_two, axis=-1, keepdims=True)
    )
    grad_attended = (live_rows * grad_middle).astype(jnp.bfloat16)
    grad_out_proj = jnp.einsum(
        "ti,td->id", context, grad_attended, preferred_element_type=jnp.float32
    )
    context_gradient = jnp.einsum(
        "td,id->ti", grad_attended, back_set[4], preferred_element_type=jnp.float32
    ).astype(jnp.bfloat16)
    context_gradient_grid = context_gradient.reshape(
        microbatch_count, microbatch_rows, KEY_VALUE_HEADS, query_group_size, HEAD_SIZE
    )
    probs_again = jnp.exp(score_block() - top_score) / row_total
    probs_again_low = probs_again.astype(jnp.bfloat16)
    grad_probs = jnp.einsum(
        "mqgrd,mkgd->mgrqk", context_gradient_grid, value_tiles, preferred_element_type=jnp.float32
    )
    value_gradient = jnp.einsum(
        "mgrqk,mqgrd->mkgd",
        probs_again_low,
        context_gradient_grid,
        preferred_element_type=jnp.float32,
    )
    grad_scores = probs_again * (
        grad_probs - jnp.sum(probs_again * grad_probs, axis=-1, keepdims=True)
    )
    grad_scores = grad_scores.astype(jnp.bfloat16)
    grad_queries = (
        jnp.einsum("mgrqk,mkgd->mqgrd", grad_scores, key_tiles, preferred_element_type=jnp.float32)
        * 0.125
    )
    grad_queries = grad_queries.reshape(count_of_rows, QUERY_HEADS * HEAD_SIZE).astype(jnp.bfloat16)
    key_gradient = (
        jnp.einsum(
            "mgrqk,mqgrd->mkgd", grad_scores, query_tiles, preferred_element_type=jnp.float32
        )
        * 0.125
    )
    key_gradient = key_gradient.reshape(count_of_rows, KEY_VALUE_HEADS * HEAD_SIZE).astype(
        jnp.bfloat16
    )
    value_gradient_narrow = value_gradient.reshape(
        count_of_rows, KEY_VALUE_HEADS * HEAD_SIZE
    ).astype(jnp.bfloat16)
    grad_query_proj = jnp.einsum(
        "td,ti->di", normed, grad_queries, preferred_element_type=jnp.float32
    )
    grad_key_proj = jnp.einsum(
        "td,ti->di", normed, key_gradient, preferred_element_type=jnp.float32
    )
    grad_value_proj = jnp.einsum(
        "td,ti->di", normed, value_gradient_narrow, preferred_element_type=jnp.float32
    )
    grad_normed = jnp.einsum(
        "ti,di->td", grad_queries, back_set[1], preferred_element_type=jnp.float32
    )
    grad_normed = grad_normed + jnp.einsum(
        "ti,di->td", key_gradient, back_set[2], preferred_element_type=jnp.float32
    )
    grad_normed = grad_normed + jnp.einsum(
        "ti,di->td", value_gradient_narrow, back_set[3], preferred_element_type=jnp.float32
    )
    back_gain_one = back_set[0].astype(jnp.float32)
    grad_gain_one = jnp.sum(grad_normed * unit_one, axis=0)
    scaled_one = grad_normed * back_gain_one
    grad_hidden = grad_middle + scale_one * (
        scaled_one - unit_one * jnp.mean(scaled_one * unit_one, axis=-1, keepdims=True)
    )
    terms = (
        grad_gain_one,
        grad_query_proj,
        grad_key_proj,
        grad_value_proj,
        grad_out_proj,
        grad_gain_two,
        grad_router,
    )
    local_shapes = (
        gain_attn.shape,
        w_query.shape,
        key_weight.shape,
        value_weight.shape,
        w_attn_out.shape,
        gain_ffn.shape,
        w_router.shape,
    )
    flat_terms = tuple((term.reshape(device_count, -1) for term in terms))
    owned = (
        lax.psum_scatter(flat_terms[0], "fsdp", scatter_dimension=0, tiled=True),
        lax.psum_scatter(flat_terms[1], "fsdp", scatter_dimension=0, tiled=True),
        lax.psum_scatter(flat_terms[2], "fsdp", scatter_dimension=0, tiled=True),
        lax.psum_scatter(flat_terms[3], "fsdp", scatter_dimension=0, tiled=True),
        lax.psum_scatter(flat_terms[4], "fsdp", scatter_dimension=0, tiled=True),
        lax.psum_scatter(flat_terms[5], "fsdp", scatter_dimension=0, tiled=True),
        lax.psum_scatter(flat_terms[6], "fsdp", scatter_dimension=0, tiled=True),
    )
    owned = tuple((piece.reshape(shape) for piece, shape in zip(owned, local_shapes)))
    return (
        block_output,
        grad_hidden.astype(jnp.bfloat16),
        owned[0],
        owned[1],
        owned[2],
        owned[3],
        owned[4],
        owned[5],
        owned[6],
        grad_w_expert_in,
        grad_w_expert_out,
    )


def solution(mesh):
    placed = (
        P("fsdp", None),
        P("fsdp", None),
        P("fsdp", None),
        P("fsdp", None),
        P("fsdp"),
        P("fsdp", None),
        P("fsdp", None),
        P("fsdp", None),
        P("fsdp", None),
        P("fsdp"),
        P("fsdp", None),
        P("fsdp", None),
        P("fsdp", None),
    )
    devices = mesh.shape["fsdp"]
    planes = devices // PLANE
    whole = devices % PLANE == 0 and planes & (planes - 1) == 0 and FE % (16 * devices) == 0
    return jax.shard_map(
        exchanged if whole else shards,
        mesh=mesh,
        in_specs=placed,
        out_specs=(
            P("fsdp", None),
            P("fsdp", None),
            P("fsdp"),
            P("fsdp", None),
            P("fsdp", None),
            P("fsdp", None),
            P("fsdp", None),
            P("fsdp"),
            P("fsdp", None),
            P("fsdp", None),
            P("fsdp", None),
        ),
        check_vma=False,
    )
```

```python
import jax
import jax.numpy as jnp
from jax import lax
from jax.experimental import pallas as pl
from jax.experimental.pallas import tpu as pltpu
from jax.sharding import PartitionSpec as P

MODEL_WIDTH = 1024
QUERY_HEADS = 16
KEY_VALUE_HEADS = 8
HEAD_SIZE = 64
FE = 512
EXPERTS = 4
TOP = 2
CAP = 80

ROWS = 128
STRIDE = 96
SLOTS = EXPERTS * STRIDE
Q_END = QUERY_HEADS * HEAD_SIZE
K_END = Q_END + KEY_VALUE_HEADS * HEAD_SIZE
QKV = K_END + KEY_VALUE_HEADS * HEAD_SIZE
EXTRA = 128
X_FIRST, Y_FIRST = (0, 2, 1, 3), (0, 1, 2, 3)
PLANE = 8
f32 = jnp.float32
bf16 = jnp.bfloat16

eps = 1e-06
highest = lax.Precision.HIGHEST
VMEM_LIMIT = 44 * 1024 * 1024


def mm(left, right, left_dim=1, right_dim=0):
    return lax.dot_general(
        left, right, (((left_dim,), (right_dim,)), ((), ())), preferred_element_type=f32
    )


def two_parts(values):
    high = values.astype(bf16)
    return high, (values - high.astype(f32)).astype(bf16)


def iota(shape, dim):
    return lax.broadcasted_iota(jnp.int32, shape, dim)


def row_scale(values):
    return lax.rsqrt(jnp.mean(values * values, axis=-1, keepdims=True) + eps)


def section_of(lens, place):
    batch = place >> 6
    inner = place & 63
    first = jnp.where(batch == 0, lens[0, 0], lens[1, 0])
    total = first + jnp.where(batch == 0, lens[0, 1], lens[1, 1])
    part = jnp.where(inner < first, 0, jnp.where(inner < total, 1, 2))
    return batch, part


def live_of(lens):
    _, part = section_of(lens, iota((ROWS, 1), 0))
    return (part < 2).astype(f32)


def allowed_of(lens):
    row, column = iota((ROWS, 1), 0), iota((1, ROWS), 1)
    row_batch, row_part = section_of(lens, row)
    column_batch, column_part = section_of(lens, column)
    return (
        (row_batch * 4 + row_part) == (column_batch * 4 + column_part)
    ) & (column <= row)


def slots_of(choice, mine):
    lane = iota((ROWS, 128), 1)
    named = [choice[:, k : k + 1] ^ mine for k in range(TOP)]
    hits = jnp.zeros((ROWS, 128), f32)
    for one in named:
        hits = hits + (lane == one).astype(f32)
    earlier = (iota((ROWS, ROWS), 1) < iota((ROWS, ROWS), 0)).astype(bf16)
    before = mm(earlier, hits.astype(bf16))
    places = []
    for one in named:
        position = jnp.sum(jnp.where(lane == one, before, 0.0), axis=1, keepdims=True)
        slot = one * STRIDE + position.astype(jnp.int32)
        places.append((iota((ROWS, SLOTS), 1) == slot).astype(f32).astype(bf16))
    return named, places


def owner(pos, planes_off, chip_off, core_off):
    return ((pos[0] ^ planes_off) * 4 + (pos[1] ^ chip_off)) * 2 + (pos[2] ^ core_off)


def load_rows(pos, pieces, rows, planes, moves):
    for core in range(2):
        for chip in range(4):
            for k in range(planes):
                place = pl.multiple_of(owner(pos, k, chip, core) * rows, rows)
                for buffer, to, at, width in moves:
                    buffer[pl.ds(place, rows), to : to + width] = pieces[core * 4 + chip][
                        k, :, at : at + width
                    ]


def store_rows(pos, buffer, kept, sent, rows, planes, order, at, width):
    for core, target in ((0, kept), (1, sent)):
        for i, chip in enumerate(order):
            for k in range(planes):
                place = pl.multiple_of(owner(pos, k, chip, core) * rows, rows)
                target[i, k] = buffer[pl.ds(place, rows), at : at + width]


def cotangent_kernel(pos, lens, choice_ref, grad_ref, *outs):
    _, places = slots_of(choice_ref[...], pos[1])
    grad_mix = (live_of(lens) * grad_ref[...].astype(f32)).astype(bf16)
    slotted = mm(places[0] + places[1], grad_mix, 0, 0)
    for f in range(EXPERTS):
        outs[f][...] = slotted[f * STRIDE : f * STRIDE + CAP].astype(bf16)


def halves(block):
    low = iota(block.shape, 1) < HEAD_SIZE
    wide = block.astype(f32)
    return jnp.concatenate(
        [jnp.where(low, wide, 0.0), jnp.where(low, 0.0, wide)], axis=0
    ).astype(bf16)


def joined(both):
    upper, lower = both[:ROWS], both[ROWS:]
    return jnp.where(iota(upper.shape, 1) < HEAD_SIZE, upper, lower)


def doubled(pair, g):
    wide = pair.astype(f32)
    turned = pltpu.roll(wide, HEAD_SIZE, 1)
    low = iota(wide.shape, 1) < HEAD_SIZE
    first, second = (wide, turned) if g % 2 == 0 else (turned, wide)
    return jnp.where(low, first, second).astype(bf16)


def head_blocks(qkv_ref, g):
    pair = (g // 2) * 128
    queries = halves(qkv_ref[:, g * 128 : (g + 1) * 128])
    keys = doubled(qkv_ref[:, Q_END + pair : Q_END + pair + 128], g)
    values = doubled(qkv_ref[:, K_END + pair : K_END + pair + 128], g)
    return queries, keys, values


def attention_kernel(planes, rows, pos, lens, hidden_ref, *refs):
    first, second = refs[:8], refs[8:16]
    normed_ref, gains_ref, qkv_ref, context_ref, stats_ref, weights = refs[16:]
    load_rows(pos, first, rows, planes, [(weights, 0, 0, K_END), (weights, QKV, K_END, EXTRA)])
    load_rows(pos, second, rows, planes, [(weights, K_END, 0, QKV - K_END)])
    hidden = hidden_ref[...].astype(f32)
    unit = hidden * row_scale(hidden)
    pick = (iota((16, EXTRA), 0) == iota((16, EXTRA), 1)).astype(f32).astype(bf16)
    gains = mm(pick, weights[:, QKV:], 1, 1)
    gains_ref[...] = gains
    normed = (unit * gains[0:1]).astype(bf16)
    normed_ref[...] = normed
    for at in range(0, QKV, 512):
        qkv_ref[:, at : at + 512] = mm(normed, weights[:, at : at + 512]).astype(bf16)
    allowed = allowed_of(lens).astype(f32)
    twice = jnp.concatenate([allowed, allowed], axis=0)
    lane = iota((ROWS, 128), 1)
    stats = jnp.zeros((ROWS, 128), f32)
    for g in range(KEY_VALUE_HEADS):
        queries, keys, values = head_blocks(qkv_ref, g)
        scores = jnp.where(twice > 0, mm(queries, keys, 1, 1) * 0.125, -1e30)
        top = jnp.max(scores, axis=-1, keepdims=True)
        exps = jnp.exp(scores - top)
        total = jnp.sum(exps, axis=-1, keepdims=True)
        probs = (exps * (1.0 / total)).astype(bf16)
        context_ref[:, g * 128 : (g + 1) * 128] = joined(mm(probs, values)).astype(bf16)
        kept = top + jnp.log(total)
        stats = jnp.where(lane == 2 * g, kept[:ROWS], stats)
        stats = jnp.where(lane == 2 * g + 1, kept[ROWS:], stats)
    stats_ref[...] = stats


def router_gates(named, normed_ffn, gains):
    logits = mm(normed_ffn, gains.astype(bf16), 1, 1)
    chosen = []
    for one in named:
        value = jnp.zeros((ROWS, 1), f32)
        for k in range(EXPERTS):
            value = value + jnp.where(one == k, logits[:, 2 + k : 3 + k], 0.0)
        chosen.append(value)
    top = jnp.maximum(chosen[0], chosen[1])
    exps = [jnp.exp(value - top) for value in chosen]
    total = exps[0] + exps[1]
    return [value / total for value in exps]


def dispatch_kernel(planes, rows, pos, lens, choice_ref, hidden_ref, context_ref, gains_ref, *refs):
    pieces = refs[:8]
    middle_ref, gates_ref = refs[8:10]
    outs = refs[10:14]
    (weights,) = refs[14:]
    load_rows(pos, pieces, rows, planes, [(weights, 0, QKV - K_END, MODEL_WIDTH)])
    choice = choice_ref[...]
    _, places = slots_of(choice, pos[1])
    attended = mm(context_ref[...], weights[...])
    middle = hidden_ref[...].astype(f32) + live_of(lens) * attended
    middle_ref[...] = middle
    gains = gains_ref[...]
    normed_ffn = (middle * row_scale(middle) * gains[1:2]).astype(bf16)
    gates = router_gates([choice[:, k : k + 1] for k in range(TOP)], normed_ffn, gains)
    lane = iota((ROWS, 128), 1)
    gates_ref[...] = jnp.where(lane == 0, gates[0], jnp.where(lane == 1, gates[1], 0.0))
    slotted = mm(places[0] + places[1], normed_ffn, 0, 0)
    beside = jnp.zeros((SLOTS, EXTRA), f32)
    for place, gate in zip(places, gates):
        high, low = two_parts(gate)
        columns = jnp.where(
            lane == 0, high.astype(f32), jnp.where(lane == 1, low.astype(f32), 0.0)
        ).astype(bf16)
        beside = beside + mm(place, columns, 0, 0)
    for f in range(EXPERTS):
        part = slice(f * STRIDE, f * STRIDE + CAP)
        outs[f][:, :MODEL_WIDTH] = slotted[part].astype(bf16)
        outs[f][:, MODEL_WIDTH:] = beside[part].astype(bf16)


def expert_places(pos, planes, rows_in, rows_out):
    places = []
    for core in range(2):
        for k in range(planes):
            for chip in range(4):
                who = owner(pos, k, chip, core)
                in_rows = pl.ds(pl.multiple_of(who * rows_in, rows_in), rows_in)
                out_rows = pl.ds(pl.multiple_of(who * rows_out, rows_out), rows_out)
                places.append((core, k, chip, in_rows, out_rows))
    return places


def expert_kernel(planes, rows_in, rows_out, pos, *refs):
    tokens, grads, pieces = refs[:4], refs[4:8], refs[8:12]
    refs = refs[12:]
    backs = refs[:4]
    x_ref, activated_ref, d_expert_ref, d_up_ref = refs[4:8]
    w_in, w_out = refs[8:]
    for core, k, chip, in_rows, out_rows in expert_places(pos, planes, rows_in, rows_out):
        source = pieces[core * 2 + k % 2]
        w_in[in_rows] = source[k // 2, chip, :rows_in]
        w_out[out_rows] = source[k // 2, chip, rows_in:]
    for f in range(EXPERTS):
        part = slice(f * CAP, (f + 1) * CAP)
        x_ref[part] = tokens[f][:, :MODEL_WIDTH]
        gate_slots = tokens[f][:, MODEL_WIDTH : MODEL_WIDTH + 1].astype(f32) + tokens[f][
            :, MODEL_WIDTH + 1 : MODEL_WIDTH + 2
        ].astype(f32)
        d_expert_ref[part] = (gate_slots * grads[f][...].astype(f32)).astype(bf16)
    x = x_ref[...]
    gate = mm(x, w_in[:, :FE])
    up = mm(x, w_in[:, FE:])
    sig = 1.0 / (1.0 + jnp.exp(-gate))
    silu = gate * sig
    activated = (silu * up).astype(bf16)
    activated_ref[...] = activated
    expert_out = mm(activated, w_out[...]).astype(bf16)
    d_act = mm(d_expert_ref[...], w_out[...], 1, 1)
    d_up_ref[:, :FE] = (d_act * up * (sig * (1.0 + gate * (1.0 - sig)))).astype(bf16)
    d_up_ref[:, FE:] = (d_act * silu).astype(bf16)
    d_x = mm(d_up_ref[...], w_in[...], 1, 1).astype(bf16)
    for f in range(EXPERTS):
        part = slice(f * CAP, (f + 1) * CAP)
        backs[f][:CAP] = expert_out[part]
        backs[f][CAP:] = d_x[part]


def expert_weights_kernel(planes, rows_in, rows_out, pos, x_ref, activated_ref, d_expert_ref, d_up_ref, *refs):
    kept, sent, d_in, d_out = refs
    d_out[...] = mm(activated_ref[...], d_expert_ref[...], 0, 0).astype(bf16)
    d_in[...] = mm(x_ref[...], d_up_ref[...], 0, 0).astype(bf16)
    for core, k, chip, in_rows, out_rows in expert_places(pos, planes, rows_in, rows_out):
        target = kept if core == 0 else sent
        target[k, chip, :rows_in] = d_in[in_rows]
        target[k, chip, rows_in:] = d_out[out_rows]


def combine_kernel(
    planes, rows, pos, lens, choice_ref, middle_ref, gates_ref, grad_ref, gains_ref, context_ref, *refs
):
    backs = refs[:4]
    out_ref, grad_middle_ref, grad_attended_ref, kept, sent = refs[4:9]
    (d_weights,) = refs[9:]
    choice = choice_ref[...]
    _, places = slots_of(choice, pos[1])
    live = live_of(lens)
    empty = jnp.zeros((STRIDE - CAP, MODEL_WIDTH), bf16)
    outs, grads = [], []
    for back in backs:
        outs += [back[:CAP], empty]
        grads += [back[CAP:], empty]
    outs = jnp.concatenate(outs, axis=0)
    grads = jnp.concatenate(grads, axis=0)
    picked = [mm(place, outs) for place in places]
    gates = [gates_ref[:, k : k + 1] for k in range(TOP)]
    middle = middle_ref[...]
    mixture = gates[0] * picked[0] + gates[1] * picked[1]
    out_ref[...] = (middle + live * mixture).astype(bf16)
    cotangent = grad_ref[...].astype(f32)
    grad_mix = live * cotangent
    grad_gates = [jnp.sum(grad_mix * one, axis=1, keepdims=True) for one in picked]
    total = gates[0] * grad_gates[0] + gates[1] * grad_gates[1]
    grad_chosen = [gate * (grad - total) for gate, grad in zip(gates, grad_gates)]
    gains = gains_ref[...]
    grad_normed = mm(places[0] + places[1], grads)
    lane = iota((ROWS, EXTRA), 1)
    grad_logits = jnp.zeros((ROWS, EXTRA), f32)
    for k in range(EXPERTS):
        one = jnp.zeros((ROWS, 1), f32)
        for choice_at in range(TOP):
            one = one + jnp.where(choice[:, choice_at : choice_at + 1] == k, grad_chosen[choice_at], 0.0)
        grad_normed = grad_normed + one * gains[2 + k : 3 + k]
        grad_logits = jnp.where(lane == 2 + k, one, grad_logits)
    scale = row_scale(middle)
    unit = middle * scale
    normed_ffn = (unit * gains[1:2]).astype(bf16)
    logits_high, logits_low = two_parts(grad_logits)
    gain_high, gain_low = two_parts(grad_normed * unit)
    first = (lane == 1).astype(f32).astype(bf16)
    d_weights[:, MODEL_WIDTH:] = (
        mm(normed_ffn, logits_high, 0, 0)
        + mm(normed_ffn, logits_low, 0, 0)
        + mm(gain_high, first, 0, 0)
        + mm(gain_low, first, 0, 0)
    ).astype(bf16)
    scaled = grad_normed * gains[1:2]
    grad_middle = cotangent + scale * (
        scaled - unit * jnp.mean(scaled * unit, axis=-1, keepdims=True)
    )
    grad_middle_ref[...] = grad_middle
    grad_attended = (live * grad_middle).astype(bf16)
    grad_attended_ref[...] = grad_attended
    d_weights[:, :MODEL_WIDTH] = mm(context_ref[...], grad_attended, 0, 0).astype(bf16)
    width = MODEL_WIDTH + EXTRA
    store_rows(pos, d_weights, kept, sent, rows, planes, range(4), 0, width)


def attend_back(allowed, qkv_ref, stats_ref, grad_context_ref, grads):
    twice = jnp.concatenate([allowed, allowed], axis=0)
    low = iota((ROWS, 128), 1) < HEAD_SIZE
    pairs = []
    for g in range(KEY_VALUE_HEADS):
        queries, keys, values = head_blocks(qkv_ref, g)
        kept = jnp.concatenate(
            [stats_ref[:, 2 * g : 2 * g + 1], stats_ref[:, 2 * g + 1 : 2 * g + 2]], axis=0
        )
        scores = jnp.where(twice > 0, mm(queries, keys, 1, 1) * 0.125, -1e30)
        probs = jnp.exp(scores - kept)
        d_context = halves(grad_context_ref[:, g * 128 : (g + 1) * 128])
        d_probs = mm(d_context, values, 1, 1)
        d_scores = (
            probs * (d_probs - jnp.sum(probs * d_probs, axis=-1, keepdims=True))
        ).astype(bf16)
        grads[:, g * 128 : (g + 1) * 128] = (joined(mm(d_scores, keys)) * 0.125).astype(bf16)
        d_keys = mm(d_scores, queries, 0, 0)
        d_values = mm(probs.astype(bf16), d_context, 0, 0)
        pairs.append([both + pltpu.roll(both, HEAD_SIZE, 1) for both in (d_keys, d_values)])
        if g % 2 == 1:
            at = Q_END + (g // 2) * 128
            d_keys = jnp.where(low, pairs[g - 1][0], pairs[g][0]) * 0.125
            d_values = jnp.where(low, pairs[g - 1][1], pairs[g][1])
            grads[:, at : at + 128] = d_keys.astype(bf16)
            at = at + K_END - Q_END
            grads[:, at : at + 128] = d_values.astype(bf16)


def context_kernel(planes, rows, pos, grad_attended_ref, *refs):
    pieces, out_ref, weights = refs[:8], refs[8], refs[9]
    load_rows(pos, pieces, rows, planes, [(weights, 0, QKV - K_END, MODEL_WIDTH)])
    out_ref[...] = mm(grad_attended_ref[...], weights[...], 1, 1).astype(bf16)


def back_kernel(planes, rows, pos, lens, normed_ref, qkv_ref, stats_ref, grad_context_ref, *refs):
    grads, kept_q, sent_q, kept_kv, sent_kv, d_weights = refs
    attend_back(allowed_of(lens).astype(f32), qkv_ref, stats_ref, grad_context_ref, grads)
    d_weights[...] = mm(normed_ref[...], grads[...], 0, 0).astype(bf16)
    store_rows(pos, d_weights, kept_q, sent_q, rows, planes, X_FIRST, 0, Q_END)
    store_rows(pos, d_weights, kept_kv, sent_kv, rows, planes, Y_FIRST, Q_END, QKV - Q_END)


def input_kernel(planes, rows, pos, hidden_ref, grad_middle_ref, gains_ref, grads_ref, *refs):
    first, second, grad_in_ref, weights = refs[:8], refs[8:16], refs[16], refs[17]
    load_rows(pos, first, rows, planes, [(weights, 0, 0, K_END)])
    load_rows(pos, second, rows, planes, [(weights, K_END, 0, QKV - K_END)])
    hidden = hidden_ref[...].astype(f32)
    scale = row_scale(hidden)
    unit = hidden * scale
    grad_normed = mm(grads_ref[...], weights[...], 1, 1)
    scaled = grad_normed * gains_ref[0:1, :]
    grad_hidden = grad_middle_ref[...] + scale * (
        scaled - unit * jnp.mean(scaled * unit, axis=-1, keepdims=True)
    )
    grad_in_ref[...] = grad_hidden.astype(bf16)


def owned_kernel(rows_in, rows_out, pos, *refs):
    pieces, in_ref, out_ref = refs[:4], refs[4], refs[5]
    for f in range(4):
        place = pl.ds(pl.multiple_of((pos[1] ^ f) * MODEL_WIDTH, MODEL_WIDTH), MODEL_WIDTH)
        in_ref[:, place] = pieces[f][:rows_in].astype(f32)
        out_ref[:, place] = pieces[f][rows_in:].astype(f32)


def call(kernel, operands, n_scalars, outs, scratch, name):
    here = pl.BlockSpec(memory_space=pltpu.VMEM)
    scalar = pl.BlockSpec(memory_space=pltpu.SMEM)
    return pl.pallas_call(
        kernel,
        out_shape=tuple(outs),
        in_specs=[scalar] * n_scalars + [here] * (len(operands) - n_scalars),
        out_specs=(here,) * len(outs),
        scratch_shapes=scratch,
        compiler_params=pltpu.CompilerParams(vmem_limit_bytes=VMEM_LIMIT),
        cost_estimate=pl.CostEstimate(flops=1000, bytes_accessed=1000, transcendentals=0),
        name=name,
    )(*operands)


def exchanged(
    hidden_in,
    grad_out,
    seq_lens,
    expert_choice,
    gain_attn,
    w_query,
    key_weight,
    value_weight,
    w_attn_out,
    gain_ffn,
    w_router,
    w_expert_in,
    w_expert_out,
):
    n = lax.axis_size("fsdp")
    planes = n // PLANE
    me = lax.axis_index("fsdp")
    plane, chip, core = me // PLANE, (me // 2) % 4, me % 2
    pos = jnp.stack([plane, chip, core]).astype(jnp.int32)
    rows = w_query.shape[0]
    rows_out = w_expert_out.shape[0]
    both = rows + rows_out

    def swap(value, offset):
        return lax.ppermute(value, "fsdp", [(i, i ^ offset) for i in range(n)])

    def after(value, *earlier):
        return lax.optimization_barrier((value, *earlier))[0]

    def array(*shape, dtype=bf16):
        return jax.ShapeDtypeStruct(shape, dtype)

    def summed(*values):
        total = values[0].astype(f32)
        for one in values[1:]:
            total = total + one.astype(f32)
        return total

    def low_sum(*values):
        return summed(*values).astype(bf16)

    def widen(blocks, offset):
        other = swap(blocks, PLANE * offset)
        return jnp.stack([blocks, other], axis=1).reshape((-1,) + blocks.shape[1:])

    def fold(parts, offset):
        return low_sum(parts[0::2], swap(parts[1::2], PLANE * offset))

    def to_chips(parts):
        return [parts[0]] + [swap(parts[f], 2 * f) for f in range(1, 4)]

    def both_cores(pieces):
        return list(pieces) + [swap(one, 1) for one in pieces]

    grad_slots = to_chips(
        call(
            cotangent_kernel,
            (pos, seq_lens, expert_choice, grad_out),
            2,
            [array(CAP, MODEL_WIDTH)] * 4,
            [],
            "slot_cotangents",
        )
    )
    by_expert = jnp.concatenate(
        [
            w_expert_in.reshape(rows, EXPERTS, 2 * FE),
            w_expert_out.reshape(rows_out, EXPERTS, MODEL_WIDTH),
        ],
        axis=0,
    ).transpose(1, 0, 2)
    expert_blocks = jnp.stack(
        to_chips([lax.dynamic_index_in_dim(by_expert, chip ^ f, 0, False) for f in range(4)])
    )[None]

    beside = jnp.concatenate(
        [gain_attn[:, None], gain_ffn[:, None], w_router, jnp.zeros((rows, EXTRA - 6), bf16)], axis=1
    )
    weights = jnp.concatenate([w_query, key_weight, beside, value_weight, w_attn_out], axis=1)[None]
    offset = planes // 2
    while offset:
        weights = widen(weights, offset)
        offset = offset // 2
    weights = after(weights, expert_blocks, *grad_slots)
    first, second = weights[:, :, : K_END + EXTRA], weights[:, :, K_END + EXTRA :]
    first_x, second_y = swap(first, 2), swap(second, 4)
    first_y, second_x = swap(first, 4), swap(second, 2)
    offset = planes // 2
    expert_blocks = after(expert_blocks, weights)
    while offset > 1:
        expert_blocks = widen(expert_blocks, offset)
        offset = offset // 2
    first_xy = swap(after(first_x, expert_blocks), 4)
    second_xy = swap(after(second_y, expert_blocks), 2)
    first_pieces = both_cores([first, first_x, first_y, first_xy])
    second_pieces = both_cores([second, second_x, second_y, second_xy])
    odd_blocks = swap(expert_blocks, PLANE)

    normed, gains, qkv, context, stats = call(
        lambda *refs: attention_kernel(planes, rows, *refs),
        (pos, seq_lens, hidden_in, *first_pieces, *second_pieces),
        2,
        [
            array(ROWS, MODEL_WIDTH),
            array(16, MODEL_WIDTH, dtype=f32),
            array(ROWS, QKV),
            array(ROWS, Q_END),
            array(ROWS, 128, dtype=f32),
        ],
        [pltpu.VMEM((MODEL_WIDTH, QKV + EXTRA), bf16)],
        "attention",
    )
    middle, gates, *dispatched = call(
        lambda *refs: dispatch_kernel(planes, rows, *refs),
        (pos, seq_lens, expert_choice, hidden_in, after(context, odd_blocks), gains, *second_pieces),
        2,
        [array(ROWS, MODEL_WIDTH, dtype=f32), array(ROWS, 128, dtype=f32)]
        + [array(CAP, MODEL_WIDTH + EXTRA)] * 4,
        [pltpu.VMEM((MODEL_WIDTH, MODEL_WIDTH), bf16)],
        "dispatch",
    )
    dispatched = to_chips(dispatched)

    expert_pieces = both_cores([after(expert_blocks, context), after(odd_blocks, middle)])
    slots = EXPERTS * CAP
    *backs, x, activated, d_expert, d_up = call(
        lambda *refs: expert_kernel(planes, rows, rows_out, *refs),
        (pos, *dispatched, *grad_slots, *expert_pieces),
        1,
        [array(2 * CAP, MODEL_WIDTH)] * 4
        + [array(slots, MODEL_WIDTH), array(slots, FE), array(slots, MODEL_WIDTH), array(slots, 2 * FE)],
        [pltpu.VMEM((MODEL_WIDTH, 2 * FE), bf16), pltpu.VMEM((FE, MODEL_WIDTH), bf16)],
        "experts",
    )
    backs = to_chips(backs)
    kept, sent = call(
        lambda *refs: expert_weights_kernel(planes, rows, rows_out, *refs),
        (pos, x, activated, d_expert, d_up),
        1,
        [array(planes, 4, both, MODEL_WIDTH)] * 2,
        [pltpu.VMEM((MODEL_WIDTH, 2 * FE), bf16), pltpu.VMEM((FE, MODEL_WIDTH), bf16)],
        "expert_weights",
    )
    expert_parts = low_sum(kept, swap(sent, 1))

    block_output, grad_middle, grad_attended, kept, sent = call(
        lambda *refs: combine_kernel(planes, rows, *refs),
        (
            pos,
            seq_lens,
            expert_choice,
            after(middle, expert_parts),
            gates,
            grad_out,
            gains,
            context,
            *backs,
        ),
        2,
        [
            array(ROWS, MODEL_WIDTH),
            array(ROWS, MODEL_WIDTH, dtype=f32),
            array(ROWS, MODEL_WIDTH),
        ]
        + [array(4, planes, rows, MODEL_WIDTH + EXTRA)] * 2,
        [pltpu.VMEM((MODEL_WIDTH, MODEL_WIDTH + EXTRA), bf16)],
        "combine",
    )
    expert_parts = fold(expert_parts, 1)
    (grad_context,) = call(
        lambda *refs: context_kernel(planes, rows, *refs),
        (pos, grad_attended, *second_pieces),
        1,
        [array(ROWS, Q_END)],
        [pltpu.VMEM((MODEL_WIDTH, MODEL_WIDTH), bf16)],
        "context_gradients",
    )
    other = swap(sent, 1)
    out_parts = [low_sum(kept[f], other[f]) for f in range(4)]
    out_sums = to_chips(out_parts)
    grads, kept_q, sent_q, kept_kv, sent_kv = call(
        lambda *refs: back_kernel(planes, rows, *refs),
        (pos, seq_lens, after(normed, expert_parts, *out_parts), qkv, stats, grad_context),
        2,
        [array(ROWS, QKV)] + [array(4, planes, rows, QKV // 2)] * 4,
        [pltpu.VMEM((MODEL_WIDTH, QKV), bf16)],
        "attention_back",
    )
    offset = 2
    while expert_parts.shape[0] > 1:
        expert_parts = fold(expert_parts, offset)
        offset = 2 * offset
    other_q, other_kv = swap(sent_q, 1), swap(sent_kv, 1)
    keep_q, send_q = low_sum(kept_q[:2], other_q[:2]), low_sum(kept_q[2:], other_q[2:])
    keep_kv, send_kv = low_sum(kept_kv[:2], other_kv[:2]), low_sum(kept_kv[2:], other_kv[2:])
    from_x = swap(after(send_q, expert_parts, *out_sums), 2)
    from_y = swap(after(send_kv, expert_parts, *out_sums), 4)
    (grad_in,) = call(
        lambda *refs: input_kernel(planes, rows, *refs),
        (
            pos,
            hidden_in,
            grad_middle,
            gains,
            after(grads, send_q, send_kv),
            *first_pieces,
            *second_pieces,
        ),
        1,
        [array(ROWS, MODEL_WIDTH)],
        [pltpu.VMEM((MODEL_WIDTH, QKV), bf16)],
        "input_gradient",
    )
    owned_out = low_sum(*out_sums)
    offset = 1
    while owned_out.shape[0] > 1:
        owned_out = fold(owned_out, offset)
        offset = 2 * offset
    half_q, half_kv = low_sum(keep_q, from_x), low_sum(keep_kv, from_y)
    rest_q, rest_kv = swap(after(half_q[1], grad_in), 4), swap(after(half_kv[1], grad_in), 2)
    owned_qkv = jnp.concatenate([low_sum(half_q[0], rest_q), low_sum(half_kv[0], rest_kv)], axis=-1)
    expert_mine = to_chips(after(expert_parts, owned_qkv)[0])
    owned_qkv = after(owned_qkv, owned_out)
    owned_qkv = summed(
        owned_qkv[0], *[swap(owned_qkv[k], PLANE * k) for k in range(1, planes)]
    )
    grad_w_expert_in, grad_w_expert_out = call(
        lambda *refs: owned_kernel(rows, rows_out, *refs),
        (pos, *expert_mine),
        1,
        [
            array(rows, EXPERTS * 2 * FE, dtype=f32),
            array(rows_out, EXPERTS * MODEL_WIDTH, dtype=f32),
        ],
        [],
        "expert_rows",
    )
    owned_out = owned_out[0].astype(f32)
    d_query, d_key, d_value = owned_qkv[:, :Q_END], owned_qkv[:, Q_END:K_END], owned_qkv[:, K_END:]
    d_gain_attn = sum(
        jnp.sum(d * w.astype(f32), axis=1)
        for d, w in ((d_query, w_query), (d_key, key_weight), (d_value, value_weight))
    ) / gain_attn.astype(f32)
    return (
        block_output,
        grad_in,
        d_gain_attn,
        d_query,
        d_key,
        d_value,
        owned_out[:, :MODEL_WIDTH],
        owned_out[:, MODEL_WIDTH + 1],
        owned_out[:, MODEL_WIDTH + 2 : MODEL_WIDTH + 2 + EXPERTS],
        grad_w_expert_in,
        grad_w_expert_out,
    )


def rms_scale(values):
    return lax.rsqrt(jnp.mean(values * values, axis=-1, keepdims=True) + eps)


def layout(lengths, count_of_rows):
    microbatch_count = lengths.shape[0]
    microbatch_rows = count_of_rows // microbatch_count
    first_len = jnp.broadcast_to(lengths[:, 0:1], (microbatch_count, microbatch_rows))
    second_len = jnp.broadcast_to(lengths[:, 1:2], (microbatch_count, microbatch_rows))
    inner_grid = jnp.broadcast_to(
        jnp.arange(microbatch_rows, dtype=jnp.int32)[None, :], (microbatch_count, microbatch_rows)
    )
    section = jnp.where(
        inner_grid < first_len, 0, jnp.where(inner_grid < first_len + second_len, 1, 2)
    )
    allowed = (section[:, :, None] == section[:, None, :]) & (
        inner_grid[:, None, :] <= inner_grid[:, :, None]
    )
    live_rows = (section < 2).astype(jnp.float32).reshape(count_of_rows, 1)
    return (live_rows, allowed)


def routing(choice_ids, capacity):
    count_of_rows, top_count = choice_ids.shape
    expert_ids = jnp.arange(EXPERTS, dtype=jnp.int32)
    expert_hits = (choice_ids[:, :, None] == expert_ids[None, None, :]).astype(jnp.int32)
    per_row = jnp.sum(expert_hits, axis=1)
    before = jnp.cumsum(per_row, axis=0) - per_row
    position = jnp.sum(expert_hits * before[:, None, :], axis=2)
    slot_index = choice_ids * capacity + position
    pair_index = jnp.arange(count_of_rows * top_count, dtype=jnp.int32)
    source = (
        jnp.full((EXPERTS * capacity,), count_of_rows * top_count, jnp.int32)
        .at[slot_index.reshape(-1)]
        .set(pair_index)
    )
    return (expert_hits, slot_index, source)


def shards(
    hidden_in,
    grad_out,
    seq_lens,
    expert_choice,
    gain_attn,
    w_query,
    key_weight,
    value_weight,
    w_attn_out,
    gain_ffn,
    w_router,
    w_expert_in,
    w_expert_out,
):
    count_of_rows = hidden_in.shape[0]
    microbatch_count = seq_lens.shape[0]
    microbatch_rows = count_of_rows // microbatch_count
    query_group_size = QUERY_HEADS // KEY_VALUE_HEADS
    device_count = lax.axis_size("fsdp")
    live_rows, allowed = layout(seq_lens, count_of_rows)
    mask_grid = allowed[:, None, None]
    hidden = hidden_in.astype(jnp.float32)
    cotangent = grad_out.astype(jnp.float32)
    attention_set = (
        lax.all_gather(gain_attn, "fsdp", axis=0, tiled=True),
        lax.all_gather(w_query, "fsdp", axis=0, tiled=True),
        lax.all_gather(key_weight, "fsdp", axis=0, tiled=True),
        lax.all_gather(value_weight, "fsdp", axis=0, tiled=True),
        lax.all_gather(w_attn_out, "fsdp", axis=0, tiled=True),
        lax.all_gather(gain_ffn, "fsdp", axis=0, tiled=True),
        lax.all_gather(w_router, "fsdp", axis=0, tiled=True),
    )
    gain_one = attention_set[0].astype(jnp.float32)
    gain_two = attention_set[5].astype(jnp.float32)
    scale_one = rms_scale(hidden)
    unit_one = hidden * scale_one
    normed = (unit_one * gain_one).astype(jnp.bfloat16)
    query_rows = jnp.dot(normed, attention_set[1], preferred_element_type=jnp.float32).astype(
        jnp.bfloat16
    )
    every_key = jnp.dot(normed, attention_set[2], preferred_element_type=jnp.float32).astype(
        jnp.bfloat16
    )
    every_value = jnp.dot(normed, attention_set[3], preferred_element_type=jnp.float32).astype(
        jnp.bfloat16
    )
    query_tiles = query_rows.reshape(
        microbatch_count, microbatch_rows, KEY_VALUE_HEADS, query_group_size, HEAD_SIZE
    )
    key_tiles = every_key.reshape(microbatch_count, microbatch_rows, KEY_VALUE_HEADS, HEAD_SIZE)
    value_tiles = every_value.reshape(microbatch_count, microbatch_rows, KEY_VALUE_HEADS, HEAD_SIZE)

    def score_block():
        raw_scores = (
            jnp.einsum(
                "mqgrd,mkgd->mgrqk", query_tiles, key_tiles, preferred_element_type=jnp.float32
            )
            * 0.125
        )
        return jnp.where(mask_grid, raw_scores, -1e30)

    scores = score_block()
    top_score = jnp.max(scores, axis=-1, keepdims=True)
    weights = jnp.exp(scores - top_score)
    row_total = jnp.sum(weights, axis=-1, keepdims=True)
    probs_low = (weights / row_total).astype(jnp.bfloat16)
    context = jnp.einsum(
        "mgrqk,mkgd->mqgrd", probs_low, value_tiles, preferred_element_type=jnp.float32
    )
    context = context.reshape(count_of_rows, QUERY_HEADS * HEAD_SIZE).astype(jnp.bfloat16)
    attended = jnp.dot(context, attention_set[4], preferred_element_type=jnp.float32)
    middle = hidden + live_rows * attended
    scale_two = rms_scale(middle)
    unit_two = middle * scale_two
    normed_ffn = (unit_two * gain_two).astype(jnp.bfloat16)
    logits = jnp.dot(normed_ffn, attention_set[6], preferred_element_type=jnp.float32)
    expert_hits, slot_index, source = routing(expert_choice, CAP)
    hits_float = expert_hits.astype(jnp.float32)
    chosen = jnp.sum(hits_float * logits[:, None, :], axis=2)
    chosen_top = jnp.max(chosen, axis=1, keepdims=True)
    gate_exp = jnp.exp(chosen - chosen_top)
    gate_weights = gate_exp / jnp.sum(gate_exp, axis=1, keepdims=True)
    padded = jnp.concatenate([normed_ffn, jnp.zeros((1, MODEL_WIDTH), jnp.bfloat16)], axis=0)
    dispatched = padded[source // TOP].reshape(EXPERTS, CAP, MODEL_WIDTH)
    expert_in_full = lax.all_gather(w_expert_in, "fsdp", axis=0, tiled=True)
    expert_out_full = lax.all_gather(w_expert_out, "fsdp", axis=0, tiled=True)
    in_grid = expert_in_full.reshape(MODEL_WIDTH, EXPERTS, 2 * FE)
    out_grid = expert_out_full.reshape(FE, EXPERTS, MODEL_WIDTH)
    gate_up = jnp.einsum("ecd,def->ecf", dispatched, in_grid, preferred_element_type=jnp.float32)
    gate_part = gate_up[:, :, :FE]
    up_part = gate_up[:, :, FE:]
    sigmoid_gate = lax.logistic(gate_part)
    silu_gate = gate_part * sigmoid_gate
    activated = (silu_gate * up_part).astype(jnp.bfloat16)
    expert_out = jnp.einsum("ecf,fed->ecd", activated, out_grid, preferred_element_type=jnp.float32)
    picked = expert_out.reshape(EXPERTS * CAP, MODEL_WIDTH)[slot_index]
    mixture = jnp.sum(gate_weights[:, :, None] * picked, axis=1)
    block_output = (middle + live_rows * mixture).astype(jnp.bfloat16)
    back_set = (
        lax.all_gather(gain_attn, "fsdp", axis=0, tiled=True),
        lax.all_gather(w_query, "fsdp", axis=0, tiled=True),
        lax.all_gather(key_weight, "fsdp", axis=0, tiled=True),
        lax.all_gather(value_weight, "fsdp", axis=0, tiled=True),
        lax.all_gather(w_attn_out, "fsdp", axis=0, tiled=True),
        lax.all_gather(gain_ffn, "fsdp", axis=0, tiled=True),
        lax.all_gather(w_router, "fsdp", axis=0, tiled=True),
    )
    out_back = lax.all_gather(w_expert_out, "fsdp", axis=0, tiled=True).reshape(
        FE, EXPERTS, MODEL_WIDTH
    )
    in_back = lax.all_gather(w_expert_in, "fsdp", axis=0, tiled=True).reshape(
        MODEL_WIDTH, EXPERTS, 2 * FE
    )
    grad_mix = live_rows * cotangent
    grad_gates = jnp.sum(grad_mix[:, None, :] * picked, axis=2)
    grad_chosen = gate_weights * (
        grad_gates - jnp.sum(gate_weights * grad_gates, axis=1, keepdims=True)
    )
    grad_logits = jnp.sum(grad_chosen[:, :, None] * hits_float, axis=1)
    pair_grads = (gate_weights[:, :, None] * grad_mix[:, None, :]).reshape(
        count_of_rows * TOP, MODEL_WIDTH
    )
    pair_padded = jnp.concatenate([pair_grads, jnp.zeros((1, MODEL_WIDTH), jnp.float32)], axis=0)
    grad_expert_out = pair_padded[source].astype(jnp.bfloat16).reshape(EXPERTS, CAP, MODEL_WIDTH)
    grad_activated = jnp.einsum(
        "ecd,fed->ecf", grad_expert_out, out_back, preferred_element_type=jnp.float32
    )
    out_rows = w_expert_out.shape[0]
    columns = activated
    grad_w_expert_out = lax.psum_scatter(
        jnp.einsum(
            "ecn,ecd->ned", columns, grad_expert_out, preferred_element_type=jnp.float32
        ).reshape(1 * lax.axis_size("fsdp"), out_rows * EXPERTS * MODEL_WIDTH),
        "fsdp",
        scatter_dimension=0,
        tiled=True,
    ).reshape(out_rows, EXPERTS * MODEL_WIDTH)
    grad_gate = grad_activated * up_part * (sigmoid_gate * (1.0 + gate_part * (1.0 - sigmoid_gate)))
    grad_up = grad_activated * silu_gate
    grad_gate_up = jnp.concatenate([grad_gate, grad_up], axis=-1).astype(jnp.bfloat16)
    grad_dispatched = jnp.einsum(
        "ecf,def->ecd", grad_gate_up, in_back, preferred_element_type=jnp.float32
    )
    in_rows = w_expert_in.shape[0]
    columns = dispatched
    grad_w_expert_in = lax.psum_scatter(
        jnp.einsum(
            "ecn,ecf->nef", columns, grad_gate_up, preferred_element_type=jnp.float32
        ).reshape(1 * lax.axis_size("fsdp"), in_rows * EXPERTS * 2 * FE),
        "fsdp",
        scatter_dimension=0,
        tiled=True,
    ).reshape(in_rows, EXPERTS * 2 * FE)
    router_full = back_set[6].astype(jnp.float32)
    grad_normed_ffn = jnp.sum(
        grad_dispatched.reshape(EXPERTS * CAP, MODEL_WIDTH)[slot_index], axis=1
    )
    grad_normed_ffn = grad_normed_ffn + jnp.dot(grad_logits, router_full.T, precision=highest)
    grad_router = jnp.dot(normed_ffn.astype(jnp.float32).T, grad_logits, precision=highest)
    back_gain_two = back_set[5].astype(jnp.float32)
    grad_gain_two = jnp.sum(grad_normed_ffn * unit_two, axis=0)
    scaled_two = grad_normed_ffn * back_gain_two
    grad_middle = cotangent + scale_two * (
        scaled_two - unit_two * jnp.mean(scaled_two * unit_two, axis=-1, keepdims=True)
    )
    grad_attended = (live_rows * grad_middle).astype(jnp.bfloat16)
    grad_out_proj = jnp.einsum(
        "ti,td->id", context, grad_attended, preferred_element_type=jnp.float32
    )
    context_gradient = jnp.einsum(
        "td,id->ti", grad_attended, back_set[4], preferred_element_type=jnp.float32
    ).astype(jnp.bfloat16)
    context_gradient_grid = context_gradient.reshape(
        microbatch_count, microbatch_rows, KEY_VALUE_HEADS, query_group_size, HEAD_SIZE
    )
    probs_again = jnp.exp(score_block() - top_score) / row_total
    probs_again_low = probs_again.astype(jnp.bfloat16)
    grad_probs = jnp.einsum(
        "mqgrd,mkgd->mgrqk", context_gradient_grid, value_tiles, preferred_element_type=jnp.float32
    )
    value_gradient = jnp.einsum(
        "mgrqk,mqgrd->mkgd",
        probs_again_low,
        context_gradient_grid,
        preferred_element_type=jnp.float32,
    )
    grad_scores = probs_again * (
        grad_probs - jnp.sum(probs_again * grad_probs, axis=-1, keepdims=True)
    )
    grad_scores = grad_scores.astype(jnp.bfloat16)
    grad_queries = (
        jnp.einsum("mgrqk,mkgd->mqgrd", grad_scores, key_tiles, preferred_element_type=jnp.float32)
        * 0.125
    )
    grad_queries = grad_queries.reshape(count_of_rows, QUERY_HEADS * HEAD_SIZE).astype(jnp.bfloat16)
    key_gradient = (
        jnp.einsum(
            "mgrqk,mqgrd->mkgd", grad_scores, query_tiles, preferred_element_type=jnp.float32
        )
        * 0.125
    )
    key_gradient = key_gradient.reshape(count_of_rows, KEY_VALUE_HEADS * HEAD_SIZE).astype(
        jnp.bfloat16
    )
    value_gradient_narrow = value_gradient.reshape(
        count_of_rows, KEY_VALUE_HEADS * HEAD_SIZE
    ).astype(jnp.bfloat16)
    grad_query_proj = jnp.einsum(
        "td,ti->di", normed, grad_queries, preferred_element_type=jnp.float32
    )
    grad_key_proj = jnp.einsum(
        "td,ti->di", normed, key_gradient, preferred_element_type=jnp.float32
    )
    grad_value_proj = jnp.einsum(
        "td,ti->di", normed, value_gradient_narrow, preferred_element_type=jnp.float32
    )
    grad_normed = jnp.einsum(
        "ti,di->td", grad_queries, back_set[1], preferred_element_type=jnp.float32
    )
    grad_normed = grad_normed + jnp.einsum(
        "ti,di->td", key_gradient, back_set[2], preferred_element_type=jnp.float32
    )
    grad_normed = grad_normed + jnp.einsum(
        "ti,di->td", value_gradient_narrow, back_set[3], preferred_element_type=jnp.float32
    )
    back_gain_one = back_set[0].astype(jnp.float32)
    grad_gain_one = jnp.sum(grad_normed * unit_one, axis=0)
    scaled_one = grad_normed * back_gain_one
    grad_hidden = grad_middle + scale_one * (
        scaled_one - unit_one * jnp.mean(scaled_one * unit_one, axis=-1, keepdims=True)
    )
    terms = (
        grad_gain_one,
        grad_query_proj,
        grad_key_proj,
        grad_value_proj,
        grad_out_proj,
        grad_gain_two,
        grad_router,
    )
    local_shapes = (
        gain_attn.shape,
        w_query.shape,
        key_weight.shape,
        value_weight.shape,
        w_attn_out.shape,
        gain_ffn.shape,
        w_router.shape,
    )
    flat_terms = tuple((term.reshape(device_count, -1) for term in terms))
    owned = (
        lax.psum_scatter(flat_terms[0], "fsdp", scatter_dimension=0, tiled=True),
        lax.psum_scatter(flat_terms[1], "fsdp", scatter_dimension=0, tiled=True),
        lax.psum_scatter(flat_terms[2], "fsdp", scatter_dimension=0, tiled=True),
        lax.psum_scatter(flat_terms[3], "fsdp", scatter_dimension=0, tiled=True),
        lax.psum_scatter(flat_terms[4], "fsdp", scatter_dimension=0, tiled=True),
        lax.psum_scatter(flat_terms[5], "fsdp", scatter_dimension=0, tiled=True),
        lax.psum_scatter(flat_terms[6], "fsdp", scatter_dimension=0, tiled=True),
    )
    owned = tuple((piece.reshape(shape) for piece, shape in zip(owned, local_shapes)))
    return (
        block_output,
        grad_hidden.astype(jnp.bfloat16),
        owned[0],
        owned[1],
        owned[2],
        owned[3],
        owned[4],
        owned[5],
        owned[6],
        grad_w_expert_in,
        grad_w_expert_out,
    )


def solution(mesh):
    placed = (
        P("fsdp", None),
        P("fsdp", None),
        P("fsdp", None),
        P("fsdp", None),
        P("fsdp"),
        P("fsdp", None),
        P("fsdp", None),
        P("fsdp", None),
        P("fsdp", None),
        P("fsdp"),
        P("fsdp", None),
        P("fsdp", None),
        P("fsdp", None),
    )
    devices = mesh.shape["fsdp"]
    planes = devices // PLANE
    whole = devices % PLANE == 0 and planes > 1 and planes & (planes - 1) == 0 and FE % (16 * devices) == 0
    return jax.shard_map(
        exchanged if whole else shards,
        mesh=mesh,
        in_specs=placed,
        out_specs=(
            P("fsdp", None),
            P("fsdp", None),
            P("fsdp"),
            P("fsdp", None),
            P("fsdp", None),
            P("fsdp", None),
            P("fsdp", None),
            P("fsdp"),
            P("fsdp", None),
            P("fsdp", None),
            P("fsdp", None),
        ),
        check_vma=False,
    )
```

```python
import jax
import jax.numpy as jnp
from jax import lax
from jax.experimental import pallas as pl
from jax.experimental.pallas import tpu as pltpu
from jax.sharding import PartitionSpec as P

MODEL_WIDTH = 1024
QUERY_HEADS = 16
KEY_VALUE_HEADS = 8
HEAD_SIZE = 64
FE = 512
EXPERTS = 4
TOP = 2
CAP = 80

ROWS = 128
STRIDE = 96
SLOTS = EXPERTS * STRIDE
Q_END = QUERY_HEADS * HEAD_SIZE
K_END = Q_END + KEY_VALUE_HEADS * HEAD_SIZE
QKV = K_END + KEY_VALUE_HEADS * HEAD_SIZE
EXTRA = 128
X_FIRST, Y_FIRST = (0, 2, 1, 3), (0, 1, 2, 3)
PLANE = 8
f32 = jnp.float32
bf16 = jnp.bfloat16

eps = 1e-06
highest = lax.Precision.HIGHEST
VMEM_LIMIT = 44 * 1024 * 1024


def mm(left, right, left_dim=1, right_dim=0):
    return lax.dot_general(
        left, right, (((left_dim,), (right_dim,)), ((), ())), preferred_element_type=f32
    )


def two_parts(values):
    high = values.astype(bf16)
    return high, (values - high.astype(f32)).astype(bf16)


def iota(shape, dim):
    return lax.broadcasted_iota(jnp.int32, shape, dim)


def row_scale(values):
    return lax.rsqrt(jnp.mean(values * values, axis=-1, keepdims=True) + eps)


def section_of(lens, place):
    batch = place >> 6
    inner = place & 63
    first = jnp.where(batch == 0, lens[0, 0], lens[1, 0])
    total = first + jnp.where(batch == 0, lens[0, 1], lens[1, 1])
    part = jnp.where(inner < first, 0, jnp.where(inner < total, 1, 2))
    return batch, part


def live_of(lens):
    _, part = section_of(lens, iota((ROWS, 1), 0))
    return (part < 2).astype(f32)


def allowed_of(lens):
    row, column = iota((ROWS, 1), 0), iota((1, ROWS), 1)
    row_batch, row_part = section_of(lens, row)
    column_batch, column_part = section_of(lens, column)
    return (
        (row_batch * 4 + row_part) == (column_batch * 4 + column_part)
    ) & (column <= row)


def slots_of(choice, mine):
    lane = iota((ROWS, 128), 1)
    named = [choice[:, k : k + 1] ^ mine for k in range(TOP)]
    hits = jnp.zeros((ROWS, 128), f32)
    for one in named:
        hits = hits + (lane == one).astype(f32)
    earlier = (iota((ROWS, ROWS), 1) < iota((ROWS, ROWS), 0)).astype(bf16)
    before = mm(earlier, hits.astype(bf16))
    places = []
    for one in named:
        position = jnp.sum(jnp.where(lane == one, before, 0.0), axis=1, keepdims=True)
        slot = one * STRIDE + position.astype(jnp.int32)
        places.append((iota((ROWS, SLOTS), 1) == slot).astype(f32).astype(bf16))
    return named, places


def owner(pos, planes_off, chip_off, core_off):
    return ((pos[0] ^ planes_off) * 4 + (pos[1] ^ chip_off)) * 2 + (pos[2] ^ core_off)


def load_rows(pos, pieces, rows, planes, moves):
    for core in range(2):
        for chip in range(4):
            for k in range(planes):
                place = pl.multiple_of(owner(pos, k, chip, core) * rows, rows)
                for buffer, to, at, width in moves:
                    buffer[pl.ds(place, rows), to : to + width] = pieces[core * 4 + chip][
                        k, :, at : at + width
                    ]


def store_rows(pos, buffer, kept, sent, rows, planes, order, at, width):
    for core, target in ((0, kept), (1, sent)):
        for i, chip in enumerate(order):
            for k in range(planes):
                place = pl.multiple_of(owner(pos, k, chip, core) * rows, rows)
                target[i, k] = buffer[pl.ds(place, rows), at : at + width]


def cotangent_kernel(pos, lens, choice_ref, grad_ref, *outs):
    _, places = slots_of(choice_ref[...], pos[1])
    grad_mix = (live_of(lens) * grad_ref[...].astype(f32)).astype(bf16)
    slotted = mm(places[0] + places[1], grad_mix, 0, 0)
    for f in range(EXPERTS):
        outs[f][...] = slotted[f * STRIDE : f * STRIDE + CAP].astype(bf16)


def halves(block):
    low = iota(block.shape, 1) < HEAD_SIZE
    wide = block.astype(f32)
    return jnp.concatenate(
        [jnp.where(low, wide, 0.0), jnp.where(low, 0.0, wide)], axis=0
    ).astype(bf16)


def joined(both):
    upper, lower = both[:ROWS], both[ROWS:]
    return jnp.where(iota(upper.shape, 1) < HEAD_SIZE, upper, lower)


def doubled(pair, g):
    wide = pair.astype(f32)
    turned = pltpu.roll(wide, HEAD_SIZE, 1)
    low = iota(wide.shape, 1) < HEAD_SIZE
    first, second = (wide, turned) if g % 2 == 0 else (turned, wide)
    return jnp.where(low, first, second).astype(bf16)


def head_blocks(qkv_ref, g):
    pair = (g // 2) * 128
    queries = halves(qkv_ref[:, g * 128 : (g + 1) * 128])
    keys = doubled(qkv_ref[:, Q_END + pair : Q_END + pair + 128], g)
    values = doubled(qkv_ref[:, K_END + pair : K_END + pair + 128], g)
    return queries, keys, values


def attention_kernel(planes, rows, pos, lens, hidden_ref, *refs):
    first, second = refs[:8], refs[8:16]
    normed_ref, gains_ref, qkv_ref, context_ref, stats_ref, weights = refs[16:]
    load_rows(pos, first, rows, planes, [(weights, 0, 0, K_END), (weights, QKV, K_END, EXTRA)])
    load_rows(pos, second, rows, planes, [(weights, K_END, 0, QKV - K_END)])
    hidden = hidden_ref[...].astype(f32)
    unit = hidden * row_scale(hidden)
    pick = (iota((16, EXTRA), 0) == iota((16, EXTRA), 1)).astype(f32).astype(bf16)
    gains = mm(pick, weights[:, QKV:], 1, 1)
    gains_ref[...] = gains
    normed = (unit * gains[0:1]).astype(bf16)
    normed_ref[...] = normed
    for at in range(0, QKV, 512):
        qkv_ref[:, at : at + 512] = mm(normed, weights[:, at : at + 512]).astype(bf16)
    allowed = allowed_of(lens).astype(f32)
    twice = jnp.concatenate([allowed, allowed], axis=0)
    lane = iota((ROWS, 128), 1)
    stats = jnp.zeros((ROWS, 128), f32)
    for g in range(KEY_VALUE_HEADS):
        queries, keys, values = head_blocks(qkv_ref, g)
        scores = jnp.where(twice > 0, mm(queries, keys, 1, 1) * 0.125, -1e30)
        top = jnp.max(scores, axis=-1, keepdims=True)
        exps = jnp.exp(scores - top)
        total = jnp.sum(exps, axis=-1, keepdims=True)
        probs = (exps * (1.0 / total)).astype(bf16)
        context_ref[:, g * 128 : (g + 1) * 128] = joined(mm(probs, values)).astype(bf16)
        kept = top + jnp.log(total)
        stats = jnp.where(lane == 2 * g, kept[:ROWS], stats)
        stats = jnp.where(lane == 2 * g + 1, kept[ROWS:], stats)
    stats_ref[...] = stats


def router_gates(named, normed_ffn, gains):
    logits = mm(normed_ffn, gains.astype(bf16), 1, 1)
    chosen = []
    for one in named:
        value = jnp.zeros((ROWS, 1), f32)
        for k in range(EXPERTS):
            value = value + jnp.where(one == k, logits[:, 2 + k : 3 + k], 0.0)
        chosen.append(value)
    top = jnp.maximum(chosen[0], chosen[1])
    exps = [jnp.exp(value - top) for value in chosen]
    total = exps[0] + exps[1]
    return [value / total for value in exps]


def dispatch_kernel(planes, rows, pos, lens, choice_ref, hidden_ref, context_ref, gains_ref, *refs):
    pieces = refs[:8]
    middle_ref, gates_ref = refs[8:10]
    outs = refs[10:14]
    (weights,) = refs[14:]
    load_rows(pos, pieces, rows, planes, [(weights, 0, QKV - K_END, MODEL_WIDTH)])
    choice = choice_ref[...]
    _, places = slots_of(choice, pos[1])
    attended = mm(context_ref[...], weights[...])
    middle = hidden_ref[...].astype(f32) + live_of(lens) * attended
    middle_ref[...] = middle
    gains = gains_ref[...]
    normed_ffn = (middle * row_scale(middle) * gains[1:2]).astype(bf16)
    gates = router_gates([choice[:, k : k + 1] for k in range(TOP)], normed_ffn, gains)
    lane = iota((ROWS, 128), 1)
    gates_ref[...] = jnp.where(lane == 0, gates[0], jnp.where(lane == 1, gates[1], 0.0))
    slotted = mm(places[0] + places[1], normed_ffn, 0, 0)
    beside = jnp.zeros((SLOTS, EXTRA), f32)
    for place, gate in zip(places, gates):
        high, low = two_parts(gate)
        columns = jnp.where(
            lane == 0, high.astype(f32), jnp.where(lane == 1, low.astype(f32), 0.0)
        ).astype(bf16)
        beside = beside + mm(place, columns, 0, 0)
    for f in range(EXPERTS):
        part = slice(f * STRIDE, f * STRIDE + CAP)
        outs[f][:, :MODEL_WIDTH] = slotted[part].astype(bf16)
        outs[f][:, MODEL_WIDTH:] = beside[part].astype(bf16)


def expert_places(pos, planes, rows_in, rows_out):
    places = []
    for core in range(2):
        for k in range(planes):
            for chip in range(4):
                who = owner(pos, k, chip, core)
                in_rows = pl.ds(pl.multiple_of(who * rows_in, rows_in), rows_in)
                out_rows = pl.ds(pl.multiple_of(who * rows_out, rows_out), rows_out)
                places.append((core, k, chip, in_rows, out_rows))
    return places


def expert_kernel(planes, rows_in, rows_out, pos, *refs):
    tokens, grads, pieces = refs[:4], refs[4:8], refs[8:12]
    refs = refs[12:]
    backs = refs[:4]
    x_ref, activated_ref, d_expert_ref, d_up_ref = refs[4:8]
    w_in, w_out = refs[8:]
    for core, k, chip, in_rows, out_rows in expert_places(pos, planes, rows_in, rows_out):
        source = pieces[core * 2 + k % 2]
        w_in[in_rows] = source[k // 2, chip, :rows_in]
        w_out[out_rows] = source[k // 2, chip, rows_in:]
    for f in range(EXPERTS):
        part = slice(f * CAP, (f + 1) * CAP)
        x_ref[part] = tokens[f][:, :MODEL_WIDTH]
        gate_slots = tokens[f][:, MODEL_WIDTH : MODEL_WIDTH + 1].astype(f32) + tokens[f][
            :, MODEL_WIDTH + 1 : MODEL_WIDTH + 2
        ].astype(f32)
        d_expert_ref[part] = (gate_slots * grads[f][...].astype(f32)).astype(bf16)
    x = x_ref[...]
    gate = mm(x, w_in[:, :FE])
    up = mm(x, w_in[:, FE:])
    sig = 1.0 / (1.0 + jnp.exp(-gate))
    silu = gate * sig
    activated = (silu * up).astype(bf16)
    activated_ref[...] = activated
    expert_out = mm(activated, w_out[...]).astype(bf16)
    d_act = mm(d_expert_ref[...], w_out[...], 1, 1)
    d_up_ref[:, :FE] = (d_act * up * (sig * (1.0 + gate * (1.0 - sig)))).astype(bf16)
    d_up_ref[:, FE:] = (d_act * silu).astype(bf16)
    d_x = mm(d_up_ref[...], w_in[...], 1, 1).astype(bf16)
    for f in range(EXPERTS):
        part = slice(f * CAP, (f + 1) * CAP)
        backs[f][:CAP] = expert_out[part]
        backs[f][CAP:] = d_x[part]


def expert_weights_kernel(planes, rows_in, rows_out, pos, x_ref, activated_ref, d_expert_ref, d_up_ref, *refs):
    kept, sent, d_in, d_out = refs
    d_out[...] = mm(activated_ref[...], d_expert_ref[...], 0, 0).astype(bf16)
    d_in[...] = mm(x_ref[...], d_up_ref[...], 0, 0).astype(bf16)
    for core, k, chip, in_rows, out_rows in expert_places(pos, planes, rows_in, rows_out):
        target = kept if core == 0 else sent
        target[k, chip, :rows_in] = d_in[in_rows]
        target[k, chip, rows_in:] = d_out[out_rows]


def combine_kernel(
    planes, rows, pos, lens, choice_ref, middle_ref, gates_ref, grad_ref, gains_ref, context_ref, *refs
):
    backs = refs[:4]
    out_ref, grad_middle_ref, grad_attended_ref, kept, sent = refs[4:9]
    (d_weights,) = refs[9:]
    choice = choice_ref[...]
    _, places = slots_of(choice, pos[1])
    live = live_of(lens)
    empty = jnp.zeros((STRIDE - CAP, MODEL_WIDTH), bf16)
    outs, grads = [], []
    for back in backs:
        outs += [back[:CAP], empty]
        grads += [back[CAP:], empty]
    outs = jnp.concatenate(outs, axis=0)
    grads = jnp.concatenate(grads, axis=0)
    picked = [mm(place, outs) for place in places]
    gates = [gates_ref[:, k : k + 1] for k in range(TOP)]
    middle = middle_ref[...]
    mixture = gates[0] * picked[0] + gates[1] * picked[1]
    out_ref[...] = (middle + live * mixture).astype(bf16)
    cotangent = grad_ref[...].astype(f32)
    grad_mix = live * cotangent
    grad_gates = [jnp.sum(grad_mix * one, axis=1, keepdims=True) for one in picked]
    total = gates[0] * grad_gates[0] + gates[1] * grad_gates[1]
    grad_chosen = [gate * (grad - total) for gate, grad in zip(gates, grad_gates)]
    gains = gains_ref[...]
    grad_normed = mm(places[0] + places[1], grads)
    lane = iota((ROWS, EXTRA), 1)
    grad_logits = jnp.zeros((ROWS, EXTRA), f32)
    for k in range(EXPERTS):
        one = jnp.zeros((ROWS, 1), f32)
        for choice_at in range(TOP):
            one = one + jnp.where(choice[:, choice_at : choice_at + 1] == k, grad_chosen[choice_at], 0.0)
        grad_normed = grad_normed + one * gains[2 + k : 3 + k]
        grad_logits = jnp.where(lane == 2 + k, one, grad_logits)
    scale = row_scale(middle)
    unit = middle * scale
    normed_ffn = (unit * gains[1:2]).astype(bf16)
    logits_high, logits_low = two_parts(grad_logits)
    gain_high, gain_low = two_parts(grad_normed * unit)
    first = (lane == 1).astype(f32).astype(bf16)
    d_weights[:, MODEL_WIDTH:] = (
        mm(normed_ffn, logits_high, 0, 0)
        + mm(normed_ffn, logits_low, 0, 0)
        + mm(gain_high, first, 0, 0)
        + mm(gain_low, first, 0, 0)
    ).astype(bf16)
    scaled = grad_normed * gains[1:2]
    grad_middle = cotangent + scale * (
        scaled - unit * jnp.mean(scaled * unit, axis=-1, keepdims=True)
    )
    grad_middle_ref[...] = grad_middle
    grad_attended = (live * grad_middle).astype(bf16)
    grad_attended_ref[...] = grad_attended
    d_weights[:, :MODEL_WIDTH] = mm(context_ref[...], grad_attended, 0, 0).astype(bf16)
    width = MODEL_WIDTH + EXTRA
    store_rows(pos, d_weights, kept, sent, rows, planes, range(4), 0, width)


def attend_back(allowed, qkv_ref, stats_ref, grad_context_ref, grads):
    twice = jnp.concatenate([allowed, allowed], axis=0)
    low = iota((ROWS, 128), 1) < HEAD_SIZE
    pairs = []
    for g in range(KEY_VALUE_HEADS):
        queries, keys, values = head_blocks(qkv_ref, g)
        kept = jnp.concatenate(
            [stats_ref[:, 2 * g : 2 * g + 1], stats_ref[:, 2 * g + 1 : 2 * g + 2]], axis=0
        )
        scores = jnp.where(twice > 0, mm(queries, keys, 1, 1) * 0.125, -1e30)
        probs = jnp.exp(scores - kept)
        d_context = halves(grad_context_ref[:, g * 128 : (g + 1) * 128])
        d_probs = mm(d_context, values, 1, 1)
        d_scores = (
            probs * (d_probs - jnp.sum(probs * d_probs, axis=-1, keepdims=True))
        ).astype(bf16)
        grads[:, g * 128 : (g + 1) * 128] = (joined(mm(d_scores, keys)) * 0.125).astype(bf16)
        d_keys = mm(d_scores, queries, 0, 0)
        d_values = mm(probs.astype(bf16), d_context, 0, 0)
        pairs.append([both + pltpu.roll(both, HEAD_SIZE, 1) for both in (d_keys, d_values)])
        if g % 2 == 1:
            at = Q_END + (g // 2) * 128
            d_keys = jnp.where(low, pairs[g - 1][0], pairs[g][0]) * 0.125
            d_values = jnp.where(low, pairs[g - 1][1], pairs[g][1])
            grads[:, at : at + 128] = d_keys.astype(bf16)
            at = at + K_END - Q_END
            grads[:, at : at + 128] = d_values.astype(bf16)


def context_kernel(planes, rows, pos, grad_attended_ref, *refs):
    pieces, out_ref, weights = refs[:8], refs[8], refs[9]
    load_rows(pos, pieces, rows, planes, [(weights, 0, QKV - K_END, MODEL_WIDTH)])
    out_ref[...] = mm(grad_attended_ref[...], weights[...], 1, 1).astype(bf16)


def back_kernel(planes, rows, pos, lens, normed_ref, qkv_ref, stats_ref, grad_context_ref, *refs):
    grads, kept, sent, d_weights = refs
    attend_back(allowed_of(lens).astype(f32), qkv_ref, stats_ref, grad_context_ref, grads)
    d_weights[...] = mm(normed_ref[...], grads[...], 0, 0).astype(bf16)
    store_rows(pos, d_weights, kept, sent, rows, planes, X_FIRST, 0, Q_END)
    kept, sent = kept.at[pl.ds(4, 4)], sent.at[pl.ds(4, 4)]
    store_rows(pos, d_weights, kept, sent, rows, planes, Y_FIRST, Q_END, QKV - Q_END)


def input_kernel(planes, rows, pos, hidden_ref, grad_middle_ref, gains_ref, grads_ref, *refs):
    first, second, grad_in_ref, weights = refs[:8], refs[8:16], refs[16], refs[17]
    load_rows(pos, first, rows, planes, [(weights, 0, 0, K_END)])
    load_rows(pos, second, rows, planes, [(weights, K_END, 0, QKV - K_END)])
    hidden = hidden_ref[...].astype(f32)
    scale = row_scale(hidden)
    unit = hidden * scale
    grad_normed = mm(grads_ref[...], weights[...], 1, 1)
    scaled = grad_normed * gains_ref[0:1, :]
    grad_hidden = grad_middle_ref[...] + scale * (
        scaled - unit * jnp.mean(scaled * unit, axis=-1, keepdims=True)
    )
    grad_in_ref[...] = grad_hidden.astype(bf16)


def owned_kernel(rows_in, rows_out, pos, *refs):
    pieces, in_ref, out_ref = refs[:4], refs[4], refs[5]
    for f in range(4):
        place = pl.ds(pl.multiple_of((pos[1] ^ f) * MODEL_WIDTH, MODEL_WIDTH), MODEL_WIDTH)
        in_ref[:, place] = pieces[f][:rows_in].astype(f32)
        out_ref[:, place] = pieces[f][rows_in:].astype(f32)


def call(kernel, operands, n_scalars, outs, scratch, name, flops=1000):
    here = pl.BlockSpec(memory_space=pltpu.VMEM)
    scalar = pl.BlockSpec(memory_space=pltpu.SMEM)
    return pl.pallas_call(
        kernel,
        out_shape=tuple(outs),
        in_specs=[scalar] * n_scalars + [here] * (len(operands) - n_scalars),
        out_specs=(here,) * len(outs),
        scratch_shapes=scratch,
        compiler_params=pltpu.CompilerParams(vmem_limit_bytes=VMEM_LIMIT),
        cost_estimate=pl.CostEstimate(flops=flops, bytes_accessed=1000, transcendentals=0),
        name=name,
    )(*operands)


def exchanged(
    hidden_in,
    grad_out,
    seq_lens,
    expert_choice,
    gain_attn,
    w_query,
    key_weight,
    value_weight,
    w_attn_out,
    gain_ffn,
    w_router,
    w_expert_in,
    w_expert_out,
):
    n = lax.axis_size("fsdp")
    planes = n // PLANE
    me = lax.axis_index("fsdp")
    plane, chip, core = me // PLANE, (me // 2) % 4, me % 2
    pos = jnp.stack([plane, chip, core]).astype(jnp.int32)
    rows = w_query.shape[0]
    rows_out = w_expert_out.shape[0]
    both = rows + rows_out

    def swap(value, offset):
        return lax.ppermute(value, "fsdp", [(i, i ^ offset) for i in range(n)])

    def after(value, *earlier):
        return lax.optimization_barrier((value, *earlier))[0]

    def array(*shape, dtype=bf16):
        return jax.ShapeDtypeStruct(shape, dtype)

    def summed(*values):
        total = values[0].astype(f32)
        for one in values[1:]:
            total = total + one.astype(f32)
        return total

    def low_sum(*values):
        return summed(*values).astype(bf16)

    def widen(blocks, offset):
        other = swap(blocks, PLANE * offset)
        return jnp.stack([blocks, other], axis=1).reshape((-1,) + blocks.shape[1:])

    def fold(parts, offset, *earlier):
        return low_sum(parts[0::2], after(swap(parts[1::2], PLANE * offset), *earlier))

    def to_chips(parts):
        return [parts[0]] + [swap(parts[f], 2 * f) for f in range(1, 4)]

    def both_cores(pieces):
        return list(pieces) + [swap(one, 1) for one in pieces]

    grad_slots = to_chips(
        call(
            cotangent_kernel,
            (pos, seq_lens, expert_choice, grad_out),
            2,
            [array(CAP, MODEL_WIDTH)] * 4,
            [],
            "slot_cotangents",
        )
    )
    by_expert = jnp.concatenate(
        [
            w_expert_in.reshape(rows, EXPERTS, 2 * FE),
            w_expert_out.reshape(rows_out, EXPERTS, MODEL_WIDTH),
        ],
        axis=0,
    ).transpose(1, 0, 2)
    expert_blocks = jnp.stack(
        to_chips([lax.dynamic_index_in_dim(by_expert, chip ^ f, 0, False) for f in range(4)])
    )[None]

    beside = jnp.concatenate(
        [gain_attn[:, None], gain_ffn[:, None], w_router, jnp.zeros((rows, EXTRA - 6), bf16)], axis=1
    )
    weights = jnp.concatenate([w_query, key_weight, beside, value_weight, w_attn_out], axis=1)[None]
    offset = planes // 2
    while offset:
        weights = widen(weights, offset)
        if offset > 1:
            weights = after(weights, expert_blocks)
        offset = offset // 2
    weights = after(weights, *grad_slots)
    first, second = weights[:, :, : K_END + EXTRA], weights[:, :, K_END + EXTRA :]
    first_x, second_y = swap(first, 2), swap(second, 4)
    first_y, second_x = swap(first, 4), swap(second, 2)
    offset = planes // 2
    expert_blocks = after(expert_blocks, weights)
    while offset > 1:
        expert_blocks = widen(expert_blocks, offset)
        offset = offset // 2
    first_xy = swap(after(first_x, expert_blocks), 4)
    second_xy = swap(after(second_y, expert_blocks), 2)
    first_pieces = both_cores([after(first, first_x, second_y), first_x, first_y, first_xy])
    second_pieces = both_cores([after(second, first_x, second_y), second_x, second_y, second_xy])
    odd_blocks = swap(expert_blocks, PLANE)

    normed, gains, qkv, context, stats = call(
        lambda *refs: attention_kernel(planes, rows, *refs),
        (pos, seq_lens, hidden_in, *first_pieces, *second_pieces),
        2,
        [
            array(ROWS, MODEL_WIDTH),
            array(16, MODEL_WIDTH, dtype=f32),
            array(ROWS, QKV),
            array(ROWS, Q_END),
            array(ROWS, 128, dtype=f32),
        ],
        [pltpu.VMEM((MODEL_WIDTH, QKV + EXTRA), bf16)],
        "attention",
    )
    middle, gates, *dispatched = call(
        lambda *refs: dispatch_kernel(planes, rows, *refs),
        (pos, seq_lens, expert_choice, hidden_in, context, gains, *second_pieces),
        2,
        [array(ROWS, MODEL_WIDTH, dtype=f32), array(ROWS, 128, dtype=f32)]
        + [array(CAP, MODEL_WIDTH + EXTRA)] * 4,
        [pltpu.VMEM((MODEL_WIDTH, MODEL_WIDTH), bf16)],
        "dispatch",
    )
    dispatched = to_chips(dispatched)

    expert_pieces = both_cores([after(expert_blocks, context), after(odd_blocks, middle)])
    slots = EXPERTS * CAP
    *backs, x, activated, d_expert, d_up = call(
        lambda *refs: expert_kernel(planes, rows, rows_out, *refs),
        (pos, *dispatched, *grad_slots, *expert_pieces),
        1,
        [array(2 * CAP, MODEL_WIDTH)] * 4
        + [array(slots, MODEL_WIDTH), array(slots, FE), array(slots, MODEL_WIDTH), array(slots, 2 * FE)],
        [pltpu.VMEM((MODEL_WIDTH, 2 * FE), bf16), pltpu.VMEM((FE, MODEL_WIDTH), bf16)],
        "experts",
    )
    backs = to_chips(backs)
    block_output, grad_middle, grad_attended, kept, sent = call(
        lambda *refs: combine_kernel(planes, rows, *refs),
        (
            pos,
            seq_lens,
            expert_choice,
            middle,
            gates,
            grad_out,
            gains,
            context,
            *backs,
        ),
        2,
        [
            array(ROWS, MODEL_WIDTH),
            array(ROWS, MODEL_WIDTH, dtype=f32),
            array(ROWS, MODEL_WIDTH),
        ]
        + [array(4, planes, rows, MODEL_WIDTH + EXTRA)] * 2,
        [pltpu.VMEM((MODEL_WIDTH, MODEL_WIDTH + EXTRA), bf16)],
        "combine",
    )
    expert_kept, expert_sent = call(
        lambda *refs: expert_weights_kernel(planes, rows, rows_out, *refs),
        (pos, after(x, grad_attended), activated, d_expert, d_up),
        1,
        [array(planes, 4, both, MODEL_WIDTH)] * 2,
        [pltpu.VMEM((MODEL_WIDTH, 2 * FE), bf16), pltpu.VMEM((FE, MODEL_WIDTH), bf16)],
        "expert_weights",
    )
    expert_parts = low_sum(expert_kept, swap(expert_sent, 1))
    (grad_context,) = call(
        lambda *refs: context_kernel(planes, rows, *refs),
        (pos, grad_attended, *second_pieces),
        1,
        [array(ROWS, Q_END)],
        [pltpu.VMEM((MODEL_WIDTH, MODEL_WIDTH), bf16)],
        "context_gradients",
    )
    other = swap(sent, 1)
    out_parts = [low_sum(kept[f], other[f]) for f in range(4)]
    out_sums = to_chips(out_parts)
    grads, kept, sent = call(
        lambda *refs: back_kernel(planes, rows, *refs),
        (pos, seq_lens, after(normed, *out_parts), qkv, stats, grad_context),
        2,
        [array(ROWS, QKV)] + [array(8, planes, rows, QKV // 2)] * 2,
        [pltpu.VMEM((MODEL_WIDTH, QKV), bf16)],
        "attention_back",
        2 * 10**9,
    )
    expert_parts = fold(expert_parts, 1, grads)
    other = swap(sent, 1)
    keep_q, send_q, keep_kv, send_kv = [
        low_sum(kept[i : i + 2], other[i : i + 2]) for i in range(0, 8, 2)
    ]
    from_x = swap(after(send_q, *out_sums), 2)
    from_y = swap(after(send_kv, *out_sums), 4)
    (grad_in,) = call(
        lambda *refs: input_kernel(planes, rows, *refs),
        (
            pos,
            hidden_in,
            grad_middle,
            gains,
            after(grads, send_q, send_kv),
            *first_pieces,
            *second_pieces,
        ),
        1,
        [array(ROWS, MODEL_WIDTH)],
        [pltpu.VMEM((MODEL_WIDTH, QKV), bf16)],
        "input_gradient",
    )
    half_q, half_kv = low_sum(keep_q, from_x), low_sum(keep_kv, from_y)
    rest_q, rest_kv = swap(after(half_q[1], grad_in), 4), swap(after(half_kv[1], grad_in), 2)
    owned_qkv = jnp.concatenate([low_sum(half_q[0], rest_q), low_sum(half_kv[0], rest_kv)], axis=-1)
    owned_out = low_sum(*[after(one, owned_qkv) for one in out_sums])
    owned_out = fold(owned_out, 1, owned_qkv)
    owned_out = fold(owned_out, 2, owned_qkv)
    offset = 2
    while expert_parts.shape[0] > 1:
        expert_parts = fold(expert_parts, offset, rest_kv)
        offset = 2 * offset
    expert_mine = to_chips(expert_parts[0])
    owned_qkv = summed(
        owned_qkv[0], *[swap(owned_qkv[k], PLANE * k) for k in range(1, planes)]
    )
    grad_w_expert_in, grad_w_expert_out = call(
        lambda *refs: owned_kernel(rows, rows_out, *refs),
        (pos, *expert_mine),
        1,
        [
            array(rows, EXPERTS * 2 * FE, dtype=f32),
            array(rows_out, EXPERTS * MODEL_WIDTH, dtype=f32),
        ],
        [],
        "expert_rows",
    )
    owned_out = owned_out[0].astype(f32)
    d_query, d_key, d_value = owned_qkv[:, :Q_END], owned_qkv[:, Q_END:K_END], owned_qkv[:, K_END:]
    d_gain_attn = sum(
        jnp.sum(d * w.astype(f32), axis=1)
        for d, w in ((d_query, w_query), (d_key, key_weight), (d_value, value_weight))
    ) / gain_attn.astype(f32)
    return (
        block_output,
        grad_in,
        d_gain_attn,
        d_query,
        d_key,
        d_value,
        owned_out[:, :MODEL_WIDTH],
        owned_out[:, MODEL_WIDTH + 1],
        owned_out[:, MODEL_WIDTH + 2 : MODEL_WIDTH + 2 + EXPERTS],
        grad_w_expert_in,
        grad_w_expert_out,
    )


def rms_scale(values):
    return lax.rsqrt(jnp.mean(values * values, axis=-1, keepdims=True) + eps)


def layout(lengths, count_of_rows):
    microbatch_count = lengths.shape[0]
    microbatch_rows = count_of_rows // microbatch_count
    first_len = jnp.broadcast_to(lengths[:, 0:1], (microbatch_count, microbatch_rows))
    second_len = jnp.broadcast_to(lengths[:, 1:2], (microbatch_count, microbatch_rows))
    inner_grid = jnp.broadcast_to(
        jnp.arange(microbatch_rows, dtype=jnp.int32)[None, :], (microbatch_count, microbatch_rows)
    )
    section = jnp.where(
        inner_grid < first_len, 0, jnp.where(inner_grid < first_len + second_len, 1, 2)
    )
    allowed = (section[:, :, None] == section[:, None, :]) & (
        inner_grid[:, None, :] <= inner_grid[:, :, None]
    )
    live_rows = (section < 2).astype(jnp.float32).reshape(count_of_rows, 1)
    return (live_rows, allowed)


def routing(choice_ids, capacity):
    count_of_rows, top_count = choice_ids.shape
    expert_ids = jnp.arange(EXPERTS, dtype=jnp.int32)
    expert_hits = (choice_ids[:, :, None] == expert_ids[None, None, :]).astype(jnp.int32)
    per_row = jnp.sum(expert_hits, axis=1)
    before = jnp.cumsum(per_row, axis=0) - per_row
    position = jnp.sum(expert_hits * before[:, None, :], axis=2)
    slot_index = choice_ids * capacity + position
    pair_index = jnp.arange(count_of_rows * top_count, dtype=jnp.int32)
    source = (
        jnp.full((EXPERTS * capacity,), count_of_rows * top_count, jnp.int32)
        .at[slot_index.reshape(-1)]
        .set(pair_index)
    )
    return (expert_hits, slot_index, source)


def shards(
    hidden_in,
    grad_out,
    seq_lens,
    expert_choice,
    gain_attn,
    w_query,
    key_weight,
    value_weight,
    w_attn_out,
    gain_ffn,
    w_router,
    w_expert_in,
    w_expert_out,
):
    count_of_rows = hidden_in.shape[0]
    microbatch_count = seq_lens.shape[0]
    microbatch_rows = count_of_rows // microbatch_count
    query_group_size = QUERY_HEADS // KEY_VALUE_HEADS
    device_count = lax.axis_size("fsdp")
    live_rows, allowed = layout(seq_lens, count_of_rows)
    mask_grid = allowed[:, None, None]
    hidden = hidden_in.astype(jnp.float32)
    cotangent = grad_out.astype(jnp.float32)
    attention_set = (
        lax.all_gather(gain_attn, "fsdp", axis=0, tiled=True),
        lax.all_gather(w_query, "fsdp", axis=0, tiled=True),
        lax.all_gather(key_weight, "fsdp", axis=0, tiled=True),
        lax.all_gather(value_weight, "fsdp", axis=0, tiled=True),
        lax.all_gather(w_attn_out, "fsdp", axis=0, tiled=True),
        lax.all_gather(gain_ffn, "fsdp", axis=0, tiled=True),
        lax.all_gather(w_router, "fsdp", axis=0, tiled=True),
    )
    gain_one = attention_set[0].astype(jnp.float32)
    gain_two = attention_set[5].astype(jnp.float32)
    scale_one = rms_scale(hidden)
    unit_one = hidden * scale_one
    normed = (unit_one * gain_one).astype(jnp.bfloat16)
    query_rows = jnp.dot(normed, attention_set[1], preferred_element_type=jnp.float32).astype(
        jnp.bfloat16
    )
    every_key = jnp.dot(normed, attention_set[2], preferred_element_type=jnp.float32).astype(
        jnp.bfloat16
    )
    every_value = jnp.dot(normed, attention_set[3], preferred_element_type=jnp.float32).astype(
        jnp.bfloat16
    )
    query_tiles = query_rows.reshape(
        microbatch_count, microbatch_rows, KEY_VALUE_HEADS, query_group_size, HEAD_SIZE
    )
    key_tiles = every_key.reshape(microbatch_count, microbatch_rows, KEY_VALUE_HEADS, HEAD_SIZE)
    value_tiles = every_value.reshape(microbatch_count, microbatch_rows, KEY_VALUE_HEADS, HEAD_SIZE)

    def score_block():
        raw_scores = (
            jnp.einsum(
                "mqgrd,mkgd->mgrqk", query_tiles, key_tiles, preferred_element_type=jnp.float32
            )
            * 0.125
        )
        return jnp.where(mask_grid, raw_scores, -1e30)

    scores = score_block()
    top_score = jnp.max(scores, axis=-1, keepdims=True)
    weights = jnp.exp(scores - top_score)
    row_total = jnp.sum(weights, axis=-1, keepdims=True)
    probs_low = (weights / row_total).astype(jnp.bfloat16)
    context = jnp.einsum(
        "mgrqk,mkgd->mqgrd", probs_low, value_tiles, preferred_element_type=jnp.float32
    )
    context = context.reshape(count_of_rows, QUERY_HEADS * HEAD_SIZE).astype(jnp.bfloat16)
    attended = jnp.dot(context, attention_set[4], preferred_element_type=jnp.float32)
    middle = hidden + live_rows * attended
    scale_two = rms_scale(middle)
    unit_two = middle * scale_two
    normed_ffn = (unit_two * gain_two).astype(jnp.bfloat16)
    logits = jnp.dot(normed_ffn, attention_set[6], preferred_element_type=jnp.float32)
    expert_hits, slot_index, source = routing(expert_choice, CAP)
    hits_float = expert_hits.astype(jnp.float32)
    chosen = jnp.sum(hits_float * logits[:, None, :], axis=2)
    chosen_top = jnp.max(chosen, axis=1, keepdims=True)
    gate_exp = jnp.exp(chosen - chosen_top)
    gate_weights = gate_exp / jnp.sum(gate_exp, axis=1, keepdims=True)
    padded = jnp.concatenate([normed_ffn, jnp.zeros((1, MODEL_WIDTH), jnp.bfloat16)], axis=0)
    dispatched = padded[source // TOP].reshape(EXPERTS, CAP, MODEL_WIDTH)
    expert_in_full = lax.all_gather(w_expert_in, "fsdp", axis=0, tiled=True)
    expert_out_full = lax.all_gather(w_expert_out, "fsdp", axis=0, tiled=True)
    in_grid = expert_in_full.reshape(MODEL_WIDTH, EXPERTS, 2 * FE)
    out_grid = expert_out_full.reshape(FE, EXPERTS, MODEL_WIDTH)
    gate_up = jnp.einsum("ecd,def->ecf", dispatched, in_grid, preferred_element_type=jnp.float32)
    gate_part = gate_up[:, :, :FE]
    up_part = gate_up[:, :, FE:]
    sigmoid_gate = lax.logistic(gate_part)
    silu_gate = gate_part * sigmoid_gate
    activated = (silu_gate * up_part).astype(jnp.bfloat16)
    expert_out = jnp.einsum("ecf,fed->ecd", activated, out_grid, preferred_element_type=jnp.float32)
    picked = expert_out.reshape(EXPERTS * CAP, MODEL_WIDTH)[slot_index]
    mixture = jnp.sum(gate_weights[:, :, None] * picked, axis=1)
    block_output = (middle + live_rows * mixture).astype(jnp.bfloat16)
    back_set = (
        lax.all_gather(gain_attn, "fsdp", axis=0, tiled=True),
        lax.all_gather(w_query, "fsdp", axis=0, tiled=True),
        lax.all_gather(key_weight, "fsdp", axis=0, tiled=True),
        lax.all_gather(value_weight, "fsdp", axis=0, tiled=True),
        lax.all_gather(w_attn_out, "fsdp", axis=0, tiled=True),
        lax.all_gather(gain_ffn, "fsdp", axis=0, tiled=True),
        lax.all_gather(w_router, "fsdp", axis=0, tiled=True),
    )
    out_back = lax.all_gather(w_expert_out, "fsdp", axis=0, tiled=True).reshape(
        FE, EXPERTS, MODEL_WIDTH
    )
    in_back = lax.all_gather(w_expert_in, "fsdp", axis=0, tiled=True).reshape(
        MODEL_WIDTH, EXPERTS, 2 * FE
    )
    grad_mix = live_rows * cotangent
    grad_gates = jnp.sum(grad_mix[:, None, :] * picked, axis=2)
    grad_chosen = gate_weights * (
        grad_gates - jnp.sum(gate_weights * grad_gates, axis=1, keepdims=True)
    )
    grad_logits = jnp.sum(grad_chosen[:, :, None] * hits_float, axis=1)
    pair_grads = (gate_weights[:, :, None] * grad_mix[:, None, :]).reshape(
        count_of_rows * TOP, MODEL_WIDTH
    )
    pair_padded = jnp.concatenate([pair_grads, jnp.zeros((1, MODEL_WIDTH), jnp.float32)], axis=0)
    grad_expert_out = pair_padded[source].astype(jnp.bfloat16).reshape(EXPERTS, CAP, MODEL_WIDTH)
    grad_activated = jnp.einsum(
        "ecd,fed->ecf", grad_expert_out, out_back, preferred_element_type=jnp.float32
    )
    out_rows = w_expert_out.shape[0]
    columns = activated
    grad_w_expert_out = lax.psum_scatter(
        jnp.einsum(
            "ecn,ecd->ned", columns, grad_expert_out, preferred_element_type=jnp.float32
        ).reshape(1 * lax.axis_size("fsdp"), out_rows * EXPERTS * MODEL_WIDTH),
        "fsdp",
        scatter_dimension=0,
        tiled=True,
    ).reshape(out_rows, EXPERTS * MODEL_WIDTH)
    grad_gate = grad_activated * up_part * (sigmoid_gate * (1.0 + gate_part * (1.0 - sigmoid_gate)))
    grad_up = grad_activated * silu_gate
    grad_gate_up = jnp.concatenate([grad_gate, grad_up], axis=-1).astype(jnp.bfloat16)
    grad_dispatched = jnp.einsum(
        "ecf,def->ecd", grad_gate_up, in_back, preferred_element_type=jnp.float32
    )
    in_rows = w_expert_in.shape[0]
    columns = dispatched
    grad_w_expert_in = lax.psum_scatter(
        jnp.einsum(
            "ecn,ecf->nef", columns, grad_gate_up, preferred_element_type=jnp.float32
        ).reshape(1 * lax.axis_size("fsdp"), in_rows * EXPERTS * 2 * FE),
        "fsdp",
        scatter_dimension=0,
        tiled=True,
    ).reshape(in_rows, EXPERTS * 2 * FE)
    router_full = back_set[6].astype(jnp.float32)
    grad_normed_ffn = jnp.sum(
        grad_dispatched.reshape(EXPERTS * CAP, MODEL_WIDTH)[slot_index], axis=1
    )
    grad_normed_ffn = grad_normed_ffn + jnp.dot(grad_logits, router_full.T, precision=highest)
    grad_router = jnp.dot(normed_ffn.astype(jnp.float32).T, grad_logits, precision=highest)
    back_gain_two = back_set[5].astype(jnp.float32)
    grad_gain_two = jnp.sum(grad_normed_ffn * unit_two, axis=0)
    scaled_two = grad_normed_ffn * back_gain_two
    grad_middle = cotangent + scale_two * (
        scaled_two - unit_two * jnp.mean(scaled_two * unit_two, axis=-1, keepdims=True)
    )
    grad_attended = (live_rows * grad_middle).astype(jnp.bfloat16)
    grad_out_proj = jnp.einsum(
        "ti,td->id", context, grad_attended, preferred_element_type=jnp.float32
    )
    context_gradient = jnp.einsum(
        "td,id->ti", grad_attended, back_set[4], preferred_element_type=jnp.float32
    ).astype(jnp.bfloat16)
    context_gradient_grid = context_gradient.reshape(
        microbatch_count, microbatch_rows, KEY_VALUE_HEADS, query_group_size, HEAD_SIZE
    )
    probs_again = jnp.exp(score_block() - top_score) / row_total
    probs_again_low = probs_again.astype(jnp.bfloat16)
    grad_probs = jnp.einsum(
        "mqgrd,mkgd->mgrqk", context_gradient_grid, value_tiles, preferred_element_type=jnp.float32
    )
    value_gradient = jnp.einsum(
        "mgrqk,mqgrd->mkgd",
        probs_again_low,
        context_gradient_grid,
        preferred_element_type=jnp.float32,
    )
    grad_scores = probs_again * (
        grad_probs - jnp.sum(probs_again * grad_probs, axis=-1, keepdims=True)
    )
    grad_scores = grad_scores.astype(jnp.bfloat16)
    grad_queries = (
        jnp.einsum("mgrqk,mkgd->mqgrd", grad_scores, key_tiles, preferred_element_type=jnp.float32)
        * 0.125
    )
    grad_queries = grad_queries.reshape(count_of_rows, QUERY_HEADS * HEAD_SIZE).astype(jnp.bfloat16)
    key_gradient = (
        jnp.einsum(
            "mgrqk,mqgrd->mkgd", grad_scores, query_tiles, preferred_element_type=jnp.float32
        )
        * 0.125
    )
    key_gradient = key_gradient.reshape(count_of_rows, KEY_VALUE_HEADS * HEAD_SIZE).astype(
        jnp.bfloat16
    )
    value_gradient_narrow = value_gradient.reshape(
        count_of_rows, KEY_VALUE_HEADS * HEAD_SIZE
    ).astype(jnp.bfloat16)
    grad_query_proj = jnp.einsum(
        "td,ti->di", normed, grad_queries, preferred_element_type=jnp.float32
    )
    grad_key_proj = jnp.einsum(
        "td,ti->di", normed, key_gradient, preferred_element_type=jnp.float32
    )
    grad_value_proj = jnp.einsum(
        "td,ti->di", normed, value_gradient_narrow, preferred_element_type=jnp.float32
    )
    grad_normed = jnp.einsum(
        "ti,di->td", grad_queries, back_set[1], preferred_element_type=jnp.float32
    )
    grad_normed = grad_normed + jnp.einsum(
        "ti,di->td", key_gradient, back_set[2], preferred_element_type=jnp.float32
    )
    grad_normed = grad_normed + jnp.einsum(
        "ti,di->td", value_gradient_narrow, back_set[3], preferred_element_type=jnp.float32
    )
    back_gain_one = back_set[0].astype(jnp.float32)
    grad_gain_one = jnp.sum(grad_normed * unit_one, axis=0)
    scaled_one = grad_normed * back_gain_one
    grad_hidden = grad_middle + scale_one * (
        scaled_one - unit_one * jnp.mean(scaled_one * unit_one, axis=-1, keepdims=True)
    )
    terms = (
        grad_gain_one,
        grad_query_proj,
        grad_key_proj,
        grad_value_proj,
        grad_out_proj,
        grad_gain_two,
        grad_router,
    )
    local_shapes = (
        gain_attn.shape,
        w_query.shape,
        key_weight.shape,
        value_weight.shape,
        w_attn_out.shape,
        gain_ffn.shape,
        w_router.shape,
    )
    flat_terms = tuple((term.reshape(device_count, -1) for term in terms))
    owned = (
        lax.psum_scatter(flat_terms[0], "fsdp", scatter_dimension=0, tiled=True),
        lax.psum_scatter(flat_terms[1], "fsdp", scatter_dimension=0, tiled=True),
        lax.psum_scatter(flat_terms[2], "fsdp", scatter_dimension=0, tiled=True),
        lax.psum_scatter(flat_terms[3], "fsdp", scatter_dimension=0, tiled=True),
        lax.psum_scatter(flat_terms[4], "fsdp", scatter_dimension=0, tiled=True),
        lax.psum_scatter(flat_terms[5], "fsdp", scatter_dimension=0, tiled=True),
        lax.psum_scatter(flat_terms[6], "fsdp", scatter_dimension=0, tiled=True),
    )
    owned = tuple((piece.reshape(shape) for piece, shape in zip(owned, local_shapes)))
    return (
        block_output,
        grad_hidden.astype(jnp.bfloat16),
        owned[0],
        owned[1],
        owned[2],
        owned[3],
        owned[4],
        owned[5],
        owned[6],
        grad_w_expert_in,
        grad_w_expert_out,
    )


def solution(mesh):
    placed = (
        P("fsdp", None),
        P("fsdp", None),
        P("fsdp", None),
        P("fsdp", None),
        P("fsdp"),
        P("fsdp", None),
        P("fsdp", None),
        P("fsdp", None),
        P("fsdp", None),
        P("fsdp"),
        P("fsdp", None),
        P("fsdp", None),
        P("fsdp", None),
    )
    devices = mesh.shape["fsdp"]
    planes = devices // PLANE
    whole = devices % PLANE == 0 and planes > 1 and planes & (planes - 1) == 0 and FE % (16 * devices) == 0
    return jax.shard_map(
        exchanged if whole else shards,
        mesh=mesh,
        in_specs=placed,
        out_specs=(
            P("fsdp", None),
            P("fsdp", None),
            P("fsdp"),
            P("fsdp", None),
            P("fsdp", None),
            P("fsdp", None),
            P("fsdp", None),
            P("fsdp"),
            P("fsdp", None),
            P("fsdp", None),
            P("fsdp", None),
        ),
        check_vma=False,
    )
```

```python
import jax
import jax.numpy as jnp
from jax import lax
from jax.experimental import pallas as pl
from jax.experimental.pallas import tpu as pltpu
from jax.sharding import PartitionSpec as P

MODEL_WIDTH = 1024
QUERY_HEADS = 16
KEY_VALUE_HEADS = 8
HEAD_SIZE = 64
FE = 512
EXPERTS = 4
TOP = 2
CAP = 80

ROWS = 128
STRIDE = 96
SLOTS = EXPERTS * STRIDE
Q_END = QUERY_HEADS * HEAD_SIZE
K_END = Q_END + KEY_VALUE_HEADS * HEAD_SIZE
QKV = K_END + KEY_VALUE_HEADS * HEAD_SIZE
EXTRA = 128
X_FIRST, Y_FIRST = (0, 2, 1, 3), (0, 1, 2, 3)
PLANE = 8
f32 = jnp.float32
bf16 = jnp.bfloat16

eps = 1e-06
highest = lax.Precision.HIGHEST
VMEM_LIMIT = 44 * 1024 * 1024


def mm(left, right, left_dim=1, right_dim=0):
    return lax.dot_general(
        left, right, (((left_dim,), (right_dim,)), ((), ())), preferred_element_type=f32
    )


def two_parts(values):
    high = values.astype(bf16)
    return high, (values - high.astype(f32)).astype(bf16)


def iota(shape, dim):
    return lax.broadcasted_iota(jnp.int32, shape, dim)


def row_scale(values):
    return lax.rsqrt(jnp.mean(values * values, axis=-1, keepdims=True) + eps)


def section_of(lens, place):
    batch = place >> 6
    inner = place & 63
    first = jnp.where(batch == 0, lens[0, 0], lens[1, 0])
    total = first + jnp.where(batch == 0, lens[0, 1], lens[1, 1])
    part = jnp.where(inner < first, 0, jnp.where(inner < total, 1, 2))
    return batch, part


def live_of(lens):
    _, part = section_of(lens, iota((ROWS, 1), 0))
    return (part < 2).astype(f32)


def allowed_of(lens):
    row, column = iota((ROWS, 1), 0), iota((1, ROWS), 1)
    row_batch, row_part = section_of(lens, row)
    column_batch, column_part = section_of(lens, column)
    return (
        (row_batch * 4 + row_part) == (column_batch * 4 + column_part)
    ) & (column <= row)


def slots_of(choice, mine):
    lane = iota((ROWS, 128), 1)
    named = [choice[:, k : k + 1] ^ mine for k in range(TOP)]
    hits = jnp.zeros((ROWS, 128), f32)
    for one in named:
        hits = hits + (lane == one).astype(f32)
    earlier = (iota((ROWS, ROWS), 1) < iota((ROWS, ROWS), 0)).astype(bf16)
    before = mm(earlier, hits.astype(bf16))
    places = []
    for one in named:
        position = jnp.sum(jnp.where(lane == one, before, 0.0), axis=1, keepdims=True)
        slot = one * STRIDE + position.astype(jnp.int32)
        places.append((iota((ROWS, SLOTS), 1) == slot).astype(f32).astype(bf16))
    return named, places


def owner(pos, planes_off, chip_off, core_off):
    return ((pos[0] ^ planes_off) * 4 + (pos[1] ^ chip_off)) * 2 + (pos[2] ^ core_off)


def load_rows(pos, pieces, rows, planes, moves):
    for core in range(2):
        for chip in range(4):
            for k in range(planes):
                place = pl.multiple_of(owner(pos, k, chip, core) * rows, rows)
                for buffer, to, at, width in moves:
                    buffer[pl.ds(place, rows), to : to + width] = pieces[core * 4 + chip][
                        k, :, at : at + width
                    ]


def store_rows(pos, buffer, kept, sent, rows, planes, order, at, width):
    for core, target in ((0, kept), (1, sent)):
        for i, chip in enumerate(order):
            for k in range(planes):
                place = pl.multiple_of(owner(pos, k, chip, core) * rows, rows)
                target[i, k] = buffer[pl.ds(place, rows), at : at + width]


def cotangent_kernel(pos, lens, choice_ref, grad_ref, *outs):
    _, places = slots_of(choice_ref[...], pos[1])
    grad_mix = (live_of(lens) * grad_ref[...].astype(f32)).astype(bf16)
    slotted = mm(places[0] + places[1], grad_mix, 0, 0)
    for f in range(EXPERTS):
        outs[f][...] = slotted[f * STRIDE : f * STRIDE + CAP].astype(bf16)


def halves(block):
    low = iota(block.shape, 1) < HEAD_SIZE
    wide = block.astype(f32)
    return jnp.concatenate(
        [jnp.where(low, wide, 0.0), jnp.where(low, 0.0, wide)], axis=0
    ).astype(bf16)


def joined(both):
    upper, lower = both[:ROWS], both[ROWS:]
    return jnp.where(iota(upper.shape, 1) < HEAD_SIZE, upper, lower)


def doubled(pair, g):
    wide = pair.astype(f32)
    turned = pltpu.roll(wide, HEAD_SIZE, 1)
    low = iota(wide.shape, 1) < HEAD_SIZE
    first, second = (wide, turned) if g % 2 == 0 else (turned, wide)
    return jnp.where(low, first, second).astype(bf16)


def head_blocks(qkv_ref, g):
    pair = (g // 2) * 128
    queries = halves(qkv_ref[:, g * 128 : (g + 1) * 128])
    keys = doubled(qkv_ref[:, Q_END + pair : Q_END + pair + 128], g)
    values = doubled(qkv_ref[:, K_END + pair : K_END + pair + 128], g)
    return queries, keys, values


def attention_kernel(planes, rows, pos, lens, hidden_ref, *refs):
    first, second = refs[:8], refs[8:16]
    normed_ref, gains_ref, qkv_ref, context_ref, stats_ref, weights = refs[16:]
    load_rows(pos, first, rows, planes, [(weights, 0, 0, K_END), (weights, QKV, K_END, EXTRA)])
    load_rows(pos, second, rows, planes, [(weights, K_END, 0, QKV - K_END)])
    hidden = hidden_ref[...].astype(f32)
    unit = hidden * row_scale(hidden)
    pick = (iota((16, EXTRA), 0) == iota((16, EXTRA), 1)).astype(f32).astype(bf16)
    gains = mm(pick, weights[:, QKV:], 1, 1)
    gains_ref[...] = gains
    normed = (unit * gains[0:1]).astype(bf16)
    normed_ref[...] = normed
    for at in range(0, QKV, 512):
        qkv_ref[:, at : at + 512] = mm(normed, weights[:, at : at + 512]).astype(bf16)
    allowed = allowed_of(lens).astype(f32)
    twice = jnp.concatenate([allowed, allowed], axis=0)
    lane = iota((ROWS, 128), 1)
    stats = jnp.zeros((ROWS, 128), f32)
    for g in range(KEY_VALUE_HEADS):
        queries, keys, values = head_blocks(qkv_ref, g)
        scores = jnp.where(twice > 0, mm(queries, keys, 1, 1) * 0.125, -1e30)
        top = jnp.max(scores, axis=-1, keepdims=True)
        exps = jnp.exp(scores - top)
        total = jnp.sum(exps, axis=-1, keepdims=True)
        probs = (exps * (1.0 / total)).astype(bf16)
        context_ref[:, g * 128 : (g + 1) * 128] = joined(mm(probs, values)).astype(bf16)
        kept = top + jnp.log(total)
        stats = jnp.where(lane == 2 * g, kept[:ROWS], stats)
        stats = jnp.where(lane == 2 * g + 1, kept[ROWS:], stats)
    stats_ref[...] = stats


def router_gates(named, normed_ffn, gains):
    logits = mm(normed_ffn, gains.astype(bf16), 1, 1)
    chosen = []
    for one in named:
        value = jnp.zeros((ROWS, 1), f32)
        for k in range(EXPERTS):
            value = value + jnp.where(one == k, logits[:, 2 + k : 3 + k], 0.0)
        chosen.append(value)
    top = jnp.maximum(chosen[0], chosen[1])
    exps = [jnp.exp(value - top) for value in chosen]
    total = exps[0] + exps[1]
    return [value / total for value in exps]


def dispatch_kernel(planes, rows, pos, lens, choice_ref, hidden_ref, context_ref, gains_ref, *refs):
    pieces = refs[:8]
    middle_ref, gates_ref = refs[8:10]
    outs = refs[10:14]
    (weights,) = refs[14:]
    load_rows(pos, pieces, rows, planes, [(weights, 0, QKV - K_END, MODEL_WIDTH)])
    choice = choice_ref[...]
    _, places = slots_of(choice, pos[1])
    attended = mm(context_ref[...], weights[...])
    middle = hidden_ref[...].astype(f32) + live_of(lens) * attended
    middle_ref[...] = middle
    gains = gains_ref[...]
    normed_ffn = (middle * row_scale(middle) * gains[1:2]).astype(bf16)
    gates = router_gates([choice[:, k : k + 1] for k in range(TOP)], normed_ffn, gains)
    lane = iota((ROWS, 128), 1)
    gates_ref[...] = jnp.where(lane == 0, gates[0], jnp.where(lane == 1, gates[1], 0.0))
    slotted = mm(places[0] + places[1], normed_ffn, 0, 0)
    beside = jnp.zeros((SLOTS, EXTRA), f32)
    for place, gate in zip(places, gates):
        high, low = two_parts(gate)
        columns = jnp.where(
            lane == 0, high.astype(f32), jnp.where(lane == 1, low.astype(f32), 0.0)
        ).astype(bf16)
        beside = beside + mm(place, columns, 0, 0)
    for f in range(EXPERTS):
        part = slice(f * STRIDE, f * STRIDE + CAP)
        outs[f][:, :MODEL_WIDTH] = slotted[part].astype(bf16)
        outs[f][:, MODEL_WIDTH:] = beside[part].astype(bf16)


def expert_places(pos, planes, rows_in, rows_out):
    places = []
    for core in range(2):
        for k in range(planes):
            for chip in range(4):
                who = owner(pos, k, chip, core)
                in_rows = pl.ds(pl.multiple_of(who * rows_in, rows_in), rows_in)
                out_rows = pl.ds(pl.multiple_of(who * rows_out, rows_out), rows_out)
                places.append((core, k, chip, in_rows, out_rows))
    return places


def expert_kernel(planes, rows_in, rows_out, pos, *refs):
    tokens, grads, pieces = refs[:4], refs[4:8], refs[8:12]
    refs = refs[12:]
    backs = refs[:4]
    x_ref, activated_ref, d_expert_ref, d_up_ref = refs[4:8]
    w_in, w_out = refs[8:]
    for core, k, chip, in_rows, out_rows in expert_places(pos, planes, rows_in, rows_out):
        source = pieces[core * 2 + k % 2]
        w_in[in_rows] = source[k // 2, chip, :rows_in]
        w_out[out_rows] = source[k // 2, chip, rows_in:]
    for f in range(EXPERTS):
        part = slice(f * CAP, (f + 1) * CAP)
        x_ref[part] = tokens[f][:, :MODEL_WIDTH]
        gate_slots = tokens[f][:, MODEL_WIDTH : MODEL_WIDTH + 1].astype(f32) + tokens[f][
            :, MODEL_WIDTH + 1 : MODEL_WIDTH + 2
        ].astype(f32)
        d_expert_ref[part] = (gate_slots * grads[f][...].astype(f32)).astype(bf16)
    x = x_ref[...]
    gate = mm(x, w_in[:, :FE])
    up = mm(x, w_in[:, FE:])
    sig = 1.0 / (1.0 + jnp.exp(-gate))
    silu = gate * sig
    activated = (silu * up).astype(bf16)
    activated_ref[...] = activated
    expert_out = mm(activated, w_out[...]).astype(bf16)
    d_act = mm(d_expert_ref[...], w_out[...], 1, 1)
    d_up_ref[:, :FE] = (d_act * up * (sig * (1.0 + gate * (1.0 - sig)))).astype(bf16)
    d_up_ref[:, FE:] = (d_act * silu).astype(bf16)
    d_x = mm(d_up_ref[...], w_in[...], 1, 1).astype(bf16)
    for f in range(EXPERTS):
        part = slice(f * CAP, (f + 1) * CAP)
        backs[f][:CAP] = expert_out[part]
        backs[f][CAP:] = d_x[part]


def expert_weights_kernel(planes, rows_in, rows_out, pos, x_ref, activated_ref, d_expert_ref, d_up_ref, *refs):
    kept, sent, d_in, d_out = refs
    d_out[...] = mm(activated_ref[...], d_expert_ref[...], 0, 0).astype(bf16)
    d_in[...] = mm(x_ref[...], d_up_ref[...], 0, 0).astype(bf16)
    for core, k, chip, in_rows, out_rows in expert_places(pos, planes, rows_in, rows_out):
        target = kept if core == 0 else sent
        target[k, chip, :rows_in] = d_in[in_rows]
        target[k, chip, rows_in:] = d_out[out_rows]


def combine_kernel(
    planes, rows, pos, lens, choice_ref, middle_ref, gates_ref, grad_ref, gains_ref, context_ref, *refs
):
    backs = refs[:4]
    out_ref, grad_middle_ref, grad_attended_ref, kept, sent = refs[4:9]
    (d_weights,) = refs[9:]
    choice = choice_ref[...]
    _, places = slots_of(choice, pos[1])
    live = live_of(lens)
    empty = jnp.zeros((STRIDE - CAP, MODEL_WIDTH), bf16)
    outs, grads = [], []
    for back in backs:
        outs += [back[:CAP], empty]
        grads += [back[CAP:], empty]
    outs = jnp.concatenate(outs, axis=0)
    grads = jnp.concatenate(grads, axis=0)
    picked = [mm(place, outs) for place in places]
    gates = [gates_ref[:, k : k + 1] for k in range(TOP)]
    middle = middle_ref[...]
    mixture = gates[0] * picked[0] + gates[1] * picked[1]
    out_ref[...] = (middle + live * mixture).astype(bf16)
    cotangent = grad_ref[...].astype(f32)
    grad_mix = live * cotangent
    grad_gates = [jnp.sum(grad_mix * one, axis=1, keepdims=True) for one in picked]
    total = gates[0] * grad_gates[0] + gates[1] * grad_gates[1]
    grad_chosen = [gate * (grad - total) for gate, grad in zip(gates, grad_gates)]
    gains = gains_ref[...]
    grad_normed = mm(places[0] + places[1], grads)
    lane = iota((ROWS, EXTRA), 1)
    grad_logits = jnp.zeros((ROWS, EXTRA), f32)
    for k in range(EXPERTS):
        one = jnp.zeros((ROWS, 1), f32)
        for choice_at in range(TOP):
            one = one + jnp.where(choice[:, choice_at : choice_at + 1] == k, grad_chosen[choice_at], 0.0)
        grad_normed = grad_normed + one * gains[2 + k : 3 + k]
        grad_logits = jnp.where(lane == 2 + k, one, grad_logits)
    scale = row_scale(middle)
    unit = middle * scale
    normed_ffn = (unit * gains[1:2]).astype(bf16)
    logits_high, logits_low = two_parts(grad_logits)
    gain_high, gain_low = two_parts(grad_normed * unit)
    first = (lane == 1).astype(f32).astype(bf16)
    d_weights[:, MODEL_WIDTH:] = (
        mm(normed_ffn, logits_high, 0, 0)
        + mm(normed_ffn, logits_low, 0, 0)
        + mm(gain_high, first, 0, 0)
        + mm(gain_low, first, 0, 0)
    ).astype(bf16)
    scaled = grad_normed * gains[1:2]
    grad_middle = cotangent + scale * (
        scaled - unit * jnp.mean(scaled * unit, axis=-1, keepdims=True)
    )
    grad_middle_ref[...] = grad_middle
    grad_attended = (live * grad_middle).astype(bf16)
    grad_attended_ref[...] = grad_attended
    d_weights[:, :MODEL_WIDTH] = mm(context_ref[...], grad_attended, 0, 0).astype(bf16)
    width = MODEL_WIDTH + EXTRA
    store_rows(pos, d_weights, kept, sent, rows, planes, range(4), 0, width)


def attend_back(allowed, qkv_ref, stats_ref, grad_context_ref, grads):
    twice = jnp.concatenate([allowed, allowed], axis=0)
    low = iota((ROWS, 128), 1) < HEAD_SIZE
    pairs = []
    for g in range(KEY_VALUE_HEADS):
        queries, keys, values = head_blocks(qkv_ref, g)
        kept = jnp.concatenate(
            [stats_ref[:, 2 * g : 2 * g + 1], stats_ref[:, 2 * g + 1 : 2 * g + 2]], axis=0
        )
        scores = jnp.where(twice > 0, mm(queries, keys, 1, 1) * 0.125, -1e30)
        probs = jnp.exp(scores - kept)
        d_context = halves(grad_context_ref[:, g * 128 : (g + 1) * 128])
        d_probs = mm(d_context, values, 1, 1)
        d_scores = (
            probs * (d_probs - jnp.sum(probs * d_probs, axis=-1, keepdims=True))
        ).astype(bf16)
        grads[:, g * 128 : (g + 1) * 128] = (joined(mm(d_scores, keys)) * 0.125).astype(bf16)
        d_keys = mm(d_scores, queries, 0, 0)
        d_values = mm(probs.astype(bf16), d_context, 0, 0)
        pairs.append([both + pltpu.roll(both, HEAD_SIZE, 1) for both in (d_keys, d_values)])
        if g % 2 == 1:
            at = Q_END + (g // 2) * 128
            d_keys = jnp.where(low, pairs[g - 1][0], pairs[g][0]) * 0.125
            d_values = jnp.where(low, pairs[g - 1][1], pairs[g][1])
            grads[:, at : at + 128] = d_keys.astype(bf16)
            at = at + K_END - Q_END
            grads[:, at : at + 128] = d_values.astype(bf16)


def context_kernel(planes, rows, pos, grad_attended_ref, *refs):
    pieces, out_ref, weights = refs[:8], refs[8], refs[9]
    load_rows(pos, pieces, rows, planes, [(weights, 0, QKV - K_END, MODEL_WIDTH)])
    out_ref[...] = mm(grad_attended_ref[...], weights[...], 1, 1).astype(bf16)


def back_kernel(planes, rows, pos, lens, normed_ref, qkv_ref, stats_ref, grad_context_ref, *refs):
    grads, kept, sent, d_weights = refs
    attend_back(allowed_of(lens).astype(f32), qkv_ref, stats_ref, grad_context_ref, grads)
    d_weights[...] = mm(normed_ref[...], grads[...], 0, 0).astype(bf16)
    store_rows(pos, d_weights, kept, sent, rows, planes, X_FIRST, 0, Q_END)
    kept, sent = kept.at[pl.ds(4, 4)], sent.at[pl.ds(4, 4)]
    store_rows(pos, d_weights, kept, sent, rows, planes, Y_FIRST, Q_END, QKV - Q_END)


def input_kernel(planes, rows, pos, hidden_ref, grad_middle_ref, gains_ref, grads_ref, *refs):
    first, second, grad_in_ref, weights = refs[:8], refs[8:16], refs[16], refs[17]
    load_rows(pos, first, rows, planes, [(weights, 0, 0, K_END)])
    load_rows(pos, second, rows, planes, [(weights, K_END, 0, QKV - K_END)])
    hidden = hidden_ref[...].astype(f32)
    scale = row_scale(hidden)
    unit = hidden * scale
    grad_normed = mm(grads_ref[...], weights[...], 1, 1)
    scaled = grad_normed * gains_ref[0:1, :]
    grad_hidden = grad_middle_ref[...] + scale * (
        scaled - unit * jnp.mean(scaled * unit, axis=-1, keepdims=True)
    )
    grad_in_ref[...] = grad_hidden.astype(bf16)


def owned_kernel(rows_in, rows_out, pos, *refs):
    pieces, in_ref, out_ref = refs[:4], refs[4], refs[5]
    for f in range(4):
        place = pl.ds(pl.multiple_of((pos[1] ^ f) * MODEL_WIDTH, MODEL_WIDTH), MODEL_WIDTH)
        in_ref[:, place] = pieces[f][:rows_in].astype(f32)
        out_ref[:, place] = pieces[f][rows_in:].astype(f32)


def call(kernel, operands, n_scalars, outs, scratch, name, flops=1000):
    here = pl.BlockSpec(memory_space=pltpu.VMEM)
    scalar = pl.BlockSpec(memory_space=pltpu.SMEM)
    return pl.pallas_call(
        kernel,
        out_shape=tuple(outs),
        in_specs=[scalar] * n_scalars + [here] * (len(operands) - n_scalars),
        out_specs=(here,) * len(outs),
        scratch_shapes=scratch,
        compiler_params=pltpu.CompilerParams(vmem_limit_bytes=VMEM_LIMIT),
        cost_estimate=pl.CostEstimate(flops=flops, bytes_accessed=1000, transcendentals=0),
        name=name,
    )(*operands)


def exchanged(
    hidden_in,
    grad_out,
    seq_lens,
    expert_choice,
    gain_attn,
    w_query,
    key_weight,
    value_weight,
    w_attn_out,
    gain_ffn,
    w_router,
    w_expert_in,
    w_expert_out,
):
    n = lax.axis_size("fsdp")
    planes = n // PLANE
    me = lax.axis_index("fsdp")
    plane, chip, core = me // PLANE, (me // 2) % 4, me % 2
    pos = jnp.stack([plane, chip, core]).astype(jnp.int32)
    rows = w_query.shape[0]
    rows_out = w_expert_out.shape[0]
    both = rows + rows_out

    def swap(value, offset):
        return lax.ppermute(value, "fsdp", [(i, i ^ offset) for i in range(n)])

    def after(value, *earlier):
        return lax.optimization_barrier((value, *earlier))[0]

    def array(*shape, dtype=bf16):
        return jax.ShapeDtypeStruct(shape, dtype)

    def summed(*values):
        total = values[0].astype(f32)
        for one in values[1:]:
            total = total + one.astype(f32)
        return total

    def low_sum(*values):
        return summed(*values).astype(bf16)

    def widen(blocks, offset):
        other = swap(blocks, PLANE * offset)
        return jnp.stack([blocks, other], axis=1).reshape((-1,) + blocks.shape[1:])

    def fold(parts, offset, *earlier):
        return low_sum(parts[0::2], after(swap(parts[1::2], PLANE * offset), *earlier))

    def to_chips(parts):
        return [parts[0]] + [swap(parts[f], 2 * f) for f in range(1, 4)]

    def both_cores(pieces):
        return list(pieces) + [swap(one, 1) for one in pieces]

    grad_slots = to_chips(
        call(
            cotangent_kernel,
            (pos, seq_lens, expert_choice, grad_out),
            2,
            [array(CAP, MODEL_WIDTH)] * 4,
            [],
            "slot_cotangents",
        )
    )
    by_expert = jnp.concatenate(
        [
            w_expert_in.reshape(rows, EXPERTS, 2 * FE),
            w_expert_out.reshape(rows_out, EXPERTS, MODEL_WIDTH),
        ],
        axis=0,
    ).transpose(1, 0, 2)
    expert_blocks = jnp.stack(
        to_chips([lax.dynamic_index_in_dim(by_expert, chip ^ f, 0, False) for f in range(4)])
    )[None]

    beside = jnp.concatenate(
        [gain_attn[:, None], gain_ffn[:, None], w_router, jnp.zeros((rows, EXTRA - 6), bf16)], axis=1
    )
    weights = jnp.concatenate([w_query, key_weight, beside, value_weight, w_attn_out], axis=1)[None]
    offset = planes // 2
    while offset:
        weights = widen(weights, offset)
        if offset > 1:
            weights = after(weights, expert_blocks)
        offset = offset // 2
    weights = after(weights, *grad_slots)
    first, second = weights[:, :, : K_END + EXTRA], weights[:, :, K_END + EXTRA :]
    first_x, second_y = swap(first, 2), swap(second, 4)
    first_y, second_x = swap(first, 4), swap(second, 2)
    offset = planes // 2
    expert_blocks = after(expert_blocks, weights)
    while offset > 1:
        expert_blocks = widen(expert_blocks, offset)
        offset = offset // 2
    first_xy = swap(after(first_x, expert_blocks), 4)
    second_xy = swap(after(second_y, expert_blocks), 2)
    first_pieces = both_cores([after(first, first_x, second_y), first_x, first_y, first_xy])
    second_pieces = both_cores([after(second, first_x, second_y), second_x, second_y, second_xy])
    odd_blocks = swap(expert_blocks, PLANE)

    normed, gains, qkv, context, stats = call(
        lambda *refs: attention_kernel(planes, rows, *refs),
        (pos, seq_lens, hidden_in, *first_pieces, *second_pieces),
        2,
        [
            array(ROWS, MODEL_WIDTH),
            array(16, MODEL_WIDTH, dtype=f32),
            array(ROWS, QKV),
            array(ROWS, Q_END),
            array(ROWS, 128, dtype=f32),
        ],
        [pltpu.VMEM((MODEL_WIDTH, QKV + EXTRA), bf16)],
        "attention",
    )
    middle, gates, *dispatched = call(
        lambda *refs: dispatch_kernel(planes, rows, *refs),
        (pos, seq_lens, expert_choice, hidden_in, context, gains, *second_pieces),
        2,
        [array(ROWS, MODEL_WIDTH, dtype=f32), array(ROWS, 128, dtype=f32)]
        + [array(CAP, MODEL_WIDTH + EXTRA)] * 4,
        [pltpu.VMEM((MODEL_WIDTH, MODEL_WIDTH), bf16)],
        "dispatch",
    )
    dispatched = to_chips(dispatched)

    expert_pieces = both_cores([after(expert_blocks, context), after(odd_blocks, middle)])
    slots = EXPERTS * CAP
    *backs, x, activated, d_expert, d_up = call(
        lambda *refs: expert_kernel(planes, rows, rows_out, *refs),
        (pos, *dispatched, *grad_slots, *expert_pieces),
        1,
        [array(2 * CAP, MODEL_WIDTH)] * 4
        + [array(slots, MODEL_WIDTH), array(slots, FE), array(slots, MODEL_WIDTH), array(slots, 2 * FE)],
        [pltpu.VMEM((MODEL_WIDTH, 2 * FE), bf16), pltpu.VMEM((FE, MODEL_WIDTH), bf16)],
        "experts",
    )
    backs = to_chips(backs)
    block_output, grad_middle, grad_attended, kept, sent = call(
        lambda *refs: combine_kernel(planes, rows, *refs),
        (
            pos,
            seq_lens,
            expert_choice,
            middle,
            gates,
            grad_out,
            gains,
            context,
            *backs,
        ),
        2,
        [
            array(ROWS, MODEL_WIDTH),
            array(ROWS, MODEL_WIDTH, dtype=f32),
            array(ROWS, MODEL_WIDTH),
        ]
        + [array(4, planes, rows, MODEL_WIDTH + EXTRA)] * 2,
        [pltpu.VMEM((MODEL_WIDTH, MODEL_WIDTH + EXTRA), bf16)],
        "combine",
    )
    expert_kept, expert_sent = call(
        lambda *refs: expert_weights_kernel(planes, rows, rows_out, *refs),
        (pos, after(x, grad_attended), activated, d_expert, d_up),
        1,
        [array(planes, 4, both, MODEL_WIDTH)] * 2,
        [pltpu.VMEM((MODEL_WIDTH, 2 * FE), bf16), pltpu.VMEM((FE, MODEL_WIDTH), bf16)],
        "expert_weights",
    )
    expert_parts = low_sum(expert_kept, swap(expert_sent, 1))
    (grad_context,) = call(
        lambda *refs: context_kernel(planes, rows, *refs),
        (pos, grad_attended, *second_pieces),
        1,
        [array(ROWS, Q_END)],
        [pltpu.VMEM((MODEL_WIDTH, MODEL_WIDTH), bf16)],
        "context_gradients",
    )
    other = swap(sent, 1)
    out_parts = [low_sum(kept[f], other[f]) for f in range(4)]
    out_sums = to_chips(out_parts)
    grads, kept, sent = call(
        lambda *refs: back_kernel(planes, rows, *refs),
        (pos, seq_lens, after(normed, *out_parts), qkv, stats, grad_context),
        2,
        [array(ROWS, QKV)] + [array(8, planes, rows, QKV // 2)] * 2,
        [pltpu.VMEM((MODEL_WIDTH, QKV), bf16)],
        "attention_back",
        2 * 10**9,
    )
    expert_parts = fold(expert_parts, 1, grads)
    other = swap(sent, 1)
    keep_q, send_q, keep_kv, send_kv = [
        low_sum(kept[i : i + 2], other[i : i + 2]) for i in range(0, 8, 2)
    ]
    from_x = swap(after(send_q, *out_sums), 2)
    from_y = swap(after(send_kv, *out_sums), 4)
    (grad_in,) = call(
        lambda *refs: input_kernel(planes, rows, *refs),
        (
            pos,
            hidden_in,
            grad_middle,
            gains,
            after(grads, send_q, send_kv),
            *first_pieces,
            *second_pieces,
        ),
        1,
        [array(ROWS, MODEL_WIDTH)],
        [pltpu.VMEM((MODEL_WIDTH, QKV), bf16)],
        "input_gradient",
    )
    half_q, half_kv = low_sum(keep_q, from_x), low_sum(keep_kv, from_y)
    rest_q, rest_kv = swap(after(half_q[1], grad_in), 4), swap(after(half_kv[1], grad_in), 2)
    owned_qkv = jnp.concatenate([low_sum(half_q[0], rest_q), low_sum(half_kv[0], rest_kv)], axis=-1)
    owned_out = low_sum(*[after(one, half_q) for one in out_sums])
    owned_out = fold(owned_out, 1, owned_qkv)
    owned_out = fold(owned_out, 2, owned_qkv)
    offset = 2
    while expert_parts.shape[0] > 1:
        expert_parts = fold(expert_parts, offset, rest_kv)
        offset = 2 * offset
    expert_mine = to_chips(expert_parts[0])
    owned_qkv = summed(
        owned_qkv[0], *[swap(owned_qkv[k], PLANE * k) for k in range(1, planes)]
    )
    grad_w_expert_in, grad_w_expert_out = call(
        lambda *refs: owned_kernel(rows, rows_out, *refs),
        (pos, *expert_mine),
        1,
        [
            array(rows, EXPERTS * 2 * FE, dtype=f32),
            array(rows_out, EXPERTS * MODEL_WIDTH, dtype=f32),
        ],
        [],
        "expert_rows",
    )
    owned_out = owned_out[0].astype(f32)
    d_query, d_key, d_value = owned_qkv[:, :Q_END], owned_qkv[:, Q_END:K_END], owned_qkv[:, K_END:]
    d_gain_attn = sum(
        jnp.sum(d * w.astype(f32), axis=1)
        for d, w in ((d_query, w_query), (d_key, key_weight), (d_value, value_weight))
    ) / gain_attn.astype(f32)
    return (
        block_output,
        grad_in,
        d_gain_attn,
        d_query,
        d_key,
        d_value,
        owned_out[:, :MODEL_WIDTH],
        owned_out[:, MODEL_WIDTH + 1],
        owned_out[:, MODEL_WIDTH + 2 : MODEL_WIDTH + 2 + EXPERTS],
        grad_w_expert_in,
        grad_w_expert_out,
    )


def rms_scale(values):
    return lax.rsqrt(jnp.mean(values * values, axis=-1, keepdims=True) + eps)


def layout(lengths, count_of_rows):
    microbatch_count = lengths.shape[0]
    microbatch_rows = count_of_rows // microbatch_count
    first_len = jnp.broadcast_to(lengths[:, 0:1], (microbatch_count, microbatch_rows))
    second_len = jnp.broadcast_to(lengths[:, 1:2], (microbatch_count, microbatch_rows))
    inner_grid = jnp.broadcast_to(
        jnp.arange(microbatch_rows, dtype=jnp.int32)[None, :], (microbatch_count, microbatch_rows)
    )
    section = jnp.where(
        inner_grid < first_len, 0, jnp.where(inner_grid < first_len + second_len, 1, 2)
    )
    allowed = (section[:, :, None] == section[:, None, :]) & (
        inner_grid[:, None, :] <= inner_grid[:, :, None]
    )
    live_rows = (section < 2).astype(jnp.float32).reshape(count_of_rows, 1)
    return (live_rows, allowed)


def routing(choice_ids, capacity):
    count_of_rows, top_count = choice_ids.shape
    expert_ids = jnp.arange(EXPERTS, dtype=jnp.int32)
    expert_hits = (choice_ids[:, :, None] == expert_ids[None, None, :]).astype(jnp.int32)
    per_row = jnp.sum(expert_hits, axis=1)
    before = jnp.cumsum(per_row, axis=0) - per_row
    position = jnp.sum(expert_hits * before[:, None, :], axis=2)
    slot_index = choice_ids * capacity + position
    pair_index = jnp.arange(count_of_rows * top_count, dtype=jnp.int32)
    source = (
        jnp.full((EXPERTS * capacity,), count_of_rows * top_count, jnp.int32)
        .at[slot_index.reshape(-1)]
        .set(pair_index)
    )
    return (expert_hits, slot_index, source)


def shards(
    hidden_in,
    grad_out,
    seq_lens,
    expert_choice,
    gain_attn,
    w_query,
    key_weight,
    value_weight,
    w_attn_out,
    gain_ffn,
    w_router,
    w_expert_in,
    w_expert_out,
):
    count_of_rows = hidden_in.shape[0]
    microbatch_count = seq_lens.shape[0]
    microbatch_rows = count_of_rows // microbatch_count
    query_group_size = QUERY_HEADS // KEY_VALUE_HEADS
    device_count = lax.axis_size("fsdp")
    live_rows, allowed = layout(seq_lens, count_of_rows)
    mask_grid = allowed[:, None, None]
    hidden = hidden_in.astype(jnp.float32)
    cotangent = grad_out.astype(jnp.float32)
    attention_set = (
        lax.all_gather(gain_attn, "fsdp", axis=0, tiled=True),
        lax.all_gather(w_query, "fsdp", axis=0, tiled=True),
        lax.all_gather(key_weight, "fsdp", axis=0, tiled=True),
        lax.all_gather(value_weight, "fsdp", axis=0, tiled=True),
        lax.all_gather(w_attn_out, "fsdp", axis=0, tiled=True),
        lax.all_gather(gain_ffn, "fsdp", axis=0, tiled=True),
        lax.all_gather(w_router, "fsdp", axis=0, tiled=True),
    )
    gain_one = attention_set[0].astype(jnp.float32)
    gain_two = attention_set[5].astype(jnp.float32)
    scale_one = rms_scale(hidden)
    unit_one = hidden * scale_one
    normed = (unit_one * gain_one).astype(jnp.bfloat16)
    query_rows = jnp.dot(normed, attention_set[1], preferred_element_type=jnp.float32).astype(
        jnp.bfloat16
    )
    every_key = jnp.dot(normed, attention_set[2], preferred_element_type=jnp.float32).astype(
        jnp.bfloat16
    )
    every_value = jnp.dot(normed, attention_set[3], preferred_element_type=jnp.float32).astype(
        jnp.bfloat16
    )
    query_tiles = query_rows.reshape(
        microbatch_count, microbatch_rows, KEY_VALUE_HEADS, query_group_size, HEAD_SIZE
    )
    key_tiles = every_key.reshape(microbatch_count, microbatch_rows, KEY_VALUE_HEADS, HEAD_SIZE)
    value_tiles = every_value.reshape(microbatch_count, microbatch_rows, KEY_VALUE_HEADS, HEAD_SIZE)

    def score_block():
        raw_scores = (
            jnp.einsum(
                "mqgrd,mkgd->mgrqk", query_tiles, key_tiles, preferred_element_type=jnp.float32
            )
            * 0.125
        )
        return jnp.where(mask_grid, raw_scores, -1e30)

    scores = score_block()
    top_score = jnp.max(scores, axis=-1, keepdims=True)
    weights = jnp.exp(scores - top_score)
    row_total = jnp.sum(weights, axis=-1, keepdims=True)
    probs_low = (weights / row_total).astype(jnp.bfloat16)
    context = jnp.einsum(
        "mgrqk,mkgd->mqgrd", probs_low, value_tiles, preferred_element_type=jnp.float32
    )
    context = context.reshape(count_of_rows, QUERY_HEADS * HEAD_SIZE).astype(jnp.bfloat16)
    attended = jnp.dot(context, attention_set[4], preferred_element_type=jnp.float32)
    middle = hidden + live_rows * attended
    scale_two = rms_scale(middle)
    unit_two = middle * scale_two
    normed_ffn = (unit_two * gain_two).astype(jnp.bfloat16)
    logits = jnp.dot(normed_ffn, attention_set[6], preferred_element_type=jnp.float32)
    expert_hits, slot_index, source = routing(expert_choice, CAP)
    hits_float = expert_hits.astype(jnp.float32)
    chosen = jnp.sum(hits_float * logits[:, None, :], axis=2)
    chosen_top = jnp.max(chosen, axis=1, keepdims=True)
    gate_exp = jnp.exp(chosen - chosen_top)
    gate_weights = gate_exp / jnp.sum(gate_exp, axis=1, keepdims=True)
    padded = jnp.concatenate([normed_ffn, jnp.zeros((1, MODEL_WIDTH), jnp.bfloat16)], axis=0)
    dispatched = padded[source // TOP].reshape(EXPERTS, CAP, MODEL_WIDTH)
    expert_in_full = lax.all_gather(w_expert_in, "fsdp", axis=0, tiled=True)
    expert_out_full = lax.all_gather(w_expert_out, "fsdp", axis=0, tiled=True)
    in_grid = expert_in_full.reshape(MODEL_WIDTH, EXPERTS, 2 * FE)
    out_grid = expert_out_full.reshape(FE, EXPERTS, MODEL_WIDTH)
    gate_up = jnp.einsum("ecd,def->ecf", dispatched, in_grid, preferred_element_type=jnp.float32)
    gate_part = gate_up[:, :, :FE]
    up_part = gate_up[:, :, FE:]
    sigmoid_gate = lax.logistic(gate_part)
    silu_gate = gate_part * sigmoid_gate
    activated = (silu_gate * up_part).astype(jnp.bfloat16)
    expert_out = jnp.einsum("ecf,fed->ecd", activated, out_grid, preferred_element_type=jnp.float32)
    picked = expert_out.reshape(EXPERTS * CAP, MODEL_WIDTH)[slot_index]
    mixture = jnp.sum(gate_weights[:, :, None] * picked, axis=1)
    block_output = (middle + live_rows * mixture).astype(jnp.bfloat16)
    back_set = (
        lax.all_gather(gain_attn, "fsdp", axis=0, tiled=True),
        lax.all_gather(w_query, "fsdp", axis=0, tiled=True),
        lax.all_gather(key_weight, "fsdp", axis=0, tiled=True),
        lax.all_gather(value_weight, "fsdp", axis=0, tiled=True),
        lax.all_gather(w_attn_out, "fsdp", axis=0, tiled=True),
        lax.all_gather(gain_ffn, "fsdp", axis=0, tiled=True),
        lax.all_gather(w_router, "fsdp", axis=0, tiled=True),
    )
    out_back = lax.all_gather(w_expert_out, "fsdp", axis=0, tiled=True).reshape(
        FE, EXPERTS, MODEL_WIDTH
    )
    in_back = lax.all_gather(w_expert_in, "fsdp", axis=0, tiled=True).reshape(
        MODEL_WIDTH, EXPERTS, 2 * FE
    )
    grad_mix = live_rows * cotangent
    grad_gates = jnp.sum(grad_mix[:, None, :] * picked, axis=2)
    grad_chosen = gate_weights * (
        grad_gates - jnp.sum(gate_weights * grad_gates, axis=1, keepdims=True)
    )
    grad_logits = jnp.sum(grad_chosen[:, :, None] * hits_float, axis=1)
    pair_grads = (gate_weights[:, :, None] * grad_mix[:, None, :]).reshape(
        count_of_rows * TOP, MODEL_WIDTH
    )
    pair_padded = jnp.concatenate([pair_grads, jnp.zeros((1, MODEL_WIDTH), jnp.float32)], axis=0)
    grad_expert_out = pair_padded[source].astype(jnp.bfloat16).reshape(EXPERTS, CAP, MODEL_WIDTH)
    grad_activated = jnp.einsum(
        "ecd,fed->ecf", grad_expert_out, out_back, preferred_element_type=jnp.float32
    )
    out_rows = w_expert_out.shape[0]
    columns = activated
    grad_w_expert_out = lax.psum_scatter(
        jnp.einsum(
            "ecn,ecd->ned", columns, grad_expert_out, preferred_element_type=jnp.float32
        ).reshape(1 * lax.axis_size("fsdp"), out_rows * EXPERTS * MODEL_WIDTH),
        "fsdp",
        scatter_dimension=0,
        tiled=True,
    ).reshape(out_rows, EXPERTS * MODEL_WIDTH)
    grad_gate = grad_activated * up_part * (sigmoid_gate * (1.0 + gate_part * (1.0 - sigmoid_gate)))
    grad_up = grad_activated * silu_gate
    grad_gate_up = jnp.concatenate([grad_gate, grad_up], axis=-1).astype(jnp.bfloat16)
    grad_dispatched = jnp.einsum(
        "ecf,def->ecd", grad_gate_up, in_back, preferred_element_type=jnp.float32
    )
    in_rows = w_expert_in.shape[0]
    columns = dispatched
    grad_w_expert_in = lax.psum_scatter(
        jnp.einsum(
            "ecn,ecf->nef", columns, grad_gate_up, preferred_element_type=jnp.float32
        ).reshape(1 * lax.axis_size("fsdp"), in_rows * EXPERTS * 2 * FE),
        "fsdp",
        scatter_dimension=0,
        tiled=True,
    ).reshape(in_rows, EXPERTS * 2 * FE)
    router_full = back_set[6].astype(jnp.float32)
    grad_normed_ffn = jnp.sum(
        grad_dispatched.reshape(EXPERTS * CAP, MODEL_WIDTH)[slot_index], axis=1
    )
    grad_normed_ffn = grad_normed_ffn + jnp.dot(grad_logits, router_full.T, precision=highest)
    grad_router = jnp.dot(normed_ffn.astype(jnp.float32).T, grad_logits, precision=highest)
    back_gain_two = back_set[5].astype(jnp.float32)
    grad_gain_two = jnp.sum(grad_normed_ffn * unit_two, axis=0)
    scaled_two = grad_normed_ffn * back_gain_two
    grad_middle = cotangent + scale_two * (
        scaled_two - unit_two * jnp.mean(scaled_two * unit_two, axis=-1, keepdims=True)
    )
    grad_attended = (live_rows * grad_middle).astype(jnp.bfloat16)
    grad_out_proj = jnp.einsum(
        "ti,td->id", context, grad_attended, preferred_element_type=jnp.float32
    )
    context_gradient = jnp.einsum(
        "td,id->ti", grad_attended, back_set[4], preferred_element_type=jnp.float32
    ).astype(jnp.bfloat16)
    context_gradient_grid = context_gradient.reshape(
        microbatch_count, microbatch_rows, KEY_VALUE_HEADS, query_group_size, HEAD_SIZE
    )
    probs_again = jnp.exp(score_block() - top_score) / row_total
    probs_again_low = probs_again.astype(jnp.bfloat16)
    grad_probs = jnp.einsum(
        "mqgrd,mkgd->mgrqk", context_gradient_grid, value_tiles, preferred_element_type=jnp.float32
    )
    value_gradient = jnp.einsum(
        "mgrqk,mqgrd->mkgd",
        probs_again_low,
        context_gradient_grid,
        preferred_element_type=jnp.float32,
    )
    grad_scores = probs_again * (
        grad_probs - jnp.sum(probs_again * grad_probs, axis=-1, keepdims=True)
    )
    grad_scores = grad_scores.astype(jnp.bfloat16)
    grad_queries = (
        jnp.einsum("mgrqk,mkgd->mqgrd", grad_scores, key_tiles, preferred_element_type=jnp.float32)
        * 0.125
    )
    grad_queries = grad_queries.reshape(count_of_rows, QUERY_HEADS * HEAD_SIZE).astype(jnp.bfloat16)
    key_gradient = (
        jnp.einsum(
            "mgrqk,mqgrd->mkgd", grad_scores, query_tiles, preferred_element_type=jnp.float32
        )
        * 0.125
    )
    key_gradient = key_gradient.reshape(count_of_rows, KEY_VALUE_HEADS * HEAD_SIZE).astype(
        jnp.bfloat16
    )
    value_gradient_narrow = value_gradient.reshape(
        count_of_rows, KEY_VALUE_HEADS * HEAD_SIZE
    ).astype(jnp.bfloat16)
    grad_query_proj = jnp.einsum(
        "td,ti->di", normed, grad_queries, preferred_element_type=jnp.float32
    )
    grad_key_proj = jnp.einsum(
        "td,ti->di", normed, key_gradient, preferred_element_type=jnp.float32
    )
    grad_value_proj = jnp.einsum(
        "td,ti->di", normed, value_gradient_narrow, preferred_element_type=jnp.float32
    )
    grad_normed = jnp.einsum(
        "ti,di->td", grad_queries, back_set[1], preferred_element_type=jnp.float32
    )
    grad_normed = grad_normed + jnp.einsum(
        "ti,di->td", key_gradient, back_set[2], preferred_element_type=jnp.float32
    )
    grad_normed = grad_normed + jnp.einsum(
        "ti,di->td", value_gradient_narrow, back_set[3], preferred_element_type=jnp.float32
    )
    back_gain_one = back_set[0].astype(jnp.float32)
    grad_gain_one = jnp.sum(grad_normed * unit_one, axis=0)
    scaled_one = grad_normed * back_gain_one
    grad_hidden = grad_middle + scale_one * (
        scaled_one - unit_one * jnp.mean(scaled_one * unit_one, axis=-1, keepdims=True)
    )
    terms = (
        grad_gain_one,
        grad_query_proj,
        grad_key_proj,
        grad_value_proj,
        grad_out_proj,
        grad_gain_two,
        grad_router,
    )
    local_shapes = (
        gain_attn.shape,
        w_query.shape,
        key_weight.shape,
        value_weight.shape,
        w_attn_out.shape,
        gain_ffn.shape,
        w_router.shape,
    )
    flat_terms = tuple((term.reshape(device_count, -1) for term in terms))
    owned = (
        lax.psum_scatter(flat_terms[0], "fsdp", scatter_dimension=0, tiled=True),
        lax.psum_scatter(flat_terms[1], "fsdp", scatter_dimension=0, tiled=True),
        lax.psum_scatter(flat_terms[2], "fsdp", scatter_dimension=0, tiled=True),
        lax.psum_scatter(flat_terms[3], "fsdp", scatter_dimension=0, tiled=True),
        lax.psum_scatter(flat_terms[4], "fsdp", scatter_dimension=0, tiled=True),
        lax.psum_scatter(flat_terms[5], "fsdp", scatter_dimension=0, tiled=True),
        lax.psum_scatter(flat_terms[6], "fsdp", scatter_dimension=0, tiled=True),
    )
    owned = tuple((piece.reshape(shape) for piece, shape in zip(owned, local_shapes)))
    return (
        block_output,
        grad_hidden.astype(jnp.bfloat16),
        owned[0],
        owned[1],
        owned[2],
        owned[3],
        owned[4],
        owned[5],
        owned[6],
        grad_w_expert_in,
        grad_w_expert_out,
    )


def solution(mesh):
    placed = (
        P("fsdp", None),
        P("fsdp", None),
        P("fsdp", None),
        P("fsdp", None),
        P("fsdp"),
        P("fsdp", None),
        P("fsdp", None),
        P("fsdp", None),
        P("fsdp", None),
        P("fsdp"),
        P("fsdp", None),
        P("fsdp", None),
        P("fsdp", None),
    )
    devices = mesh.shape["fsdp"]
    planes = devices // PLANE
    whole = devices % PLANE == 0 and planes > 1 and planes & (planes - 1) == 0 and FE % (16 * devices) == 0
    return jax.shard_map(
        exchanged if whole else shards,
        mesh=mesh,
        in_specs=placed,
        out_specs=(
            P("fsdp", None),
            P("fsdp", None),
            P("fsdp"),
            P("fsdp", None),
            P("fsdp", None),
            P("fsdp", None),
            P("fsdp", None),
            P("fsdp"),
            P("fsdp", None),
            P("fsdp", None),
            P("fsdp", None),
        ),
        check_vma=False,
    )
```

```python
import jax
import jax.numpy as jnp
from jax import lax
from jax.experimental import pallas as pl
from jax.experimental.pallas import tpu as pltpu
from jax.sharding import PartitionSpec as P

MODEL_WIDTH = 1024
QUERY_HEADS = 16
KEY_VALUE_HEADS = 8
HEAD_SIZE = 64
FE = 512
EXPERTS = 4
TOP = 2
CAP = 80

ROWS = 128
STRIDE = 96
SLOTS = EXPERTS * STRIDE
Q_END = QUERY_HEADS * HEAD_SIZE
K_END = Q_END + KEY_VALUE_HEADS * HEAD_SIZE
QKV = K_END + KEY_VALUE_HEADS * HEAD_SIZE
EXTRA = 128
X_FIRST, Y_FIRST = (0, 2, 1, 3), (0, 1, 2, 3)
PLANE = 8
f32 = jnp.float32
bf16 = jnp.bfloat16

eps = 1e-06
highest = lax.Precision.HIGHEST
VMEM_LIMIT = 44 * 1024 * 1024


def mm(left, right, left_dim=1, right_dim=0):
    return lax.dot_general(
        left, right, (((left_dim,), (right_dim,)), ((), ())), preferred_element_type=f32
    )


def two_parts(values):
    high = values.astype(bf16)
    return high, (values - high.astype(f32)).astype(bf16)


def iota(shape, dim):
    return lax.broadcasted_iota(jnp.int32, shape, dim)


def row_scale(values):
    return lax.rsqrt(jnp.mean(values * values, axis=-1, keepdims=True) + eps)


def section_of(lens, place):
    batch = place >> 6
    inner = place & 63
    first = jnp.where(batch == 0, lens[0, 0], lens[1, 0])
    total = first + jnp.where(batch == 0, lens[0, 1], lens[1, 1])
    part = jnp.where(inner < first, 0, jnp.where(inner < total, 1, 2))
    return batch, part


def live_of(lens):
    _, part = section_of(lens, iota((ROWS, 1), 0))
    return (part < 2).astype(f32)


def allowed_of(lens):
    row, column = iota((ROWS, 1), 0), iota((1, ROWS), 1)
    row_batch, row_part = section_of(lens, row)
    column_batch, column_part = section_of(lens, column)
    return (
        (row_batch * 4 + row_part) == (column_batch * 4 + column_part)
    ) & (column <= row)


def slots_of(choice, mine):
    lane = iota((ROWS, 128), 1)
    named = [choice[:, k : k + 1] ^ mine for k in range(TOP)]
    hits = jnp.zeros((ROWS, 128), f32)
    for one in named:
        hits = hits + (lane == one).astype(f32)
    earlier = (iota((ROWS, ROWS), 1) < iota((ROWS, ROWS), 0)).astype(bf16)
    before = mm(earlier, hits.astype(bf16))
    places = []
    for one in named:
        position = jnp.sum(jnp.where(lane == one, before, 0.0), axis=1, keepdims=True)
        slot = one * STRIDE + position.astype(jnp.int32)
        places.append((iota((ROWS, SLOTS), 1) == slot).astype(f32).astype(bf16))
    return named, places


def owner(pos, planes_off, chip_off, core_off):
    return ((pos[0] ^ planes_off) * 4 + (pos[1] ^ chip_off)) * 2 + (pos[2] ^ core_off)


def load_rows(pos, pieces, rows, planes, moves):
    for core in range(2):
        for chip in range(4):
            for k in range(planes):
                place = pl.multiple_of(owner(pos, k, chip, core) * rows, rows)
                for buffer, to, at, width in moves:
                    buffer[pl.ds(place, rows), to : to + width] = pieces[core * 4 + chip][
                        k, :, at : at + width
                    ]


def store_rows(pos, buffer, kept, sent, rows, planes, order, at, width):
    for core, target in ((0, kept), (1, sent)):
        for i, chip in enumerate(order):
            for k in range(planes):
                place = pl.multiple_of(owner(pos, k, chip, core) * rows, rows)
                target[i, k] = buffer[pl.ds(place, rows), at : at + width]


def cotangent_kernel(pos, lens, choice_ref, grad_ref, *outs):
    _, places = slots_of(choice_ref[...], pos[1])
    grad_mix = (live_of(lens) * grad_ref[...].astype(f32)).astype(bf16)
    slotted = mm(places[0] + places[1], grad_mix, 0, 0)
    for f in range(EXPERTS):
        outs[f][...] = slotted[f * STRIDE : f * STRIDE + CAP].astype(bf16)


def halves(block):
    low = iota(block.shape, 1) < HEAD_SIZE
    wide = block.astype(f32)
    return jnp.concatenate(
        [jnp.where(low, wide, 0.0), jnp.where(low, 0.0, wide)], axis=0
    ).astype(bf16)


def joined(both):
    upper, lower = both[:ROWS], both[ROWS:]
    return jnp.where(iota(upper.shape, 1) < HEAD_SIZE, upper, lower)


def doubled(pair, g):
    wide = pair.astype(f32)
    turned = pltpu.roll(wide, HEAD_SIZE, 1)
    low = iota(wide.shape, 1) < HEAD_SIZE
    first, second = (wide, turned) if g % 2 == 0 else (turned, wide)
    return jnp.where(low, first, second).astype(bf16)


def head_blocks(qkv_ref, g):
    pair = (g // 2) * 128
    queries = halves(qkv_ref[:, g * 128 : (g + 1) * 128])
    keys = doubled(qkv_ref[:, Q_END + pair : Q_END + pair + 128], g)
    values = doubled(qkv_ref[:, K_END + pair : K_END + pair + 128], g)
    return queries, keys, values


def attention_kernel(planes, rows, pos, lens, hidden_ref, *refs):
    first, second = refs[:8], refs[8:16]
    normed_ref, gains_ref, qkv_ref, context_ref, stats_ref, weights = refs[16:]
    load_rows(pos, first, rows, planes, [(weights, 0, 0, K_END), (weights, QKV, K_END, EXTRA)])
    load_rows(pos, second, rows, planes, [(weights, K_END, 0, QKV - K_END)])
    hidden = hidden_ref[...].astype(f32)
    unit = hidden * row_scale(hidden)
    pick = (iota((16, EXTRA), 0) == iota((16, EXTRA), 1)).astype(f32).astype(bf16)
    gains = mm(pick, weights[:, QKV:], 1, 1)
    gains_ref[...] = gains
    normed = (unit * gains[0:1]).astype(bf16)
    normed_ref[...] = normed
    for at in range(0, QKV, 512):
        qkv_ref[:, at : at + 512] = mm(normed, weights[:, at : at + 512]).astype(bf16)
    allowed = allowed_of(lens).astype(f32)
    twice = jnp.concatenate([allowed, allowed], axis=0)
    lane = iota((ROWS, 128), 1)
    stats = jnp.zeros((ROWS, 128), f32)
    for g in range(KEY_VALUE_HEADS):
        queries, keys, values = head_blocks(qkv_ref, g)
        scores = jnp.where(twice > 0, mm(queries, keys, 1, 1) * 0.125, -1e30)
        top = jnp.max(scores, axis=-1, keepdims=True)
        exps = jnp.exp(scores - top)
        total = jnp.sum(exps, axis=-1, keepdims=True)
        probs = (exps * (1.0 / total)).astype(bf16)
        context_ref[:, g * 128 : (g + 1) * 128] = joined(mm(probs, values)).astype(bf16)
        kept = top + jnp.log(total)
        stats = jnp.where(lane == 2 * g, kept[:ROWS], stats)
        stats = jnp.where(lane == 2 * g + 1, kept[ROWS:], stats)
    stats_ref[...] = stats


def router_gates(named, normed_ffn, gains):
    logits = mm(normed_ffn, gains.astype(bf16), 1, 1)
    chosen = []
    for one in named:
        value = jnp.zeros((ROWS, 1), f32)
        for k in range(EXPERTS):
            value = value + jnp.where(one == k, logits[:, 2 + k : 3 + k], 0.0)
        chosen.append(value)
    top = jnp.maximum(chosen[0], chosen[1])
    exps = [jnp.exp(value - top) for value in chosen]
    total = exps[0] + exps[1]
    return [value / total for value in exps]


def dispatch_kernel(planes, rows, pos, lens, choice_ref, hidden_ref, context_ref, gains_ref, *refs):
    pieces = refs[:8]
    middle_ref, gates_ref = refs[8:10]
    outs = refs[10:14]
    (weights,) = refs[14:]
    load_rows(pos, pieces, rows, planes, [(weights, 0, QKV - K_END, MODEL_WIDTH)])
    choice = choice_ref[...]
    _, places = slots_of(choice, pos[1])
    attended = mm(context_ref[...], weights[...])
    middle = hidden_ref[...].astype(f32) + live_of(lens) * attended
    middle_ref[...] = middle
    gains = gains_ref[...]
    normed_ffn = (middle * row_scale(middle) * gains[1:2]).astype(bf16)
    gates = router_gates([choice[:, k : k + 1] for k in range(TOP)], normed_ffn, gains)
    lane = iota((ROWS, 128), 1)
    gates_ref[...] = jnp.where(lane == 0, gates[0], jnp.where(lane == 1, gates[1], 0.0))
    slotted = mm(places[0] + places[1], normed_ffn, 0, 0)
    beside = jnp.zeros((SLOTS, EXTRA), f32)
    for place, gate in zip(places, gates):
        high, low = two_parts(gate)
        columns = jnp.where(
            lane == 0, high.astype(f32), jnp.where(lane == 1, low.astype(f32), 0.0)
        ).astype(bf16)
        beside = beside + mm(place, columns, 0, 0)
    for f in range(EXPERTS):
        part = slice(f * STRIDE, f * STRIDE + CAP)
        outs[f][:, :MODEL_WIDTH] = slotted[part].astype(bf16)
        outs[f][:, MODEL_WIDTH:] = beside[part].astype(bf16)


def expert_places(pos, planes, rows_in, rows_out):
    places = []
    for core in range(2):
        for k in range(planes):
            for chip in range(4):
                who = owner(pos, k, chip, core)
                in_rows = pl.ds(pl.multiple_of(who * rows_in, rows_in), rows_in)
                out_rows = pl.ds(pl.multiple_of(who * rows_out, rows_out), rows_out)
                places.append((core, k, chip, in_rows, out_rows))
    return places


def expert_kernel(planes, rows_in, rows_out, pos, *refs):
    tokens, grads, pieces = refs[:4], refs[4:8], refs[8:12]
    refs = refs[12:]
    backs = refs[:4]
    x_ref, activated_ref, d_expert_ref, d_up_ref = refs[4:8]
    w_in, w_out = refs[8:]
    for core, k, chip, in_rows, out_rows in expert_places(pos, planes, rows_in, rows_out):
        source = pieces[core * 2 + k % 2]
        w_in[in_rows] = source[k // 2, chip, :rows_in]
        w_out[out_rows] = source[k // 2, chip, rows_in:]
    for f in range(EXPERTS):
        part = slice(f * CAP, (f + 1) * CAP)
        x_ref[part] = tokens[f][:, :MODEL_WIDTH]
        gate_slots = tokens[f][:, MODEL_WIDTH : MODEL_WIDTH + 1].astype(f32) + tokens[f][
            :, MODEL_WIDTH + 1 : MODEL_WIDTH + 2
        ].astype(f32)
        d_expert_ref[part] = (gate_slots * grads[f][...].astype(f32)).astype(bf16)
    x = x_ref[...]
    gate = mm(x, w_in[:, :FE])
    up = mm(x, w_in[:, FE:])
    sig = 1.0 / (1.0 + jnp.exp(-gate))
    silu = gate * sig
    activated = (silu * up).astype(bf16)
    activated_ref[...] = activated
    expert_out = mm(activated, w_out[...]).astype(bf16)
    d_act = mm(d_expert_ref[...], w_out[...], 1, 1)
    d_up_ref[:, :FE] = (d_act * up * (sig * (1.0 + gate * (1.0 - sig)))).astype(bf16)
    d_up_ref[:, FE:] = (d_act * silu).astype(bf16)
    d_x = mm(d_up_ref[...], w_in[...], 1, 1).astype(bf16)
    for f in range(EXPERTS):
        part = slice(f * CAP, (f + 1) * CAP)
        backs[f][:CAP] = expert_out[part]
        backs[f][CAP:] = d_x[part]


def expert_weights_kernel(planes, rows_in, rows_out, pos, x_ref, activated_ref, d_expert_ref, d_up_ref, *refs):
    kept, sent, d_in, d_out = refs
    d_out[...] = mm(activated_ref[...], d_expert_ref[...], 0, 0).astype(bf16)
    d_in[...] = mm(x_ref[...], d_up_ref[...], 0, 0).astype(bf16)
    for core, k, chip, in_rows, out_rows in expert_places(pos, planes, rows_in, rows_out):
        target = kept if core == 0 else sent
        target[k, chip, :rows_in] = d_in[in_rows]
        target[k, chip, rows_in:] = d_out[out_rows]


def combine_kernel(
    planes, rows, pos, lens, choice_ref, middle_ref, gates_ref, grad_ref, gains_ref, context_ref, *refs
):
    backs = refs[:4]
    out_ref, grad_middle_ref, grad_attended_ref, kept, sent = refs[4:9]
    (d_weights,) = refs[9:]
    choice = choice_ref[...]
    _, places = slots_of(choice, pos[1])
    live = live_of(lens)
    empty = jnp.zeros((STRIDE - CAP, MODEL_WIDTH), bf16)
    outs, grads = [], []
    for back in backs:
        outs += [back[:CAP], empty]
        grads += [back[CAP:], empty]
    outs = jnp.concatenate(outs, axis=0)
    grads = jnp.concatenate(grads, axis=0)
    picked = [mm(place, outs) for place in places]
    gates = [gates_ref[:, k : k + 1] for k in range(TOP)]
    middle = middle_ref[...]
    mixture = gates[0] * picked[0] + gates[1] * picked[1]
    out_ref[...] = (middle + live * mixture).astype(bf16)
    cotangent = grad_ref[...].astype(f32)
    grad_mix = live * cotangent
    grad_gates = [jnp.sum(grad_mix * one, axis=1, keepdims=True) for one in picked]
    total = gates[0] * grad_gates[0] + gates[1] * grad_gates[1]
    grad_chosen = [gate * (grad - total) for gate, grad in zip(gates, grad_gates)]
    gains = gains_ref[...]
    grad_normed = mm(places[0] + places[1], grads)
    lane = iota((ROWS, EXTRA), 1)
    grad_logits = jnp.zeros((ROWS, EXTRA), f32)
    for k in range(EXPERTS):
        one = jnp.zeros((ROWS, 1), f32)
        for choice_at in range(TOP):
            one = one + jnp.where(choice[:, choice_at : choice_at + 1] == k, grad_chosen[choice_at], 0.0)
        grad_normed = grad_normed + one * gains[2 + k : 3 + k]
        grad_logits = jnp.where(lane == 2 + k, one, grad_logits)
    scale = row_scale(middle)
    unit = middle * scale
    normed_ffn = (unit * gains[1:2]).astype(bf16)
    logits_high, logits_low = two_parts(grad_logits)
    gain_high, gain_low = two_parts(grad_normed * unit)
    first = (lane == 1).astype(f32).astype(bf16)
    d_weights[:, MODEL_WIDTH:] = (
        mm(normed_ffn, logits_high, 0, 0)
        + mm(normed_ffn, logits_low, 0, 0)
        + mm(gain_high, first, 0, 0)
        + mm(gain_low, first, 0, 0)
    ).astype(bf16)
    scaled = grad_normed * gains[1:2]
    grad_middle = cotangent + scale * (
        scaled - unit * jnp.mean(scaled * unit, axis=-1, keepdims=True)
    )
    grad_middle_ref[...] = grad_middle
    grad_attended = (live * grad_middle).astype(bf16)
    grad_attended_ref[...] = grad_attended
    d_weights[:, :MODEL_WIDTH] = mm(context_ref[...], grad_attended, 0, 0).astype(bf16)
    width = MODEL_WIDTH + EXTRA
    store_rows(pos, d_weights, kept, sent, rows, planes, range(4), 0, width)


def attend_back(allowed, qkv_ref, stats_ref, grad_context_ref, grads):
    twice = jnp.concatenate([allowed, allowed], axis=0)
    low = iota((ROWS, 128), 1) < HEAD_SIZE
    pairs = []
    for g in range(KEY_VALUE_HEADS):
        queries, keys, values = head_blocks(qkv_ref, g)
        kept = jnp.concatenate(
            [stats_ref[:, 2 * g : 2 * g + 1], stats_ref[:, 2 * g + 1 : 2 * g + 2]], axis=0
        )
        scores = jnp.where(twice > 0, mm(queries, keys, 1, 1) * 0.125, -1e30)
        probs = jnp.exp(scores - kept)
        d_context = halves(grad_context_ref[:, g * 128 : (g + 1) * 128])
        d_probs = mm(d_context, values, 1, 1)
        d_scores = (
            probs * (d_probs - jnp.sum(probs * d_probs, axis=-1, keepdims=True))
        ).astype(bf16)
        grads[:, g * 128 : (g + 1) * 128] = (joined(mm(d_scores, keys)) * 0.125).astype(bf16)
        d_keys = mm(d_scores, queries, 0, 0)
        d_values = mm(probs.astype(bf16), d_context, 0, 0)
        pairs.append([both + pltpu.roll(both, HEAD_SIZE, 1) for both in (d_keys, d_values)])
        if g % 2 == 1:
            at = Q_END + (g // 2) * 128
            d_keys = jnp.where(low, pairs[g - 1][0], pairs[g][0]) * 0.125
            d_values = jnp.where(low, pairs[g - 1][1], pairs[g][1])
            grads[:, at : at + 128] = d_keys.astype(bf16)
            at = at + K_END - Q_END
            grads[:, at : at + 128] = d_values.astype(bf16)


def context_kernel(planes, rows, pos, grad_attended_ref, *refs):
    pieces, out_ref, weights = refs[:8], refs[8], refs[9]
    load_rows(pos, pieces, rows, planes, [(weights, 0, QKV - K_END, MODEL_WIDTH)])
    out_ref[...] = mm(grad_attended_ref[...], weights[...], 1, 1).astype(bf16)


def back_kernel(planes, rows, pos, lens, normed_ref, qkv_ref, stats_ref, grad_context_ref, *refs):
    grads, kept, sent, d_weights = refs
    attend_back(allowed_of(lens).astype(f32), qkv_ref, stats_ref, grad_context_ref, grads)
    d_weights[...] = mm(normed_ref[...], grads[...], 0, 0).astype(bf16)
    store_rows(pos, d_weights, kept, sent, rows, planes, X_FIRST, 0, Q_END)
    kept, sent = kept.at[pl.ds(4, 4)], sent.at[pl.ds(4, 4)]
    store_rows(pos, d_weights, kept, sent, rows, planes, Y_FIRST, Q_END, QKV - Q_END)


def input_kernel(planes, rows, pos, hidden_ref, grad_middle_ref, gains_ref, grads_ref, *refs):
    first, second, grad_in_ref, weights = refs[:8], refs[8:16], refs[16], refs[17]
    load_rows(pos, first, rows, planes, [(weights, 0, 0, K_END)])
    load_rows(pos, second, rows, planes, [(weights, K_END, 0, QKV - K_END)])
    hidden = hidden_ref[...].astype(f32)
    scale = row_scale(hidden)
    unit = hidden * scale
    grad_normed = mm(grads_ref[...], weights[...], 1, 1)
    scaled = grad_normed * gains_ref[0:1, :]
    grad_hidden = grad_middle_ref[...] + scale * (
        scaled - unit * jnp.mean(scaled * unit, axis=-1, keepdims=True)
    )
    grad_in_ref[...] = grad_hidden.astype(bf16)


def owned_kernel(rows_in, rows_out, pos, *refs):
    pieces, in_ref, out_ref = refs[:4], refs[4], refs[5]
    for f in range(4):
        place = pl.ds(pl.multiple_of((pos[1] ^ f) * MODEL_WIDTH, MODEL_WIDTH), MODEL_WIDTH)
        in_ref[:, place] = pieces[f][:rows_in].astype(f32)
        out_ref[:, place] = pieces[f][rows_in:].astype(f32)


def call(kernel, operands, n_scalars, outs, scratch, name, flops=1000):
    here = pl.BlockSpec(memory_space=pltpu.VMEM)
    scalar = pl.BlockSpec(memory_space=pltpu.SMEM)
    return pl.pallas_call(
        kernel,
        out_shape=tuple(outs),
        in_specs=[scalar] * n_scalars + [here] * (len(operands) - n_scalars),
        out_specs=(here,) * len(outs),
        scratch_shapes=scratch,
        compiler_params=pltpu.CompilerParams(vmem_limit_bytes=VMEM_LIMIT),
        cost_estimate=pl.CostEstimate(flops=flops, bytes_accessed=1000, transcendentals=0),
        name=name,
    )(*operands)


def exchanged(
    hidden_in,
    grad_out,
    seq_lens,
    expert_choice,
    gain_attn,
    w_query,
    key_weight,
    value_weight,
    w_attn_out,
    gain_ffn,
    w_router,
    w_expert_in,
    w_expert_out,
):
    n = lax.axis_size("fsdp")
    planes = n // PLANE
    me = lax.axis_index("fsdp")
    plane, chip, core = me // PLANE, (me // 2) % 4, me % 2
    pos = jnp.stack([plane, chip, core]).astype(jnp.int32)
    rows = w_query.shape[0]
    rows_out = w_expert_out.shape[0]
    both = rows + rows_out

    def swap(value, offset):
        return lax.ppermute(value, "fsdp", [(i, i ^ offset) for i in range(n)])

    def after(value, *earlier):
        return lax.optimization_barrier((value, *earlier))[0]

    def array(*shape, dtype=bf16):
        return jax.ShapeDtypeStruct(shape, dtype)

    def summed(*values):
        total = values[0].astype(f32)
        for one in values[1:]:
            total = total + one.astype(f32)
        return total

    def low_sum(*values):
        return summed(*values).astype(bf16)

    def widen(blocks, offset):
        other = swap(blocks, PLANE * offset)
        return jnp.stack([blocks, other], axis=1).reshape((-1,) + blocks.shape[1:])

    def fold(parts, offset, *earlier):
        return low_sum(parts[0::2], after(swap(parts[1::2], PLANE * offset), *earlier))

    def to_chips(parts):
        return [parts[0]] + [swap(parts[f], 2 * f) for f in range(1, 4)]

    def both_cores(pieces):
        return list(pieces) + [swap(one, 1) for one in pieces]

    grad_slots = to_chips(
        call(
            cotangent_kernel,
            (pos, seq_lens, expert_choice, grad_out),
            2,
            [array(CAP, MODEL_WIDTH)] * 4,
            [],
            "slot_cotangents",
        )
    )
    by_expert = jnp.concatenate(
        [
            w_expert_in.reshape(rows, EXPERTS, 2 * FE),
            w_expert_out.reshape(rows_out, EXPERTS, MODEL_WIDTH),
        ],
        axis=0,
    ).transpose(1, 0, 2)
    expert_blocks = jnp.stack(
        to_chips([lax.dynamic_index_in_dim(by_expert, chip ^ f, 0, False) for f in range(4)])
    )[None]

    beside = jnp.concatenate(
        [gain_attn[:, None], gain_ffn[:, None], w_router, jnp.zeros((rows, EXTRA - 6), bf16)], axis=1
    )
    weights = jnp.concatenate([w_query, key_weight, beside, value_weight, w_attn_out], axis=1)[None]
    offset = planes // 2
    while offset:
        weights = widen(weights, offset)
        if offset > 1:
            weights = after(weights, expert_blocks)
        offset = offset // 2
    weights = after(weights, *grad_slots)
    first, second = weights[:, :, : K_END + EXTRA], weights[:, :, K_END + EXTRA :]
    first_x, second_y = swap(first, 2), swap(second, 4)
    first_y, second_x = swap(first, 4), swap(second, 2)
    offset = planes // 2
    expert_blocks = after(expert_blocks, weights)
    while offset > 1:
        expert_blocks = widen(expert_blocks, offset)
        offset = offset // 2
    first_xy = swap(after(first_x, expert_blocks), 4)
    second_xy = swap(after(second_y, expert_blocks), 2)
    first_pieces = both_cores([after(first, first_x, second_y), first_x, first_y, first_xy])
    second_pieces = both_cores([after(second, first_x, second_y), second_x, second_y, second_xy])
    odd_blocks = swap(expert_blocks, PLANE)

    normed, gains, qkv, context, stats = call(
        lambda *refs: attention_kernel(planes, rows, *refs),
        (pos, seq_lens, hidden_in, *first_pieces, *second_pieces),
        2,
        [
            array(ROWS, MODEL_WIDTH),
            array(16, MODEL_WIDTH, dtype=f32),
            array(ROWS, QKV),
            array(ROWS, Q_END),
            array(ROWS, 128, dtype=f32),
        ],
        [pltpu.VMEM((MODEL_WIDTH, QKV + EXTRA), bf16)],
        "attention",
    )
    middle, gates, *dispatched = call(
        lambda *refs: dispatch_kernel(planes, rows, *refs),
        (pos, seq_lens, expert_choice, hidden_in, context, gains, *second_pieces),
        2,
        [array(ROWS, MODEL_WIDTH, dtype=f32), array(ROWS, 128, dtype=f32)]
        + [array(CAP, MODEL_WIDTH + EXTRA)] * 4,
        [pltpu.VMEM((MODEL_WIDTH, MODEL_WIDTH), bf16)],
        "dispatch",
    )
    dispatched = to_chips(dispatched)

    expert_pieces = both_cores([after(expert_blocks, context), after(odd_blocks, middle)])
    slots = EXPERTS * CAP
    *backs, x, activated, d_expert, d_up = call(
        lambda *refs: expert_kernel(planes, rows, rows_out, *refs),
        (pos, *dispatched, *grad_slots, *expert_pieces),
        1,
        [array(2 * CAP, MODEL_WIDTH)] * 4
        + [array(slots, MODEL_WIDTH), array(slots, FE), array(slots, MODEL_WIDTH), array(slots, 2 * FE)],
        [pltpu.VMEM((MODEL_WIDTH, 2 * FE), bf16), pltpu.VMEM((FE, MODEL_WIDTH), bf16)],
        "experts",
    )
    backs = to_chips(backs)
    block_output, grad_middle, grad_attended, kept, sent = call(
        lambda *refs: combine_kernel(planes, rows, *refs),
        (
            pos,
            seq_lens,
            expert_choice,
            middle,
            gates,
            grad_out,
            gains,
            context,
            *backs,
        ),
        2,
        [
            array(ROWS, MODEL_WIDTH),
            array(ROWS, MODEL_WIDTH, dtype=f32),
            array(ROWS, MODEL_WIDTH),
        ]
        + [array(4, planes, rows, MODEL_WIDTH + EXTRA)] * 2,
        [pltpu.VMEM((MODEL_WIDTH, MODEL_WIDTH + EXTRA), bf16)],
        "combine",
    )
    expert_kept, expert_sent = call(
        lambda *refs: expert_weights_kernel(planes, rows, rows_out, *refs),
        (pos, after(x, grad_attended), activated, d_expert, d_up),
        1,
        [array(planes, 4, both, MODEL_WIDTH)] * 2,
        [pltpu.VMEM((MODEL_WIDTH, 2 * FE), bf16), pltpu.VMEM((FE, MODEL_WIDTH), bf16)],
        "expert_weights",
    )
    expert_parts = low_sum(expert_kept, swap(expert_sent, 1))
    (grad_context,) = call(
        lambda *refs: context_kernel(planes, rows, *refs),
        (pos, grad_attended, *second_pieces),
        1,
        [array(ROWS, Q_END)],
        [pltpu.VMEM((MODEL_WIDTH, MODEL_WIDTH), bf16)],
        "context_gradients",
    )
    other = swap(sent, 1)
    out_parts = [low_sum(kept[f], other[f]) for f in range(4)]
    out_sums = to_chips(out_parts)
    grads, kept, sent = call(
        lambda *refs: back_kernel(planes, rows, *refs),
        (pos, seq_lens, after(normed, *out_parts), qkv, stats, grad_context),
        2,
        [array(ROWS, QKV)] + [array(8, planes, rows, QKV // 2)] * 2,
        [pltpu.VMEM((MODEL_WIDTH, QKV), bf16)],
        "attention_back",
        2 * 10**9,
    )
    expert_parts = fold(expert_parts, 1)
    other = swap(sent, 1)
    keep_q, send_q, keep_kv, send_kv = [
        low_sum(kept[i : i + 2], other[i : i + 2]) for i in range(0, 8, 2)
    ]
    from_x = swap(after(send_q, *out_sums), 2)
    from_y = swap(after(send_kv, *out_sums), 4)
    (grad_in,) = call(
        lambda *refs: input_kernel(planes, rows, *refs),
        (
            pos,
            hidden_in,
            grad_middle,
            gains,
            after(grads, send_q, send_kv),
            *first_pieces,
            *second_pieces,
        ),
        1,
        [array(ROWS, MODEL_WIDTH)],
        [pltpu.VMEM((MODEL_WIDTH, QKV), bf16)],
        "input_gradient",
    )
    half_q, half_kv = low_sum(keep_q, from_x), low_sum(keep_kv, from_y)
    rest_q, rest_kv = swap(after(half_q[1], grad_in), 4), swap(after(half_kv[1], grad_in), 2)
    owned_qkv = jnp.concatenate([low_sum(half_q[0], rest_q), low_sum(half_kv[0], rest_kv)], axis=-1)
    owned_out = low_sum(*[after(one, half_q) for one in out_sums])
    owned_out = fold(owned_out, 1, owned_qkv)
    owned_out = fold(owned_out, 2, owned_qkv)
    offset = 2
    while expert_parts.shape[0] > 1:
        expert_parts = fold(expert_parts, offset, rest_kv)
        offset = 2 * offset
    expert_mine = to_chips(expert_parts[0])
    owned_qkv = summed(
        owned_qkv[0], *[swap(owned_qkv[k], PLANE * k) for k in range(1, planes)]
    )
    grad_w_expert_in, grad_w_expert_out = call(
        lambda *refs: owned_kernel(rows, rows_out, *refs),
        (pos, *expert_mine),
        1,
        [
            array(rows, EXPERTS * 2 * FE, dtype=f32),
            array(rows_out, EXPERTS * MODEL_WIDTH, dtype=f32),
        ],
        [],
        "expert_rows",
    )
    owned_out = owned_out[0].astype(f32)
    d_query, d_key, d_value = owned_qkv[:, :Q_END], owned_qkv[:, Q_END:K_END], owned_qkv[:, K_END:]
    d_gain_attn = sum(
        jnp.sum(d * w.astype(f32), axis=1)
        for d, w in ((d_query, w_query), (d_key, key_weight), (d_value, value_weight))
    ) / gain_attn.astype(f32)
    return (
        block_output,
        grad_in,
        d_gain_attn,
        d_query,
        d_key,
        d_value,
        owned_out[:, :MODEL_WIDTH],
        owned_out[:, MODEL_WIDTH + 1],
        owned_out[:, MODEL_WIDTH + 2 : MODEL_WIDTH + 2 + EXPERTS],
        grad_w_expert_in,
        grad_w_expert_out,
    )


def rms_scale(values):
    return lax.rsqrt(jnp.mean(values * values, axis=-1, keepdims=True) + eps)


def layout(lengths, count_of_rows):
    microbatch_count = lengths.shape[0]
    microbatch_rows = count_of_rows // microbatch_count
    first_len = jnp.broadcast_to(lengths[:, 0:1], (microbatch_count, microbatch_rows))
    second_len = jnp.broadcast_to(lengths[:, 1:2], (microbatch_count, microbatch_rows))
    inner_grid = jnp.broadcast_to(
        jnp.arange(microbatch_rows, dtype=jnp.int32)[None, :], (microbatch_count, microbatch_rows)
    )
    section = jnp.where(
        inner_grid < first_len, 0, jnp.where(inner_grid < first_len + second_len, 1, 2)
    )
    allowed = (section[:, :, None] == section[:, None, :]) & (
        inner_grid[:, None, :] <= inner_grid[:, :, None]
    )
    live_rows = (section < 2).astype(jnp.float32).reshape(count_of_rows, 1)
    return (live_rows, allowed)


def routing(choice_ids, capacity):
    count_of_rows, top_count = choice_ids.shape
    expert_ids = jnp.arange(EXPERTS, dtype=jnp.int32)
    expert_hits = (choice_ids[:, :, None] == expert_ids[None, None, :]).astype(jnp.int32)
    per_row = jnp.sum(expert_hits, axis=1)
    before = jnp.cumsum(per_row, axis=0) - per_row
    position = jnp.sum(expert_hits * before[:, None, :], axis=2)
    slot_index = choice_ids * capacity + position
    pair_index = jnp.arange(count_of_rows * top_count, dtype=jnp.int32)
    source = (
        jnp.full((EXPERTS * capacity,), count_of_rows * top_count, jnp.int32)
        .at[slot_index.reshape(-1)]
        .set(pair_index)
    )
    return (expert_hits, slot_index, source)


def shards(
    hidden_in,
    grad_out,
    seq_lens,
    expert_choice,
    gain_attn,
    w_query,
    key_weight,
    value_weight,
    w_attn_out,
    gain_ffn,
    w_router,
    w_expert_in,
    w_expert_out,
):
    count_of_rows = hidden_in.shape[0]
    microbatch_count = seq_lens.shape[0]
    microbatch_rows = count_of_rows // microbatch_count
    query_group_size = QUERY_HEADS // KEY_VALUE_HEADS
    device_count = lax.axis_size("fsdp")
    live_rows, allowed = layout(seq_lens, count_of_rows)
    mask_grid = allowed[:, None, None]
    hidden = hidden_in.astype(jnp.float32)
    cotangent = grad_out.astype(jnp.float32)
    attention_set = (
        lax.all_gather(gain_attn, "fsdp", axis=0, tiled=True),
        lax.all_gather(w_query, "fsdp", axis=0, tiled=True),
        lax.all_gather(key_weight, "fsdp", axis=0, tiled=True),
        lax.all_gather(value_weight, "fsdp", axis=0, tiled=True),
        lax.all_gather(w_attn_out, "fsdp", axis=0, tiled=True),
        lax.all_gather(gain_ffn, "fsdp", axis=0, tiled=True),
        lax.all_gather(w_router, "fsdp", axis=0, tiled=True),
    )
    gain_one = attention_set[0].astype(jnp.float32)
    gain_two = attention_set[5].astype(jnp.float32)
    scale_one = rms_scale(hidden)
    unit_one = hidden * scale_one
    normed = (unit_one * gain_one).astype(jnp.bfloat16)
    query_rows = jnp.dot(normed, attention_set[1], preferred_element_type=jnp.float32).astype(
        jnp.bfloat16
    )
    every_key = jnp.dot(normed, attention_set[2], preferred_element_type=jnp.float32).astype(
        jnp.bfloat16
    )
    every_value = jnp.dot(normed, attention_set[3], preferred_element_type=jnp.float32).astype(
        jnp.bfloat16
    )
    query_tiles = query_rows.reshape(
        microbatch_count, microbatch_rows, KEY_VALUE_HEADS, query_group_size, HEAD_SIZE
    )
    key_tiles = every_key.reshape(microbatch_count, microbatch_rows, KEY_VALUE_HEADS, HEAD_SIZE)
    value_tiles = every_value.reshape(microbatch_count, microbatch_rows, KEY_VALUE_HEADS, HEAD_SIZE)

    def score_block():
        raw_scores = (
            jnp.einsum(
                "mqgrd,mkgd->mgrqk", query_tiles, key_tiles, preferred_element_type=jnp.float32
            )
            * 0.125
        )
        return jnp.where(mask_grid, raw_scores, -1e30)

    scores = score_block()
    top_score = jnp.max(scores, axis=-1, keepdims=True)
    weights = jnp.exp(scores - top_score)
    row_total = jnp.sum(weights, axis=-1, keepdims=True)
    probs_low = (weights / row_total).astype(jnp.bfloat16)
    context = jnp.einsum(
        "mgrqk,mkgd->mqgrd", probs_low, value_tiles, preferred_element_type=jnp.float32
    )
    context = context.reshape(count_of_rows, QUERY_HEADS * HEAD_SIZE).astype(jnp.bfloat16)
    attended = jnp.dot(context, attention_set[4], preferred_element_type=jnp.float32)
    middle = hidden + live_rows * attended
    scale_two = rms_scale(middle)
    unit_two = middle * scale_two
    normed_ffn = (unit_two * gain_two).astype(jnp.bfloat16)
    logits = jnp.dot(normed_ffn, attention_set[6], preferred_element_type=jnp.float32)
    expert_hits, slot_index, source = routing(expert_choice, CAP)
    hits_float = expert_hits.astype(jnp.float32)
    chosen = jnp.sum(hits_float * logits[:, None, :], axis=2)
    chosen_top = jnp.max(chosen, axis=1, keepdims=True)
    gate_exp = jnp.exp(chosen - chosen_top)
    gate_weights = gate_exp / jnp.sum(gate_exp, axis=1, keepdims=True)
    padded = jnp.concatenate([normed_ffn, jnp.zeros((1, MODEL_WIDTH), jnp.bfloat16)], axis=0)
    dispatched = padded[source // TOP].reshape(EXPERTS, CAP, MODEL_WIDTH)
    expert_in_full = lax.all_gather(w_expert_in, "fsdp", axis=0, tiled=True)
    expert_out_full = lax.all_gather(w_expert_out, "fsdp", axis=0, tiled=True)
    in_grid = expert_in_full.reshape(MODEL_WIDTH, EXPERTS, 2 * FE)
    out_grid = expert_out_full.reshape(FE, EXPERTS, MODEL_WIDTH)
    gate_up = jnp.einsum("ecd,def->ecf", dispatched, in_grid, preferred_element_type=jnp.float32)
    gate_part = gate_up[:, :, :FE]
    up_part = gate_up[:, :, FE:]
    sigmoid_gate = lax.logistic(gate_part)
    silu_gate = gate_part * sigmoid_gate
    activated = (silu_gate * up_part).astype(jnp.bfloat16)
    expert_out = jnp.einsum("ecf,fed->ecd", activated, out_grid, preferred_element_type=jnp.float32)
    picked = expert_out.reshape(EXPERTS * CAP, MODEL_WIDTH)[slot_index]
    mixture = jnp.sum(gate_weights[:, :, None] * picked, axis=1)
    block_output = (middle + live_rows * mixture).astype(jnp.bfloat16)
    back_set = (
        lax.all_gather(gain_attn, "fsdp", axis=0, tiled=True),
        lax.all_gather(w_query, "fsdp", axis=0, tiled=True),
        lax.all_gather(key_weight, "fsdp", axis=0, tiled=True),
        lax.all_gather(value_weight, "fsdp", axis=0, tiled=True),
        lax.all_gather(w_attn_out, "fsdp", axis=0, tiled=True),
        lax.all_gather(gain_ffn, "fsdp", axis=0, tiled=True),
        lax.all_gather(w_router, "fsdp", axis=0, tiled=True),
    )
    out_back = lax.all_gather(w_expert_out, "fsdp", axis=0, tiled=True).reshape(
        FE, EXPERTS, MODEL_WIDTH
    )
    in_back = lax.all_gather(w_expert_in, "fsdp", axis=0, tiled=True).reshape(
        MODEL_WIDTH, EXPERTS, 2 * FE
    )
    grad_mix = live_rows * cotangent
    grad_gates = jnp.sum(grad_mix[:, None, :] * picked, axis=2)
    grad_chosen = gate_weights * (
        grad_gates - jnp.sum(gate_weights * grad_gates, axis=1, keepdims=True)
    )
    grad_logits = jnp.sum(grad_chosen[:, :, None] * hits_float, axis=1)
    pair_grads = (gate_weights[:, :, None] * grad_mix[:, None, :]).reshape(
        count_of_rows * TOP, MODEL_WIDTH
    )
    pair_padded = jnp.concatenate([pair_grads, jnp.zeros((1, MODEL_WIDTH), jnp.float32)], axis=0)
    grad_expert_out = pair_padded[source].astype(jnp.bfloat16).reshape(EXPERTS, CAP, MODEL_WIDTH)
    grad_activated = jnp.einsum(
        "ecd,fed->ecf", grad_expert_out, out_back, preferred_element_type=jnp.float32
    )
    out_rows = w_expert_out.shape[0]
    columns = activated
    grad_w_expert_out = lax.psum_scatter(
        jnp.einsum(
            "ecn,ecd->ned", columns, grad_expert_out, preferred_element_type=jnp.float32
        ).reshape(1 * lax.axis_size("fsdp"), out_rows * EXPERTS * MODEL_WIDTH),
        "fsdp",
        scatter_dimension=0,
        tiled=True,
    ).reshape(out_rows, EXPERTS * MODEL_WIDTH)
    grad_gate = grad_activated * up_part * (sigmoid_gate * (1.0 + gate_part * (1.0 - sigmoid_gate)))
    grad_up = grad_activated * silu_gate
    grad_gate_up = jnp.concatenate([grad_gate, grad_up], axis=-1).astype(jnp.bfloat16)
    grad_dispatched = jnp.einsum(
        "ecf,def->ecd", grad_gate_up, in_back, preferred_element_type=jnp.float32
    )
    in_rows = w_expert_in.shape[0]
    columns = dispatched
    grad_w_expert_in = lax.psum_scatter(
        jnp.einsum(
            "ecn,ecf->nef", columns, grad_gate_up, preferred_element_type=jnp.float32
        ).reshape(1 * lax.axis_size("fsdp"), in_rows * EXPERTS * 2 * FE),
        "fsdp",
        scatter_dimension=0,
        tiled=True,
    ).reshape(in_rows, EXPERTS * 2 * FE)
    router_full = back_set[6].astype(jnp.float32)
    grad_normed_ffn = jnp.sum(
        grad_dispatched.reshape(EXPERTS * CAP, MODEL_WIDTH)[slot_index], axis=1
    )
    grad_normed_ffn = grad_normed_ffn + jnp.dot(grad_logits, router_full.T, precision=highest)
    grad_router = jnp.dot(normed_ffn.astype(jnp.float32).T, grad_logits, precision=highest)
    back_gain_two = back_set[5].astype(jnp.float32)
    grad_gain_two = jnp.sum(grad_normed_ffn * unit_two, axis=0)
    scaled_two = grad_normed_ffn * back_gain_two
    grad_middle = cotangent + scale_two * (
        scaled_two - unit_two * jnp.mean(scaled_two * unit_two, axis=-1, keepdims=True)
    )
    grad_attended = (live_rows * grad_middle).astype(jnp.bfloat16)
    grad_out_proj = jnp.einsum(
        "ti,td->id", context, grad_attended, preferred_element_type=jnp.float32
    )
    context_gradient = jnp.einsum(
        "td,id->ti", grad_attended, back_set[4], preferred_element_type=jnp.float32
    ).astype(jnp.bfloat16)
    context_gradient_grid = context_gradient.reshape(
        microbatch_count, microbatch_rows, KEY_VALUE_HEADS, query_group_size, HEAD_SIZE
    )
    probs_again = jnp.exp(score_block() - top_score) / row_total
    probs_again_low = probs_again.astype(jnp.bfloat16)
    grad_probs = jnp.einsum(
        "mqgrd,mkgd->mgrqk", context_gradient_grid, value_tiles, preferred_element_type=jnp.float32
    )
    value_gradient = jnp.einsum(
        "mgrqk,mqgrd->mkgd",
        probs_again_low,
        context_gradient_grid,
        preferred_element_type=jnp.float32,
    )
    grad_scores = probs_again * (
        grad_probs - jnp.sum(probs_again * grad_probs, axis=-1, keepdims=True)
    )
    grad_scores = grad_scores.astype(jnp.bfloat16)
    grad_queries = (
        jnp.einsum("mgrqk,mkgd->mqgrd", grad_scores, key_tiles, preferred_element_type=jnp.float32)
        * 0.125
    )
    grad_queries = grad_queries.reshape(count_of_rows, QUERY_HEADS * HEAD_SIZE).astype(jnp.bfloat16)
    key_gradient = (
        jnp.einsum(
            "mgrqk,mqgrd->mkgd", grad_scores, query_tiles, preferred_element_type=jnp.float32
        )
        * 0.125
    )
    key_gradient = key_gradient.reshape(count_of_rows, KEY_VALUE_HEADS * HEAD_SIZE).astype(
        jnp.bfloat16
    )
    value_gradient_narrow = value_gradient.reshape(
        count_of_rows, KEY_VALUE_HEADS * HEAD_SIZE
    ).astype(jnp.bfloat16)
    grad_query_proj = jnp.einsum(
        "td,ti->di", normed, grad_queries, preferred_element_type=jnp.float32
    )
    grad_key_proj = jnp.einsum(
        "td,ti->di", normed, key_gradient, preferred_element_type=jnp.float32
    )
    grad_value_proj = jnp.einsum(
        "td,ti->di", normed, value_gradient_narrow, preferred_element_type=jnp.float32
    )
    grad_normed = jnp.einsum(
        "ti,di->td", grad_queries, back_set[1], preferred_element_type=jnp.float32
    )
    grad_normed = grad_normed + jnp.einsum(
        "ti,di->td", key_gradient, back_set[2], preferred_element_type=jnp.float32
    )
    grad_normed = grad_normed + jnp.einsum(
        "ti,di->td", value_gradient_narrow, back_set[3], preferred_element_type=jnp.float32
    )
    back_gain_one = back_set[0].astype(jnp.float32)
    grad_gain_one = jnp.sum(grad_normed * unit_one, axis=0)
    scaled_one = grad_normed * back_gain_one
    grad_hidden = grad_middle + scale_one * (
        scaled_one - unit_one * jnp.mean(scaled_one * unit_one, axis=-1, keepdims=True)
    )
    terms = (
        grad_gain_one,
        grad_query_proj,
        grad_key_proj,
        grad_value_proj,
        grad_out_proj,
        grad_gain_two,
        grad_router,
    )
    local_shapes = (
        gain_attn.shape,
        w_query.shape,
        key_weight.shape,
        value_weight.shape,
        w_attn_out.shape,
        gain_ffn.shape,
        w_router.shape,
    )
    flat_terms = tuple((term.reshape(device_count, -1) for term in terms))
    owned = (
        lax.psum_scatter(flat_terms[0], "fsdp", scatter_dimension=0, tiled=True),
        lax.psum_scatter(flat_terms[1], "fsdp", scatter_dimension=0, tiled=True),
        lax.psum_scatter(flat_terms[2], "fsdp", scatter_dimension=0, tiled=True),
        lax.psum_scatter(flat_terms[3], "fsdp", scatter_dimension=0, tiled=True),
        lax.psum_scatter(flat_terms[4], "fsdp", scatter_dimension=0, tiled=True),
        lax.psum_scatter(flat_terms[5], "fsdp", scatter_dimension=0, tiled=True),
        lax.psum_scatter(flat_terms[6], "fsdp", scatter_dimension=0, tiled=True),
    )
    owned = tuple((piece.reshape(shape) for piece, shape in zip(owned, local_shapes)))
    return (
        block_output,
        grad_hidden.astype(jnp.bfloat16),
        owned[0],
        owned[1],
        owned[2],
        owned[3],
        owned[4],
        owned[5],
        owned[6],
        grad_w_expert_in,
        grad_w_expert_out,
    )


def solution(mesh):
    placed = (
        P("fsdp", None),
        P("fsdp", None),
        P("fsdp", None),
        P("fsdp", None),
        P("fsdp"),
        P("fsdp", None),
        P("fsdp", None),
        P("fsdp", None),
        P("fsdp", None),
        P("fsdp"),
        P("fsdp", None),
        P("fsdp", None),
        P("fsdp", None),
    )
    devices = mesh.shape["fsdp"]
    planes = devices // PLANE
    whole = devices % PLANE == 0 and planes > 1 and planes & (planes - 1) == 0 and FE % (16 * devices) == 0
    return jax.shard_map(
        exchanged if whole else shards,
        mesh=mesh,
        in_specs=placed,
        out_specs=(
            P("fsdp", None),
            P("fsdp", None),
            P("fsdp"),
            P("fsdp", None),
            P("fsdp", None),
            P("fsdp", None),
            P("fsdp", None),
            P("fsdp"),
            P("fsdp", None),
            P("fsdp", None),
            P("fsdp", None),
        ),
        check_vma=False,
    )
```
